32 devices in a mesh: loop: 2 (over x), inner: 16 (over z, y, core).
Axes of the slice: x: 2, y: 2, z: 4, core: 2. Of those that a mesh axis runs over, the one named last changes fastest.
Arguments:
- site_blocks: bfloat16 [2, 16, 4, 256, 256], P('loop', 'inner'), may hold values from -6 to 6
- bond_weights: float32 [2, 16, 256], P('loop', 'inner'), may hold values from 0.2 to 2
- bond_gates: float32 [2, 16, 16], P('loop'), may hold values from -3 to 3
- kept_slots: int32 [2, 16], P('loop', 'inner'), may hold values from 64 to 256, as said below
Outputs:
- new_sites: bfloat16 [2, 16, 4, 256, 256], P('loop', 'inner')
- new_weights: float32 [2, 16, 256], P('loop', 'inner')
The draws below stay inside these ranges and needn't reach their ends.
Inputs may be any that keep to these rules, and one draw needn't show every extreme that they name: `kept_slots`: every bond has at least one sector block with all 256 slots kept.
All inputs are finite; a program needn't handle non-finite values.
Results may differ from the reference program's by a relative error of at most 0.015.
The reference program's roundings to bfloat16 on the way count: a program that leaves them out, or rounds other values in their place, can miss the bound.
Values may be sent and summed in bfloat16 or wider, within the bound.
No kernel may reach another device: no remote copies, remote signals or barrier semaphores. Data moves between devices by JAX's collectives and lax.ppermute only.
A program may use at most 64 MiB of HBM per device.

```python
import math
import jax
import jax.numpy as jnp
import numpy as np
from jax import lax

PHYS = 4
SB = 256
NSEC = 16
NSITE = 2


def draw_kept_slots(key, part):
    first_key, second_key = jax.random.split(jax.random.fold_in(key, 17))
    values = jax.random.randint(first_key, (NSITE, NSEC), SB // 4, SB + 1)
    spot = jax.random.randint(second_key, (NSITE, 1), 0, NSEC)
    column = jnp.arange(NSEC)[None, :]
    return jnp.where(column == spot, SB, values).astype(jnp.int32)


def block_levels(stream_key, shape, cuts, smallest, largest):
    gain, own = 1.0, jax.random.fold_in(stream_key, 6)
    for dim, parts in cuts:
        draws = jnp.exp(jax.random.uniform(jax.random.fold_in(own, dim), (parts,), jnp.float32, smallest / len(cuts), largest / len(cuts)))
        gain = gain * jnp.repeat(draws, shape[dim] // parts).reshape([-1 if axis == dim else 1 for axis in range(len(shape))])
    return gain


def bell_draw(stream_key, shape, scale, limit, cuts=(), kind=jnp.bfloat16):
    loudness = block_levels(stream_key, shape, cuts, -0.22, 0.18) if cuts else 1.0
    values = jax.random.normal(stream_key, shape, jnp.float32) * scale * loudness
    return jnp.minimum(jnp.maximum(values, -limit), limit).astype(kind)


def setup_inputs(seed: int = 0) -> dict:
    key_list = jax.random.split(jax.random.key(seed), 5)
    return {
        "site_blocks": bell_draw(key_list[0], (NSITE, NSEC, PHYS, SB, SB), 1.0, 6.0, ((0, 2), (1, 16))),
        "bond_weights": jnp.clip(jnp.exp(math.log(2.0) - 2.3025851 * jax.random.uniform(key_list[1], (NSITE, NSEC, SB), jnp.float32) ** block_levels(key_list[1], (NSITE, NSEC, SB), ((0, 2), (1, 16)), -0.2, 0.2)), 0.2, 2.0),
        "bond_gates": bell_draw(key_list[2], (NSITE, PHYS * PHYS, PHYS * PHYS), 0.5, 3.0, ((0, 2),), jnp.float32),
        "kept_slots": draw_kept_slots(jax.random.fold_in(key_list[4], 71), 0),
    }


CHARGE = np.array([0, 1, 1, 2])

def gate_masks():
    table = np.zeros((3, 16, 16), np.float32)
    for outer_a in range(4):
        for outer_b in range(4):
            for source_a in range(4):
                for source_b in range(4):
                    offset = CHARGE[source_a] - CHARGE[outer_a]
                    same_total = CHARGE[outer_a] + CHARGE[outer_b] == CHARGE[source_a] + CHARGE[source_b]
                    if same_total and offset >= -1 and (offset <= 1):
                        table[offset + 1, outer_a * 4 + outer_b, source_a * 4 + source_b] = 1.0
    return table

def rounded(values):
    return lax.optimization_barrier(values.astype(jnp.bfloat16))

def pair_products(scaled, pieces):
    products = jnp.einsum('mars,mbst->mabrt', scaled.astype(jnp.float32), pieces.astype(jnp.float32), precision=lax.Precision.HIGHEST)
    return rounded(products * (1.0 / math.sqrt(SB))).reshape(NSEC, PHYS * PHYS, SB, SB)

def bond_update(left_site, right_site, weight_row, gate_matrix, kept_row):
    row_count = PHYS * SB
    pieces = jnp.stack([jnp.roll(right_site[:, state], -int(CHARGE[state]), axis=0) for state in range(PHYS)], axis=1)
    scaled = rounded(left_site.astype(jnp.float32) * weight_row[:, None, None, :])
    theta_terms = pair_products(scaled, pieces).astype(jnp.float32)
    mixer_table = rounded(gate_matrix[None] * jnp.asarray(gate_masks())).astype(jnp.float32)
    mixed_terms = jnp.zeros((NSEC, PHYS * PHYS, SB, SB), jnp.float32)
    for position, offset in enumerate((-1, 0, 1)):
        source = jnp.roll(theta_terms, -offset, axis=0)
        mixed_terms = mixed_terms + jnp.einsum('kj,mjrs->mkrs', mixer_table[position], source, precision=lax.Precision.HIGHEST)
    mixed_terms = rounded(mixed_terms).astype(jnp.float32)
    matrix = mixed_terms.reshape(NSEC, PHYS, PHYS, SB, SB).transpose(0, 1, 3, 2, 4).reshape(NSEC, row_count, row_count)
    column = jnp.arange(SB)[None, None, None, :]
    old_basis = jnp.where(column < kept_row[:, None, None, None], left_site, jnp.zeros_like(left_site))
    old_basis = old_basis.astype(jnp.float32).reshape(NSEC, row_count, SB)
    projected = jnp.einsum('mij,mik->mjk', matrix, old_basis, precision=lax.Precision.HIGHEST)
    gram_matrix = jnp.einsum('mjk,mjl->mkl', projected, projected, precision=lax.Precision.HIGHEST) + jnp.eye(SB, dtype=jnp.float32)
    factor = jnp.linalg.cholesky(gram_matrix)
    solved = jax.vmap(lambda lower_part, right_part: jax.scipy.linalg.solve_triangular(lower_part, right_part, lower=True))(factor, jnp.swapaxes(projected, 1, 2))
    orthonormal = jnp.swapaxes(solved, 1, 2)
    isometry = rounded(orthonormal * math.sqrt(row_count))
    carried = jnp.einsum('mij,mjk->mik', matrix, isometry.astype(jnp.float32), precision=lax.Precision.HIGHEST) * (1.0 / math.sqrt(row_count))
    new_level = jnp.sqrt(lax.optimization_barrier(jnp.mean(carried * carried, axis=1)) + 1e-06)
    new_left = (carried / new_level[:, None, :]).astype(jnp.bfloat16).reshape(NSEC, PHYS, SB, SB)
    right_parts = isometry.reshape(NSEC, PHYS, SB, SB).transpose(0, 1, 3, 2)
    new_right = jnp.stack([jnp.roll(right_parts[:, state], int(CHARGE[state]), axis=0) for state in range(PHYS)], axis=1)
    return (new_left, new_level, new_right)

def reference(site_blocks, bond_weights, bond_gates, kept_slots):
    sites = [site_blocks[position] for position in range(NSITE)]
    levels = [bond_weights[position] for position in range(NSITE)]
    for parity in (0, 1):
        for left_index in range(parity, NSITE, 2):
            right_index = (left_index + 1) % NSITE
            new_left, new_level, new_right = bond_update(sites[left_index], sites[right_index], levels[left_index], bond_gates[left_index], kept_slots[left_index])
            sites[left_index] = new_left
            sites[right_index] = new_right
            levels[left_index] = new_level
    results = []
    for position in range(NSITE):
        earlier = levels[(position - 1) % NSITE]
        row_scale = jnp.stack([jnp.roll(earlier, int(CHARGE[state]), axis=0) for state in range(PHYS)], axis=1)
        results.append((sites[position].astype(jnp.float32) * row_scale[:, :, :, None]).astype(jnp.bfloat16))
    return (jnp.stack(results), jnp.stack(levels))
```

```python
import functools
import math

import jax
import jax.numpy as jnp
import numpy as np
from jax import lax
from jax.experimental import pallas as pl
from jax.experimental.pallas import tpu as pltpu
from jax.sharding import PartitionSpec as P

CHARGE = (0, 1, 1, 2)
AXES = ("loop", "inner")
BF16, F32 = jnp.bfloat16, jnp.float32
VMEM_BYTES = 40 << 20
HIGHEST = lax.Precision.HIGHEST


def gate_terms():
    table = {}
    for a in range(4):
        for b in range(4):
            table[a, b] = [
                (CHARGE[p] - CHARGE[a], p, q)
                for p in range(4)
                for q in range(4)
                if CHARGE[p] + CHARGE[q] == CHARGE[a] + CHARGE[b]
                and abs(CHARGE[p] - CHARGE[a]) <= 1
            ]
    return table


TERMS = gate_terms()
PIECES = {
    (0, 0): (0, 3, 4, 0),
    (0, 1): (4, 3, 4, 0),
    (0, 2): (5, 3, 4, 0),
    (0, 3): (9, 3, 4, 0),
    (-1, 1): (1, 0, 3, 0),
    (-1, 2): (2, 0, 3, 0),
    (-1, 3): (6, 0, 3, 0),
    (1, 0): (3, 7, 3, 1),
    (1, 1): (7, 7, 3, 1),
    (1, 2): (8, 7, 3, 1),
}


def theta_slots():
    slots, count = {}, 0
    for (distance, q), (_, _, rows, first) in PIECES.items():
        for p in range(rows):
            slots[distance, first + p, q] = count
            count += 1
    return slots, count


SLOTS, SLOT_COUNT = theta_slots()


def dot(a, b, dims, precision=None):
    return lax.dot_general(a, b, (dims, ((), ())), precision=precision, preferred_element_type=F32)


def split3(a):
    h = a.astype(BF16)
    r = a - h.astype(F32)
    m = r.astype(BF16)
    return h, m, (r - m.astype(F32)).astype(BF16)


def factor_rows(work, size, panel=32):
    rowid = lax.broadcasted_iota(jnp.int32, (panel, 128), 0)
    for start in range(0, size, panel):
        low = start < size // 2
        chunks = [0, 1, 2] if low else [1, 2, 3]
        rows = [work[start : start + panel, 128 * c : 128 * c + 128] for c in chunks]
        pivots = jnp.ones((panel, 128), F32)
        for group in range(panel // 8):
            base = start % 128 + 8 * group
            cols = [
                jnp.broadcast_to(rows[0][:, base + k : base + k + 1], (panel, 128))
                for k in range(8)
            ]
            for j in range(8):
                at = 8 * group + j
                pivot = cols[j][at : at + 1, :]
                factor = jnp.where(rowid > at, cols[j], 0.0) * (1.0 / pivot)
                for k in range(j + 1, 8):
                    cols[k] = cols[k] - factor * cols[k][at : at + 1, :]
                rows = [x - factor * x[at : at + 1, :] for x in rows]
                pivots = jnp.where(rowid == at, pivot, pivots)
        scale = lax.rsqrt(pivots)
        rows = [x * scale for x in rows]
        for c, x in zip(chunks, rows):
            work[start : start + panel, 128 * c : 128 * c + 128] = x
        after = start + panel
        if after < size:
            h, m, l = split3(jnp.concatenate(rows, axis=1))
            right = jnp.concatenate([h, m, h, l, h, m], axis=0)
            left = jnp.concatenate([h, h, m, h, l, m], axis=0)
            first = 128 * chunks[0]
            for lo, hi in ((after, after + panel), (after + panel, size)):
                if lo < hi:
                    update = dot(left[:, lo - first : hi - first], right, ((0,), (0,)))
                    for i, c in enumerate(chunks):
                        work[lo:hi, 128 * c : 128 * c + 128] -= update[:, 128 * i : 128 * i + 128]


def bond_body(bond, x, c, table, gates, sem, a_ref, b_ref, scaled, theta, matrix, proj, work, iso):
    def row(core, which):
        return table.at[jnp.where(core == c, 0, 1), which]

    def weights(core, which):
        ref = row(core, which)
        return jnp.concatenate([ref[0:1, :], ref[1:2, :]], axis=1)

    plain = jnp.where(x == bond, 0, 1)
    across = jnp.where(x == bond, 2, 3)
    holder = jnp.where(x == bond, 1 - x, x)
    at_even, at_odd, beyond = weights(0, plain), weights(1, plain), weights(holder, across)
    even_role = x == 0
    below = jnp.where(even_role, beyond, at_even)
    here = jnp.where(even_role, at_even, at_odd)
    above = jnp.where(even_role, at_odd, beyond)
    copy = pltpu.make_async_copy(table.at[0, plain], gates, sem)
    copy.start()
    copy.wait()
    kept = table[0, plain, 4:5, 0:1]
    kept = jnp.where(even_role, row(0, plain)[4:5, 0:1], row(1, plain)[4:5, 0:1])

    for slot, w in [(s, below) for s in range(3)] + [(s, here) for s in range(3, 7)] + [
        (s, above) for s in range(7, 10)
    ]:
        scaled[slot] = (a_ref[slot].astype(F32) * w).astype(BF16)
    blocks = a_ref.shape[-1]
    for (distance, q), (right, left, count, first) in PIECES.items():
        product = dot(
            scaled[left : left + count].reshape(count * blocks, blocks), b_ref[right], ((1,), (0,))
        )
        product = (product * (1.0 / math.sqrt(blocks))).astype(BF16)
        slot = SLOTS[distance, first, q]
        theta[slot : slot + count] = product.reshape(count, blocks, blocks)

    def gate(a, b, p, q):
        flat = (4 * a + b) * 16 + 4 * p + q
        return gates[2 + flat // 128, flat % 128]

    step = 16

    @pl.loop(0, blocks // step)
    def mix(chunk):
        at = pl.multiple_of(chunk * step, step)
        for half in range(blocks // 128):
            cut = slice(128 * half, 128 * half + 128)
            held = {}

            def term(distance, p, q):
                slot = SLOTS[distance, p, q]
                if slot not in held:
                    held[slot] = theta[slot, pl.ds(at, step), cut].astype(F32)
                return held[slot]

            for total in range(5):
                for a in range(4):
                    for b in range(4):
                        if CHARGE[a] + CHARGE[b] != total:
                            continue
                        value = None
                        for distance, p, q in TERMS[a, b]:
                            part = gate(a, b, p, q) * term(distance, p, q)
                            value = part if value is None else value + part
                        matrix[
                            pl.ds(pl.multiple_of(a * blocks + at, step), step),
                            b * blocks + 128 * half : b * blocks + 128 * half + 128,
                        ] = value.astype(BF16)
                held.clear()

    basis = a_ref[3:7].reshape(4 * blocks, blocks)
    projected = dot(basis, matrix[...], ((0,), (0,)))
    slot_id = lax.broadcasted_iota(jnp.int32, projected.shape, 0).astype(F32)
    projected = jnp.where(slot_id < kept, projected, 0.0)
    proj[...] = projected
    work[:, :blocks] = dot(projected, projected, ((1,), (1,)), HIGHEST)
    ri = lax.broadcasted_iota(jnp.int32, (blocks, blocks), 0)
    ci = lax.broadcasted_iota(jnp.int32, (blocks, blocks), 1)
    eye = jnp.where(ri == ci, 1.0, 0.0).astype(F32)
    work[:, :blocks] += eye
    work[:, blocks:] = eye
    factor_rows(work, blocks)
    ortho = dot(work[:, blocks:], proj[...], ((1,), (0,)), HIGHEST)
    ortho = (ortho * math.sqrt(4 * blocks)).astype(BF16)
    for p in range(4):
        iso[p] = ortho[:, p * blocks : (p + 1) * blocks]


def finish_iso(c, iso, iso_half, iso_three):
    half = iso.shape[1] // 2
    mine = iso[:, pl.ds(pl.multiple_of(c * half, half), half), :]
    iso_half[...] = mine
    iso_three[...] = mine[1:]


def first_kernel(
    table, own, far, near, cross, own_s, far_s, near_s, cross_s,
    matrix, iso, iso_half, iso_three,
    a_ref, b_ref, scaled, theta, proj, work, gates, sems, sem,
):
    x = lax.axis_index("loop") % 2
    c = lax.axis_index("inner") % 2
    pairs = {"own": (own, own_s), "far": (far, far_s), "near": (near, near_s), "cross": (cross, cross_s)}
    plans = {
        0: [
            (a_ref, 0, "near", 1, 0, 3),
            (a_ref, 3, "own", 0, 0, 4),
            (a_ref, 7, "own", 1, 1, 3),
            (b_ref, 0, "far", 0, 0, 3),
            (b_ref, 3, "far", 1, 0, 4),
            (b_ref, 7, "cross", 0, 0, 3),
        ],
        1: [
            (a_ref, 0, "far", 0, 0, 3),
            (a_ref, 3, "far", 1, 0, 4),
            (a_ref, 7, "cross", 1, 0, 3),
            (b_ref, 0, "own", 1, 0, 3),
            (b_ref, 3, "near", 0, 0, 4),
            (b_ref, 7, "near", 1, 1, 3),
        ],
    }
    for role, plan in plans.items():
        for core in (0, 1):

            @pl.when(jnp.logical_and(x == role, c == core))
            def _(plan=plan, core=core):
                for n, (target, at, name, holder, first, count) in enumerate(plan):
                    source = pairs[name][0 if holder == core else 1]
                    pltpu.make_async_copy(
                        source.at[pl.ds(first, count)], target.at[pl.ds(at, count)], sems.at[n]
                    ).start()

    for n, (target, at, _, _, _, count) in enumerate(plans[0]):
        pltpu.make_async_copy(
            own.at[pl.ds(0, count)], target.at[pl.ds(at, count)], sems.at[n]
        ).wait()
    bond_body(0, x, c, table, gates, sem, a_ref, b_ref, scaled, theta, matrix, proj, work, iso)
    finish_iso(c, iso, iso_half, iso_three)


def second_kernel(
    table, iso_0, iso_1, iso_2, left_0, left_1, left_2, iso_1s, iso_2s, left_1s, left_2s,
    matrix, iso,
    a_ref, b_ref, scaled, theta, proj, work, gates, sems, sem,
):
    x = lax.axis_index("loop") % 2
    c = lax.axis_index("inner") % 2
    half = iso_1.shape[1]
    mine = pl.ds(pl.multiple_of(c * half, half), half)
    other = pl.ds(pl.multiple_of((1 - c) * half, half), half)
    copies = []

    def move(source, target):
        copy = pltpu.make_async_copy(source, target, sems.at[len(copies)])
        copy.start()
        copies.append(copy)

    move(iso_0.at[pl.ds(0, 1)], a_ref.at[pl.ds(3, 1)])
    move(iso_0.at[pl.ds(1, 2)], a_ref.at[pl.ds(7, 2)])
    move(left_0.at[pl.ds(0, 3)], b_ref.at[pl.ds(0, 3)])
    for rows, one, two, three, four in (
        (mine, iso_1, iso_2, left_1, left_2),
        (other, iso_1s, iso_2s, left_1s, left_2s),
    ):
        move(one.at[pl.ds(0, 1)], a_ref.at[pl.ds(0, 1), rows])
        move(one.at[pl.ds(1, 2)], a_ref.at[pl.ds(4, 2), rows])
        move(one.at[pl.ds(3, 1)], a_ref.at[pl.ds(9, 1), rows])
        move(two.at[pl.ds(0, 2)], a_ref.at[pl.ds(1, 2), rows])
        move(two.at[pl.ds(2, 1)], a_ref.at[pl.ds(6, 1), rows])
        move(three, b_ref.at[pl.ds(3, 4), rows])
        move(four, b_ref.at[pl.ds(7, 3), rows])
    for copy in copies:
        copy.wait()
    bond_body(1, x, c, table, gates, sem, a_ref, b_ref, scaled, theta, matrix, proj, work, iso)


def carry(matrix, iso):
    blocks = iso.shape[-1]
    total = None
    for p in range(4):
        part = dot(matrix[:, p * blocks : (p + 1) * blocks], iso[p], ((1,), (1,)))
        total = part if total is None else total + part
    carried = total * (1.0 / math.sqrt(4 * blocks))
    level = jnp.sqrt(jnp.mean(carried * carried, axis=0, keepdims=True) + 1e-06)
    return (carried / level).astype(BF16).reshape(4, blocks, blocks), level


def first_carry(matrix, iso, left, left_half, left_three, level_ref):
    c = lax.axis_index("inner") % 2
    new_left, level = carry(matrix, iso)
    left[...] = new_left
    half = left.shape[1] // 2
    mine = left[:, pl.ds(pl.multiple_of(c * half, half), half), :]
    left_half[...] = mine
    left_three[...] = mine[1:]
    level_ref[...] = jnp.broadcast_to(level, level_ref.shape)


def as_column(row):
    return jnp.broadcast_to(row, (row.shape[1], row.shape[1])).T


def second_carry(
    matrix, iso, level_0, level_1, level_2, left_out, iso_out, iso_mid, iso_last, iso_first, level_ref
):
    x = lax.axis_index("loop") % 2
    new_left, level = carry(matrix, iso)
    scales = [as_column(ref[0:1, :]) for ref in (level_0, level_1, level_2)]
    for p in range(4):
        left_out[p] = (new_left[p].astype(F32) * scales[CHARGE[p]]).astype(BF16)
    column = as_column(level)
    for p in range(4):
        iso_out[p] = (iso[p].astype(F32) * column).astype(BF16)
    iso_first[...] = iso_out[0:1]
    iso_mid[...] = iso_out[1:3]
    iso_last[...] = iso_out[3:4]
    level_ref[0:8, :] = jnp.broadcast_to(level, (8, level.shape[1]))
    level_ref[8:16, :] = jnp.where(x == 1, level_0[...], level_ref[0:8, :])


def final_kernel(left_out, iso_out, mid, last, first, whole, out, sems):
    x = lax.axis_index("loop") % 2
    c = lax.axis_index("inner") % 2
    plans = {
        (0, 0): [(iso_out, 0, 0, 1), (mid, 0, 1, 2), (last, 0, 3, 1)],
        (0, 1): [(first, 0, 0, 1), (iso_out, 1, 1, 2), (last, 0, 3, 1)],
        (1, 0): [(whole, 0, 0, 4)],
        (1, 1): [(left_out, 0, 0, 4)],
    }
    for (role, core), plan in plans.items():

        @pl.when(jnp.logical_and(x == role, c == core))
        def _(plan=plan):
            copies = [
                pltpu.make_async_copy(
                    source.at[pl.ds(at, count)], out.at[pl.ds(to, count)], sems.at[n]
                )
                for n, (source, at, to, count) in enumerate(plan)
            ]
            for copy in copies:
                copy.start()
            for copy in copies:
                copy.wait()


def scratch(blocks):
    return [
        pltpu.VMEM((10, blocks, blocks), BF16),
        pltpu.VMEM((10, blocks, blocks), BF16),
        pltpu.VMEM((10, blocks, blocks), BF16),
        pltpu.VMEM((SLOT_COUNT, blocks, blocks), BF16),
        pltpu.VMEM((blocks, 4 * blocks), F32),
        pltpu.VMEM((blocks, 2 * blocks), F32),
        pltpu.SMEM((8, 128), F32),
        pltpu.SemaphoreType.DMA((20,)),
        pltpu.SemaphoreType.DMA,
    ]


def vmem():
    return pl.BlockSpec(memory_space=pltpu.VMEM)


def hbm():
    return pl.BlockSpec(memory_space=pl.ANY)


def params():
    return pltpu.CompilerParams(vmem_limit_bytes=VMEM_BYTES)


def cost(flops, nbytes):
    return pl.CostEstimate(flops=flops, bytes_accessed=nbytes, transcendentals=0)


def per_device(loops, inners, site_blocks, bond_weights, bond_gates, kept_slots):
    blocks = site_blocks.shape[-1]

    def send(value, where):
        route = []
        for l in range(loops):
            for i in range(inners):
                source = where(l, i)
                if source is not None:
                    sl, si = source
                    route.append(((sl % loops) * inners + si % inners, l * inners + i))
        return lax.ppermute(value, AXES, route)

    def mirror(l, i):
        return (l ^ 1, i)

    def swap(l, i):
        return (l, i ^ 1)

    def near(l, i):
        if l % 2 == 0:
            return (l, i - 2) if i % 2 == 1 else None
        return (l, i + 2)

    def cross(l, i):
        if l % 2 == 0:
            return (l + 1, i + 2) if i % 2 == 0 else None
        return (l - 1, i + 1) if i % 2 == 1 else None

    def cross_weights(l, i):
        if l % 2 == 0:
            return (l + 1, i - 1) if i % 2 == 0 else None
        return (l - 1, i + 1) if i % 2 == 1 else None

    def below_one(l, i):
        return (l + 1, i - 2) if l % 2 == 0 else (l - 1, i)

    def below_two(l, i):
        return (l, i - 2)

    def above_none(l, i):
        return (l + 2, i)

    def above_one(l, i):
        return (l + 3, i) if l % 2 == 0 else (l + 1, i + 2)

    def above_two(l, i):
        return (l + 2, i + 2)

    block = site_blocks[0, 0]
    pack = jnp.concatenate(
        [
            bond_weights.reshape(2, 128),
            lax.reduce_precision(bond_gates.reshape(2, 128), 8, 7),
            jnp.broadcast_to(kept_slots.astype(F32).reshape(1, 1), (1, 128)),
            jnp.zeros((3, 128), F32),
        ],
        axis=0,
    )
    far_r = send(block, mirror)
    near_r = send(block, near)
    cross_r = send(block[1:], cross)
    own_s = send(block, swap)
    pack_far = send(pack, mirror)
    pack_near = send(pack, near)
    pack_cross = send(pack, cross_weights)
    mine = jnp.stack([pack, pack_far, pack_near, pack_cross])
    table = jnp.stack([mine, send(mine, swap)])
    far_s = send(far_r, swap)
    near_s = send(near_r, swap)
    cross_s = send(cross_r, swap)

    four = jax.ShapeDtypeStruct((4, blocks, blocks), BF16)
    four_half = jax.ShapeDtypeStruct((4, blocks // 2, blocks), BF16)
    three_half = jax.ShapeDtypeStruct((3, blocks // 2, blocks), BF16)
    square = jax.ShapeDtypeStruct((4 * blocks, 4 * blocks), BF16)
    level_shape = jax.ShapeDtypeStruct((8, blocks), F32)

    matrix, iso, iso_half, iso_three = pl.pallas_call(
        first_kernel,
        out_shape=(square, four, four_half, three_half),
        in_specs=[vmem()] + [hbm()] * 8,
        out_specs=(vmem(),) * 4,
        scratch_shapes=scratch(blocks),
        compiler_params=params(),
        name="first_bond",
    )(table, block, far_r, near_r, cross_r, own_s, far_s, near_s, cross_s)

    iso_1 = send(iso_half, below_one)
    iso_2 = send(iso_three, below_two)
    left, left_half, left_three, level = pl.pallas_call(
        first_carry,
        out_shape=(four, four_half, three_half, level_shape),
        in_specs=[vmem()] * 2,
        out_specs=(vmem(),) * 4,
        compiler_params=params(),
        cost_estimate=cost(2 * 1024 * 1024 * 256, 4 << 20),
        name="first_carry",
    )(matrix, iso)
    left_1 = send(left_half, above_one)
    left_2 = send(left_three, above_two)
    left_0 = left if loops == 2 else send(left, above_none)
    iso_1s = send(iso_1, swap)
    iso_2s = send(iso_2, swap)
    left_1s = send(left_1, swap)
    left_2s = send(left_2, swap)
    level_1 = send(level, below_one)
    level_2 = send(level, below_two)

    matrix, iso = pl.pallas_call(
        second_kernel,
        out_shape=(square, four),
        in_specs=[vmem()] + [hbm()] * 10,
        out_specs=(vmem(),) * 2,
        scratch_shapes=scratch(blocks),
        compiler_params=params(),
        cost_estimate=cost(8 * 1024 * 1024 * 256, 8 << 20),
        name="second_bond",
    )(table, iso, iso_1, iso_2, left_0, left_1, left_2, iso_1s, iso_2s, left_1s, left_2s)

    left_out, iso_out, iso_mid, iso_last, iso_first, levels = pl.pallas_call(
        second_carry,
        out_shape=(
            four,
            four,
            jax.ShapeDtypeStruct((2, blocks, blocks), BF16),
            jax.ShapeDtypeStruct((1, blocks, blocks), BF16),
            jax.ShapeDtypeStruct((1, blocks, blocks), BF16),
            jax.ShapeDtypeStruct((16, blocks), F32),
        ),
        in_specs=[vmem()] * 5,
        out_specs=(vmem(),) * 6,
        compiler_params=params(),
        name="second_carry",
    )(matrix, iso, level, level_1, level_2)

    def mid_from(l, i):
        return (l - 1, i - 2) if l % 2 == 0 and i % 2 == 0 else None

    def last_from(l, i):
        if l % 2:
            return None
        return (l - 2, i - 2) if i % 2 == 0 else (l - 1, i - 2)

    def first_from(l, i):
        return (l - 1, i - 1) if l % 2 == 0 and i % 2 == 1 else None

    def whole_from(l, i):
        return (l - 1, i) if l % 2 == 1 and i % 2 == 0 else None

    def level_from(l, i):
        if l % 2 == 0:
            return (l + 1, i - 1) if i % 2 == 1 else None
        return (l - 1, i) if i % 2 == 0 else None

    mid = send(iso_mid, mid_from)
    last = send(iso_last, last_from)
    first = send(iso_first, first_from)
    whole = send(left_out, whole_from)
    level_got = send(levels[8:9], level_from)
    iso_mine = iso_out if loops == 2 else send(iso_out, lambda l, i: (l - 2, i))
    sites = pl.pallas_call(
        final_kernel,
        out_shape=four,
        in_specs=[hbm()] * 6,
        out_specs=hbm(),
        scratch_shapes=[pltpu.SemaphoreType.DMA((3,))],
        name="assemble",
    )(left_out, iso_mine, mid, last, first, whole)
    x = lax.axis_index("loop") % 2
    c = lax.axis_index("inner") % 2
    local = jnp.where(x == 0, level[0:1], levels[0:1])
    weights = jnp.where(x == c, local, level_got)
    return sites[None, None], weights[None]


def solution(mesh):
    return jax.shard_map(
        functools.partial(per_device, mesh.shape["loop"], mesh.shape["inner"]),
        mesh=mesh,
        in_specs=(
            P("loop", "inner", None, None, None),
            P("loop", "inner", None),
            P("loop", None, None),
            P("loop", "inner"),
        ),
        out_specs=(P("loop", "inner", None, None, None), P("loop", "inner", None)),
        check_vma=False,
    )
```

```python
import functools
import math

import jax
import jax.numpy as jnp
import numpy as np
from jax import lax
from jax.experimental import pallas as pl
from jax.experimental.pallas import tpu as pltpu
from jax.sharding import PartitionSpec as P

CHARGE = (0, 1, 1, 2)
AXES = ("loop", "inner")
BF16, F32 = jnp.bfloat16, jnp.float32
VMEM_BYTES = 40 << 20
HIGHEST = lax.Precision.HIGHEST


def gate_terms():
    table = {}
    for a in range(4):
        for b in range(4):
            table[a, b] = [
                (CHARGE[p] - CHARGE[a], p, q)
                for p in range(4)
                for q in range(4)
                if CHARGE[p] + CHARGE[q] == CHARGE[a] + CHARGE[b]
                and abs(CHARGE[p] - CHARGE[a]) <= 1
            ]
    return table


TERMS = gate_terms()
PIECES = {
    (0, 0): (0, 3, 4, 0),
    (0, 1): (4, 3, 4, 0),
    (0, 2): (5, 3, 4, 0),
    (0, 3): (9, 3, 4, 0),
    (-1, 1): (1, 0, 3, 0),
    (-1, 2): (2, 0, 3, 0),
    (-1, 3): (6, 0, 3, 0),
    (1, 0): (3, 7, 3, 1),
    (1, 1): (7, 7, 3, 1),
    (1, 2): (8, 7, 3, 1),
}


def theta_slots():
    slots, count = {}, 0
    for (distance, q), (_, _, rows, first) in PIECES.items():
        for p in range(rows):
            slots[distance, first + p, q] = count
            count += 1
    return slots, count


SLOTS, SLOT_COUNT = theta_slots()


def dot(a, b, dims, precision=None):
    return lax.dot_general(a, b, (dims, ((), ())), precision=precision, preferred_element_type=F32)


def split3(a):
    h = a.astype(BF16)
    r = a - h.astype(F32)
    m = r.astype(BF16)
    return h, m, (r - m.astype(F32)).astype(BF16)


def factor_rows(work, size, panel=32):
    rowid = lax.broadcasted_iota(jnp.int32, (panel, 128), 0)
    for start in range(0, size, panel):
        low = start < size // 2
        chunks = [0, 1, 2] if low else [1, 2, 3]
        rows = [work[start : start + panel, 128 * c : 128 * c + 128] for c in chunks]
        pivots = jnp.ones((panel, 128), F32)
        for group in range(panel // 8):
            base = start % 128 + 8 * group
            cols = [
                jnp.broadcast_to(rows[0][:, base + k : base + k + 1], (panel, 128))
                for k in range(8)
            ]
            for j in range(8):
                at = 8 * group + j
                pivot = cols[j][at : at + 1, :]
                factor = jnp.where(rowid > at, cols[j], 0.0) * (1.0 / pivot)
                for k in range(j + 1, 8):
                    cols[k] = cols[k] - factor * cols[k][at : at + 1, :]
                rows = [x - factor * x[at : at + 1, :] for x in rows]
                pivots = jnp.where(rowid == at, pivot, pivots)
        scale = lax.rsqrt(pivots)
        rows = [x * scale for x in rows]
        for c, x in zip(chunks, rows):
            work[start : start + panel, 128 * c : 128 * c + 128] = x
        after = start + panel
        if after < size:
            h, m, l = split3(jnp.concatenate(rows, axis=1))
            right = jnp.concatenate([h, m, h, l, h, m], axis=0)
            left = jnp.concatenate([h, h, m, h, l, m], axis=0)
            first = 128 * chunks[0]
            for lo, hi in ((after, after + panel), (after + panel, size)):
                if lo < hi:
                    update = dot(left[:, lo - first : hi - first], right, ((0,), (0,)))
                    for i, c in enumerate(chunks):
                        work[lo:hi, 128 * c : 128 * c + 128] -= update[:, 128 * i : 128 * i + 128]


SMALL = 32
W_ROW, K_ROW = 16, 19
LEVEL_ROW = 3


def put_split(ref, at, row):
    for n, part in enumerate(split3(row)):
        ref[at + n : at + n + 1, :] = part


def get_split(ref, at):
    h, m, l = (ref[at + n : at + n + 1, :].astype(F32) for n in range(3))
    return (h + m) + l


def prepare(block_ref, weight_ref, gate_ref, kept_ref, full, head, tail):
    blocks = block_ref.shape[-1]
    rows = block_ref[...].reshape(4 * blocks, blocks)
    small = jnp.zeros((SMALL, blocks), F32)
    rowid = lax.broadcasted_iota(jnp.int32, (SMALL, blocks), 0)
    for n, part in enumerate(split3(weight_ref[...])):
        small = jnp.where(rowid == W_ROW + n, part.astype(F32), small)
    small = jnp.where(rowid == K_ROW, kept_ref[...].astype(F32), small).astype(BF16)
    for ref, lo, hi in ((full, 0, 4), (head, 0, 3), (tail, 1, 4)):
        size = (hi - lo) * blocks
        ref[0:size, :] = rows[lo * blocks : hi * blocks]
        ref[size : size + SMALL, :] = small
        ref[size : size + 16, 0:16] = gate_ref[...].astype(BF16)


def bond_body(
    a_ref, b_ref, below, here, above, kept, gate_rows, scaled, theta, matrix, proj, work, iso, left,
    gate_stage, gates, sem
):
    blocks = b_ref.shape[-1]
    gate_stage[...] = gate_rows.astype(F32)
    copy = pltpu.make_async_copy(gate_stage, gates, sem)
    copy.start()
    copy.wait()
    for first, count, w in ((0, 3, below), (3, 4, here), (7, 3, above)):
        rows = slice(first * blocks, (first + count) * blocks)
        scaled[rows, :] = (a_ref[rows, :].astype(F32) * w).astype(BF16)
    for (distance, q), (right, first_row, count, first) in PIECES.items():
        product = dot(
            scaled[first_row * blocks : (first_row + count) * blocks, :],
            b_ref[right * blocks : (right + 1) * blocks, :],
            ((1,), (0,)),
        )
        slot = SLOTS[distance, first, q]
        theta[slot * blocks : (slot + count) * blocks, :] = (
            product * (1.0 / math.sqrt(blocks))
        ).astype(BF16)

    def gate(a, b, p, q):
        return gates[4 * a + b, 4 * p + q]

    step = 16

    @pl.loop(0, blocks // step)
    def mix(chunk):
        at = pl.multiple_of(chunk * step, step)
        for half in range(blocks // 128):
            cut = slice(128 * half, 128 * half + 128)
            held = {}

            def term(distance, p, q):
                slot = SLOTS[distance, p, q]
                if slot not in held:
                    place = pl.ds(pl.multiple_of(slot * blocks + at, step), step)
                    held[slot] = theta[place, cut].astype(F32)
                return held[slot]

            for total in range(5):
                for a in range(4):
                    for b in range(4):
                        if CHARGE[a] + CHARGE[b] != total:
                            continue
                        value = None
                        for distance, p, q in TERMS[a, b]:
                            part = gate(a, b, p, q) * term(distance, p, q)
                            value = part if value is None else value + part
                        matrix[
                            pl.ds(pl.multiple_of(a * blocks + at, step), step),
                            b * blocks + 128 * half : b * blocks + 128 * half + 128,
                        ] = value.astype(BF16)
                held.clear()

    basis = a_ref[3 * blocks : 7 * blocks, :]
    projected = dot(basis, matrix[...], ((0,), (0,)))
    slot_id = lax.broadcasted_iota(jnp.int32, projected.shape, 0).astype(F32)
    projected = jnp.where(slot_id < kept, projected, 0.0)
    proj[...] = projected
    ri = lax.broadcasted_iota(jnp.int32, (blocks, blocks), 0)
    ci = lax.broadcasted_iota(jnp.int32, (blocks, blocks), 1)
    eye = jnp.where(ri == ci, 1.0, 0.0).astype(F32)
    work[:, :blocks] = dot(projected, projected, ((1,), (1,)), HIGHEST) + eye
    work[:, blocks:] = eye
    factor_rows(work, blocks)
    ortho = dot(work[:, blocks:], proj[...], ((1,), (0,)), HIGHEST)
    ortho = (ortho * math.sqrt(4 * blocks)).astype(BF16)
    for p in range(4):
        iso[p * blocks : (p + 1) * blocks, :] = ortho[:, p * blocks : (p + 1) * blocks]
    carried = dot(matrix[...], ortho, ((1,), (1,))) * (1.0 / math.sqrt(4 * blocks))
    level = jnp.sqrt(jnp.mean(carried * carried, axis=0, keepdims=True) + 1e-06)
    left[...] = (carried / level).astype(BF16)
    return level


def first_kernel(
    own, core, mirror, mirror_core, near, next_one, next_two,
    iso_msg, iso_three, left, left_three, small_out,
    a_ref, b_ref, small, scaled, theta, matrix, proj, work, gate_stage, gates, sems, sem,
):
    x = lax.axis_index("loop") % 2
    c = lax.axis_index("inner") % 2
    blocks = a_ref.shape[-1]
    plans = {
        0: [
            (a_ref, 0, near, 0, 3), (a_ref, 3, own, 0, 4), (a_ref, 7, core, 1, 3),
            (b_ref, 0, mirror, 0, 3), (b_ref, 3, mirror_core, 0, 4), (b_ref, 7, next_one, 0, 3),
        ],
        1: [
            (a_ref, 0, mirror, 0, 3), (a_ref, 3, mirror_core, 0, 4), (a_ref, 7, next_two, 0, 3),
            (b_ref, 0, core, 0, 3), (b_ref, 3, near, 0, 4), (b_ref, 7, next_one, 0, 3),
        ],
    }
    smalls = {
        0: [near, own, core, mirror, mirror_core],
        1: [mirror, mirror_core, next_two, core, near],
    }

    def move(source, at, target, to, rows, n):
        return pltpu.make_async_copy(
            source.at[pl.ds(at, rows)], target.at[pl.ds(to, rows)], sems.at[n]
        )

    @pl.when(c == 0)
    def _():
        for role in (0, 1):

            @pl.when(x == role)
            def _(role=role):
                for n, (target, to, source, at, count) in enumerate(plans[role]):
                    move(source, at * blocks, target, to * blocks, count * blocks, n).start()
                for n, source in enumerate(smalls[role]):
                    move(source, source.shape[0] - SMALL, small, n * SMALL, SMALL, 6 + n).start()

        for n, (target, to, _, _, count) in enumerate(plans[0]):
            move(own, 0, target, to * blocks, count * blocks, n).wait()
        for n in range(5):
            move(own, 0, small, n * SMALL, SMALL, 6 + n).wait()
        below, here, above = (get_split(small, n * SMALL + W_ROW) for n in range(3))
        kept = small[SMALL + K_ROW : SMALL + K_ROW + 1, 0:1].astype(F32)
        level = bond_body(
            a_ref, b_ref, below, here, above, kept, small[SMALL : SMALL + 16, 0:128],
            scaled, theta, matrix, proj, work, iso_msg, left, gate_stage, gates, sem,
        )
        iso_three[0 : 3 * blocks, :] = iso_msg[blocks : 4 * blocks, :]
        left_three[...] = left[blocks : 4 * blocks, :]
        for ref in (iso_msg, iso_three):
            base = ref.shape[0] - SMALL
            ref[base : base + SMALL, :] = jnp.zeros((SMALL, blocks), BF16)
            put_split(ref, base, get_split(small, 3 * SMALL + W_ROW))
            put_split(ref, base + LEVEL_ROW, level)
        small_out[...] = small[3 * SMALL : 5 * SMALL, :]


def as_column(row):
    return jnp.broadcast_to(row, (row.shape[1], row.shape[1])).T


def second_kernel(
    iso_0, iso_1, iso_2, left_0, left_1, left_2, small_in,
    mid, last, first, whole,
    a_ref, b_ref, small, scaled, theta, matrix, proj, work, gate_stage, gates, sems, sem,
    iso, left,
):
    c = lax.axis_index("inner") % 2
    blocks = a_ref.shape[-1]
    moves = [
        (iso_1, 0, a_ref, 0, 1), (iso_2, 0, a_ref, 1, 2), (iso_0, 0, a_ref, 3, 1),
        (iso_1, 1, a_ref, 4, 2), (iso_2, 2, a_ref, 6, 1), (iso_0, 1, a_ref, 7, 2),
        (iso_1, 3, a_ref, 9, 1), (left_0, 0, b_ref, 0, 3), (left_1, 0, b_ref, 3, 4),
        (left_2, 0, b_ref, 7, 3),
    ]

    @pl.when(c == 0)
    def _():
        copies = [
            pltpu.make_async_copy(
                source.at[pl.ds(at * blocks, count * blocks)],
                target.at[pl.ds(to * blocks, count * blocks)],
                sems.at[n],
            )
            for n, (source, at, target, to, count) in enumerate(moves)
        ]
        for n, source in enumerate((iso_0, iso_1, iso_2)):
            copies.append(
                pltpu.make_async_copy(
                    source.at[pl.ds(source.shape[0] - SMALL, SMALL)],
                    small.at[pl.ds(n * SMALL, SMALL)],
                    sems.at[10 + n],
                )
            )
        for copy in copies:
            copy.start()
        for copy in copies:
            copy.wait()
        below = get_split(small, SMALL)
        here, above = (get_split(small_in, n * SMALL + W_ROW) for n in range(2))
        kept = small_in[K_ROW : K_ROW + 1, 0:1].astype(F32)
        level = bond_body(
            a_ref, b_ref, below, here, above, kept, small_in[0:16, 0:128],
            scaled, theta, matrix, proj, work, iso, left, gate_stage, gates, sem,
        )
        scales = [as_column(get_split(small, n * SMALL + LEVEL_ROW)) for n in range(3)]
        column = as_column(level)
        for p in range(4):
            rows = slice(p * blocks, (p + 1) * blocks)
            whole[rows, :] = (left[rows, :].astype(F32) * scales[CHARGE[p]]).astype(BF16)
        for ref, lo, hi in ((first, 0, 1), (mid, 1, 3), (last, 3, 4)):
            for p in range(lo, hi):
                value = iso[p * blocks : (p + 1) * blocks, :].astype(F32) * column
                ref[(p - lo) * blocks : (p - lo + 1) * blocks, :] = value.astype(BF16)
        for ref, value in ((first, get_split(small, LEVEL_ROW)), (whole, level)):
            base = ref.shape[0] - SMALL
            ref[base : base + SMALL, :] = jnp.zeros((SMALL, blocks), BF16)
            put_split(ref, base + LEVEL_ROW, value)


def final_kernel(first_mine, mid, last, first, whole, level_mine, level_far, out, weights, small, sems):
    x = lax.axis_index("loop") % 2
    c = lax.axis_index("inner") % 2
    blocks = out.shape[-1]
    plans = {
        (0, 0): [(first_mine, 0, 1), (mid, 1, 2), (last, 3, 1), (level_mine, 0, 0)],
        (0, 1): [(first, 0, 1), (mid, 1, 2), (last, 3, 1), (level_far, 0, 0)],
        (1, 0): [(whole, 0, 4), (whole, 0, 0)],
        (1, 1): [(whole, 0, 4), (whole, 0, 0)],
    }
    for (role, core), plan in plans.items():

        @pl.when(jnp.logical_and(x == role, c == core))
        def _(plan=plan):
            copies = []
            for n, (source, to, count) in enumerate(plan):
                if count:
                    rows, goal = pl.ds(0, count * blocks), out.at[pl.ds(to * blocks, count * blocks)]
                else:
                    rows, goal = pl.ds(source.shape[0] - SMALL, SMALL), small
                copies.append(pltpu.make_async_copy(source.at[rows], goal, sems.at[n]))
            for copy in copies:
                copy.start()
            for copy in copies:
                copy.wait()

    weights[...] = get_split(small, LEVEL_ROW)


def scratch(blocks):
    return [
        pltpu.VMEM((10 * blocks, blocks), BF16),
        pltpu.VMEM((10 * blocks, blocks), BF16),
        pltpu.VMEM((5 * SMALL, blocks), BF16),
        pltpu.VMEM((10 * blocks, blocks), BF16),
        pltpu.VMEM((SLOT_COUNT * blocks, blocks), BF16),
        pltpu.VMEM((4 * blocks, 4 * blocks), BF16),
        pltpu.VMEM((blocks, 4 * blocks), F32),
        pltpu.VMEM((blocks, 2 * blocks), F32),
        pltpu.VMEM((16, 128), F32),
        pltpu.SMEM((16, 128), F32),
        pltpu.SemaphoreType.DMA((13,)),
        pltpu.SemaphoreType.DMA,
    ]


def vmem():
    return pl.BlockSpec(memory_space=pltpu.VMEM)


def hbm():
    return pl.BlockSpec(memory_space=pl.ANY)


def params():
    return pltpu.CompilerParams(vmem_limit_bytes=VMEM_BYTES)


def per_device(loops, inners, site_blocks, bond_weights, bond_gates, kept_slots):
    blocks = site_blocks.shape[-1]

    def rows(count, small=0):
        return jax.ShapeDtypeStruct((count * blocks + small, blocks), BF16)

    def send(value, where):
        route = []
        for l in range(loops):
            for i in range(inners):
                source = where(l, i)
                if source is not None:
                    sl, si = source
                    route.append(((sl % loops) * inners + si % inners, l * inners + i))
        return lax.ppermute(value, AXES, route)

    def worker(where):
        return lambda l, i: where(l, i) if i % 2 == 0 else None

    full, head, tail = pl.pallas_call(
        prepare,
        out_shape=(rows(4, SMALL), rows(3, SMALL), rows(3, SMALL)),
        in_specs=[vmem()] * 4,
        out_specs=(vmem(),) * 3,
        name="prepare",
    )(site_blocks[0, 0], bond_weights[0], bond_gates[0], kept_slots)

    core = send(full, worker(lambda l, i: (l, i + 1)))
    mirror = send(head, worker(lambda l, i: (l ^ 1, i)))
    mirror_core = send(full, worker(lambda l, i: (l ^ 1, i + 1)))
    near = send(full, worker(lambda l, i: (l, i - 1) if l % 2 == 0 else (l, i + 2)))
    next_one = send(tail, worker(lambda l, i: (l + 1, i + 2) if l % 2 == 0 else (l, i + 3)))
    next_two = send(tail, worker(lambda l, i: None if l % 2 == 0 else (l - 1, i + 2)))

    iso_msg, iso_three, left, left_three, small = pl.pallas_call(
        first_kernel,
        out_shape=(
            rows(4, SMALL), rows(3, SMALL), rows(4), rows(3),
            jax.ShapeDtypeStruct((2 * SMALL, blocks), BF16),
        ),
        in_specs=[hbm()] * 7,
        out_specs=(vmem(),) * 5,
        scratch_shapes=scratch(blocks),
        compiler_params=params(),
        name="first_bond",
    )(full, core, mirror, mirror_core, near, next_one, next_two)

    iso_1 = send(iso_msg, worker(lambda l, i: (l + 1, i - 2) if l % 2 == 0 else (l - 1, i)))
    iso_2 = send(iso_three, worker(lambda l, i: (l, i - 2)))
    left_1 = send(left, worker(lambda l, i: (l + 3, i) if l % 2 == 0 else (l + 1, i + 2)))
    left_2 = send(left_three, worker(lambda l, i: (l + 2, i + 2)))
    left_0 = left if loops == 2 else send(left, worker(lambda l, i: (l + 2, i)))

    mid, last, first, whole = pl.pallas_call(
        second_kernel,
        out_shape=(rows(2), rows(1), rows(1, SMALL), rows(4, SMALL)),
        in_specs=[hbm()] * 6 + [vmem()],
        out_specs=(vmem(),) * 4,
        scratch_shapes=scratch(blocks)
        + [pltpu.VMEM((4 * blocks, blocks), BF16), pltpu.VMEM((4 * blocks, blocks), BF16)],
        compiler_params=params(),
        name="second_bond",
    )(iso_msg, iso_1, iso_2, left_0, left_1, left_2, small)

    def mid_from(l, i):
        if l % 2:
            return None
        return (l - 1, i - 2) if i % 2 == 0 else (l - 2, i - 1)

    def last_from(l, i):
        if l % 2:
            return None
        return (l - 2, i - 2) if i % 2 == 0 else (l - 1, i - 3)

    def first_from(l, i):
        return (l - 1, i - 1) if l % 2 == 0 and i % 2 else None

    def whole_from(l, i):
        if l % 2 == 0:
            return None
        return (l - 1, i) if i % 2 == 0 else (l, i - 1)

    mid_r = send(mid, mid_from)
    last_r = send(last, last_from)
    first_r = send(first, first_from)
    whole_r = send(whole, whole_from)
    if loops == 2:
        first_mine, level_far = first, first_r
    else:
        first_mine = send(first, worker(lambda l, i: (l - 2, i) if l % 2 == 0 else None))
        level_far = send(
            iso_msg[4 * blocks :], lambda l, i: (l + 1, i - 1) if l % 2 == 0 and i % 2 else None
        )
    sites, weights = pl.pallas_call(
        final_kernel,
        out_shape=(rows(4), jax.ShapeDtypeStruct((1, blocks), F32)),
        in_specs=[hbm()] * 7,
        out_specs=(vmem(),) * 2,
        scratch_shapes=[pltpu.VMEM((SMALL, blocks), BF16), pltpu.SemaphoreType.DMA((4,))],
        name="assemble",
    )(first_mine, mid_r, last_r, first_r, whole_r, iso_msg, level_far)
    return sites.reshape(1, 1, 4, blocks, blocks), weights[None]


def solution(mesh):
    return jax.shard_map(
        functools.partial(per_device, mesh.shape["loop"], mesh.shape["inner"]),
        mesh=mesh,
        in_specs=(
            P("loop", "inner", None, None, None),
            P("loop", "inner", None),
            P("loop", None, None),
            P("loop", "inner"),
        ),
        out_specs=(P("loop", "inner", None, None, None), P("loop", "inner", None)),
        check_vma=False,
    )
```

```python
import functools
import math

import jax
import jax.numpy as jnp
import numpy as np
from jax import lax
from jax.experimental import pallas as pl
from jax.experimental.pallas import tpu as pltpu
from jax.sharding import PartitionSpec as P

CHARGE = (0, 1, 1, 2)
AXES = ("loop", "inner")
BF16, F32 = jnp.bfloat16, jnp.float32
VMEM_BYTES = 60 << 20
HIGHEST = lax.Precision.HIGHEST


def gate_terms():
    table = {}
    for a in range(4):
        for b in range(4):
            table[a, b] = [
                (CHARGE[p] - CHARGE[a], p, q)
                for p in range(4)
                for q in range(4)
                if CHARGE[p] + CHARGE[q] == CHARGE[a] + CHARGE[b]
                and abs(CHARGE[p] - CHARGE[a]) <= 1
            ]
    return table


TERMS = gate_terms()
PIECES = {
    (0, 0): (0, 3, 4, 0),
    (0, 1): (4, 3, 4, 0),
    (0, 2): (5, 3, 4, 0),
    (0, 3): (9, 3, 4, 0),
    (-1, 1): (1, 0, 3, 0),
    (-1, 2): (2, 0, 3, 0),
    (-1, 3): (6, 0, 3, 0),
    (1, 0): (3, 7, 3, 1),
    (1, 1): (7, 7, 3, 1),
    (1, 2): (8, 7, 3, 1),
}


def theta_slots():
    slots, count = {}, 0
    for (distance, q), (_, _, rows, first) in PIECES.items():
        for p in range(rows):
            slots[distance, first + p, q] = count
            count += 1
    return slots, count


SLOTS, SLOT_COUNT = theta_slots()


def dot(a, b, dims, precision=None):
    return lax.dot_general(a, b, (dims, ((), ())), precision=precision, preferred_element_type=F32)


def split3(a):
    h = a.astype(BF16)
    r = a - h.astype(F32)
    m = r.astype(BF16)
    return h, m, (r - m.astype(F32)).astype(BF16)


def factor_rows(work, size, panel=32):
    rowid = lax.broadcasted_iota(jnp.int32, (panel, 128), 0)
    for start in range(0, size, panel):
        low = start < size // 2
        chunks = [0, 1, 2] if low else [1, 2, 3]
        rows = [work[start : start + panel, 128 * c : 128 * c + 128] for c in chunks]
        pivots = jnp.ones((panel, 128), F32)
        for group in range(panel // 8):
            base = start % 128 + 8 * group
            cols = [
                jnp.broadcast_to(rows[0][:, base + k : base + k + 1], (panel, 128))
                for k in range(8)
            ]
            for j in range(8):
                at = 8 * group + j
                pivot = cols[j][at : at + 1, :]
                factor = jnp.where(rowid > at, cols[j], 0.0) * (1.0 / pivot)
                for k in range(j + 1, 8):
                    cols[k] = cols[k] - factor * cols[k][at : at + 1, :]
                rows = [x - factor * x[at : at + 1, :] for x in rows]
                pivots = jnp.where(rowid == at, pivot, pivots)
        scale = lax.rsqrt(pivots)
        rows = [x * scale for x in rows]
        for c, x in zip(chunks, rows):
            work[start : start + panel, 128 * c : 128 * c + 128] = x
        after = start + panel
        if after < size:
            h, m, l = split3(jnp.concatenate(rows, axis=1))
            right = jnp.concatenate([h, m, h, l, h, m], axis=0)
            left = jnp.concatenate([h, h, m, h, l, m], axis=0)
            first = 128 * chunks[0]
            for lo, hi in ((after, after + panel), (after + panel, size)):
                if lo < hi:
                    update = dot(left[:, lo - first : hi - first], right, ((0,), (0,)))
                    for i, c in enumerate(chunks):
                        work[lo:hi, 128 * c : 128 * c + 128] -= update[:, 128 * i : 128 * i + 128]


SMALL = 32
W_ROW, K_ROW = 16, 19
LEVEL_ROW = 3


def put_split(ref, at, row):
    for n, part in enumerate(split3(row)):
        ref[at + n : at + n + 1, :] = part


def get_split(ref, at):
    h, m, l = (ref[at + n : at + n + 1, :].astype(F32) for n in range(3))
    return (h + m) + l


def prepare(block_ref, weight_ref, gate_ref, kept_ref, full, three_a, three_b):
    x = lax.axis_index("loop") % 2
    c = lax.axis_index("inner") % 2
    blocks = block_ref.shape[-1]
    small = jnp.zeros((SMALL, blocks), F32)
    rowid = lax.broadcasted_iota(jnp.int32, (SMALL, blocks), 0)
    for n, part in enumerate(split3(weight_ref[...])):
        small = jnp.where(rowid == W_ROW + n, part.astype(F32), small)
    small = jnp.where(rowid == K_ROW, kept_ref[...].astype(F32), small).astype(BF16)
    shift = jnp.where(jnp.logical_and(x == 1, c == 1), 1, 0)
    for n in range(4):
        full[n * blocks : (n + 1) * blocks, :] = block_ref[n]
    for n in range(3):
        three_a[n * blocks : (n + 1) * blocks, :] = block_ref[n + shift]
        three_b[n * blocks : (n + 1) * blocks, :] = block_ref[n + 1]
    for ref in (full, three_a, three_b):
        base = ref.shape[0] - SMALL
        ref[base : base + SMALL, :] = small
        ref[base : base + 16, 0:16] = gate_ref[...].astype(BF16)


def bond_body(
    a_ref, b_ref, below, here, above, kept, gate_rows, scaled, theta, matrix, proj, work, iso, left,
    gate_stage, gates, sem
):
    blocks = b_ref.shape[-1]
    gate_stage[...] = gate_rows.astype(F32)
    copy = pltpu.make_async_copy(gate_stage, gates, sem)
    copy.start()
    copy.wait()
    for first, count, w in ((0, 3, below), (3, 4, here), (7, 3, above)):
        rows = slice(first * blocks, (first + count) * blocks)
        scaled[rows, :] = (a_ref[rows, :].astype(F32) * w).astype(BF16)
    for (distance, q), (right, first_row, count, first) in PIECES.items():
        product = dot(
            scaled[first_row * blocks : (first_row + count) * blocks, :],
            b_ref[right * blocks : (right + 1) * blocks, :],
            ((1,), (0,)),
        )
        slot = SLOTS[distance, first, q]
        theta[slot * blocks : (slot + count) * blocks, :] = (
            product * (1.0 / math.sqrt(blocks))
        ).astype(BF16)

    def gate(a, b, p, q):
        return gates[4 * a + b, 4 * p + q]

    step = 16

    @pl.loop(0, blocks // step)
    def mix(chunk):
        at = pl.multiple_of(chunk * step, step)
        for half in range(blocks // 128):
            cut = slice(128 * half, 128 * half + 128)
            held = {}

            def term(distance, p, q):
                slot = SLOTS[distance, p, q]
                if slot not in held:
                    place = pl.ds(pl.multiple_of(slot * blocks + at, step), step)
                    held[slot] = theta[place, cut].astype(F32)
                return held[slot]

            for total in range(5):
                for a in range(4):
                    for b in range(4):
                        if CHARGE[a] + CHARGE[b] != total:
                            continue
                        value = None
                        for distance, p, q in TERMS[a, b]:
                            part = gate(a, b, p, q) * term(distance, p, q)
                            value = part if value is None else value + part
                        matrix[
                            pl.ds(pl.multiple_of(a * blocks + at, step), step),
                            b * blocks + 128 * half : b * blocks + 128 * half + 128,
                        ] = value.astype(BF16)
                held.clear()

    basis = a_ref[3 * blocks : 7 * blocks, :]
    projected = dot(basis, matrix[...], ((0,), (0,)))
    slot_id = lax.broadcasted_iota(jnp.int32, projected.shape, 0).astype(F32)
    projected = jnp.where(slot_id < kept, projected, 0.0)
    proj[...] = projected
    ri = lax.broadcasted_iota(jnp.int32, (blocks, blocks), 0)
    ci = lax.broadcasted_iota(jnp.int32, (blocks, blocks), 1)
    eye = jnp.where(ri == ci, 1.0, 0.0).astype(F32)
    work[:, :blocks] = dot(projected, projected, ((1,), (1,)), HIGHEST) + eye
    work[:, blocks:] = eye
    factor_rows(work, blocks)
    ortho = dot(work[:, blocks:], proj[...], ((1,), (0,)), HIGHEST)
    ortho = (ortho * math.sqrt(4 * blocks)).astype(BF16)
    for p in range(4):
        iso[p * blocks : (p + 1) * blocks, :] = ortho[:, p * blocks : (p + 1) * blocks]
    carried = dot(matrix[...], ortho, ((1,), (1,))) * (1.0 / math.sqrt(4 * blocks))
    level = jnp.sqrt(jnp.mean(carried * carried, axis=0, keepdims=True) + 1e-06)
    left[...] = (carried / level).astype(BF16)
    return level


def first_kernel(
    own, edge, cross, mirror_odd, mirror_even, beside,
    iso_msg, iso_three, left, left_three, local,
    a_ref, b_ref, small, scaled, theta, matrix, proj, work, gate_stage, gates, sems, sem,
):
    x = lax.axis_index("loop") % 2
    c = lax.axis_index("inner") % 2
    blocks = a_ref.shape[-1]
    plans = {
        0: [
            (a_ref, 0, edge, 0, 3), (a_ref, 3, own, 0, 4), (a_ref, 7, beside, 1, 3),
            (b_ref, 0, mirror_even, 0, 3), (b_ref, 3, mirror_odd, 0, 4), (b_ref, 7, cross, 0, 3),
        ],
        1: [
            (a_ref, 0, mirror_even, 0, 3), (a_ref, 3, mirror_odd, 0, 4), (a_ref, 7, cross, 0, 3),
            (b_ref, 0, own, 0, 3), (b_ref, 3, beside, 0, 4), (b_ref, 7, edge, 0, 3),
        ],
    }
    smalls = {
        0: [edge, own, beside, mirror_even, mirror_odd],
        1: [mirror_even, mirror_odd, cross, own, beside],
    }

    def move(source, at, target, to, rows, n):
        return pltpu.make_async_copy(
            source.at[pl.ds(at, rows)], target.at[pl.ds(to, rows)], sems.at[n]
        )

    @pl.when(x == c)
    def _():
        for role in (0, 1):

            @pl.when(x == role)
            def _(role=role):
                for n, (target, to, source, at, count) in enumerate(plans[role]):
                    move(source, at * blocks, target, to * blocks, count * blocks, n).start()
                for n, source in enumerate(smalls[role]):
                    move(source, source.shape[0] - SMALL, small, n * SMALL, SMALL, 6 + n).start()

        for n, (target, to, _, _, count) in enumerate(plans[0]):
            move(own, 0, target, to * blocks, count * blocks, n).wait()
        for n in range(5):
            move(own, 0, small, n * SMALL, SMALL, 6 + n).wait()
        below, here, above = (get_split(small, n * SMALL + W_ROW) for n in range(3))
        kept = small[SMALL + K_ROW : SMALL + K_ROW + 1, 0:1].astype(F32)
        level = bond_body(
            a_ref, b_ref, below, here, above, kept, small[SMALL : SMALL + 16, 0:128],
            scaled, theta, matrix, proj, work, iso_msg, left, gate_stage, gates, sem,
        )
        iso_three[0 : 3 * blocks, :] = iso_msg[blocks : 4 * blocks, :]
        left_three[...] = left[blocks : 4 * blocks, :]
        local[0 : 3 * blocks, :] = iso_msg[0 : 3 * blocks, :]
        local[3 * blocks : 6 * blocks, :] = left[0 : 3 * blocks, :]
        local[6 * blocks : 6 * blocks + 2 * SMALL, :] = small[3 * SMALL : 5 * SMALL, :]
        for ref in (iso_msg, iso_three, local):
            base = ref.shape[0] - SMALL
            ref[base : base + SMALL, :] = jnp.zeros((SMALL, blocks), BF16)
            put_split(ref, base, get_split(small, 3 * SMALL + W_ROW))
            put_split(ref, base + LEVEL_ROW, level)


def as_column(row):
    return jnp.broadcast_to(row, (row.shape[1], row.shape[1])).T


def second_kernel(
    local, iso_1, iso_2, left_0, left_1, left_2,
    mid, last, first, whole,
    a_ref, b_ref, small, scaled, theta, matrix, proj, work, gate_stage, gates, sems, sem,
    iso, left,
):
    x = lax.axis_index("loop") % 2
    c = lax.axis_index("inner") % 2
    blocks = a_ref.shape[-1]
    moves = [
        (source, at * blocks, target, to * blocks, count * blocks)
        for source, at, target, to, count in (
            (iso_1, 0, a_ref, 0, 1), (iso_2, 0, a_ref, 1, 2), (local, 0, a_ref, 3, 1),
            (iso_1, 1, a_ref, 4, 2), (iso_2, 2, a_ref, 6, 1), (local, 1, a_ref, 7, 2),
            (iso_1, 3, a_ref, 9, 1), (left_0, left_0.shape[0] // blocks - 3, b_ref, 0, 3),
            (left_1, 0, b_ref, 3, 4), (left_2, 0, b_ref, 7, 3),
        )
    ]
    moves.append((local, 6 * blocks, small, 0, 3 * SMALL))
    for n, source in enumerate((iso_1, iso_2)):
        moves.append((source, source.shape[0] - SMALL, small, (3 + n) * SMALL, SMALL))

    @pl.when(x != c)
    def _():
        copies = [
            pltpu.make_async_copy(
                source.at[pl.ds(at, rows)], target.at[pl.ds(to, rows)], sems.at[n]
            )
            for n, (source, at, target, to, rows) in enumerate(moves)
        ]
        for copy in copies:
            copy.start()
        for copy in copies:
            copy.wait()
        below = get_split(small, 3 * SMALL)
        here, above = (get_split(small, n * SMALL + W_ROW) for n in range(2))
        kept = small[K_ROW : K_ROW + 1, 0:1].astype(F32)
        level = bond_body(
            a_ref, b_ref, below, here, above, kept, small[0:16, 0:128],
            scaled, theta, matrix, proj, work, iso, left, gate_stage, gates, sem,
        )
        scales = [as_column(get_split(small, n * SMALL + LEVEL_ROW)) for n in range(2, 5)]
        column = as_column(level)
        for p in range(4):
            rows = slice(p * blocks, (p + 1) * blocks)
            whole[rows, :] = (left[rows, :].astype(F32) * scales[CHARGE[p]]).astype(BF16)
        for ref, lo, hi in ((first, 0, 1), (mid, 1, 3), (last, 3, 4)):
            for p in range(lo, hi):
                value = iso[p * blocks : (p + 1) * blocks, :].astype(F32) * column
                ref[(p - lo) * blocks : (p - lo + 1) * blocks, :] = value.astype(BF16)
        for ref, value in ((first, get_split(small, 2 * SMALL + LEVEL_ROW)), (whole, level)):
            base = ref.shape[0] - SMALL
            ref[base : base + SMALL, :] = jnp.zeros((SMALL, blocks), BF16)
            put_split(ref, base + LEVEL_ROW, value)


def final_kernel(
    first, mid_mine, mid, last, whole, level_mine, level_far, out, weights, small, sems
):
    x = lax.axis_index("loop") % 2
    c = lax.axis_index("inner") % 2
    blocks = out.shape[-1]
    plans = {
        (0, 0): [(first, 0, 1), (mid, 1, 2), (last, 3, 1), (level_mine, 0, 0)],
        (0, 1): [(first, 0, 1), (mid_mine, 1, 2), (last, 3, 1), (level_far, 0, 0)],
        (1, 0): [(whole, 0, 4), (whole, 0, 0)],
        (1, 1): [(whole, 0, 4), (whole, 0, 0)],
    }
    for (role, core), plan in plans.items():

        @pl.when(jnp.logical_and(x == role, c == core))
        def _(plan=plan):
            copies = []
            for n, (source, to, count) in enumerate(plan):
                if count:
                    rows, goal = pl.ds(0, count * blocks), out.at[pl.ds(to * blocks, count * blocks)]
                else:
                    rows, goal = pl.ds(source.shape[0] - SMALL, SMALL), small
                copies.append(pltpu.make_async_copy(source.at[rows], goal, sems.at[n]))
            for copy in copies:
                copy.start()
            for copy in copies:
                copy.wait()

    weights[...] = get_split(small, LEVEL_ROW)


def scratch(blocks):
    return [
        pltpu.VMEM((10 * blocks, blocks), BF16),
        pltpu.VMEM((10 * blocks, blocks), BF16),
        pltpu.VMEM((5 * SMALL, blocks), BF16),
        pltpu.VMEM((10 * blocks, blocks), BF16),
        pltpu.VMEM((SLOT_COUNT * blocks, blocks), BF16),
        pltpu.VMEM((4 * blocks, 4 * blocks), BF16),
        pltpu.VMEM((blocks, 4 * blocks), F32),
        pltpu.VMEM((blocks, 2 * blocks), F32),
        pltpu.VMEM((16, 128), F32),
        pltpu.SMEM((16, 128), F32),
        pltpu.SemaphoreType.DMA((13,)),
        pltpu.SemaphoreType.DMA,
    ]


def vmem():
    return pl.BlockSpec(memory_space=pltpu.VMEM)


def hbm():
    return pl.BlockSpec(memory_space=pl.ANY)


def params():
    return pltpu.CompilerParams(vmem_limit_bytes=VMEM_BYTES)


def per_device(loops, inners, site_blocks, bond_weights, bond_gates, kept_slots):
    blocks = site_blocks.shape[-1]

    def rows(count, small=0):
        return jax.ShapeDtypeStruct((count * blocks + small, blocks), BF16)

    def send(value, where):
        route = []
        for l in range(loops):
            for i in range(inners):
                source = where(l, i)
                if source is not None:
                    sl, si = source
                    route.append(((sl % loops) * inners + si % inners, l * inners + i))
        return lax.ppermute(value, AXES, route)

    def to_first(where):
        return lambda l, i: where(l, i // 2) if i % 2 == l % 2 else None

    def to_second(where):
        return lambda l, i: where(l, i // 2) if i % 2 != l % 2 else None

    full, three_a, three_b = pl.pallas_call(
        prepare,
        out_shape=(rows(4, SMALL), rows(3, SMALL), rows(3, SMALL)),
        in_specs=[vmem()] * 4,
        out_specs=(vmem(),) * 3,
        compiler_params=params(),
        name="prepare",
    )(site_blocks[0, 0], bond_weights[0], bond_gates[0], kept_slots)

    def pick(even, odd):
        return to_first(lambda l, k: (even if l % 2 == 0 else odd)(l, k))

    edge = send(
        three_a, pick(lambda l, k: (l, 2 * k - 1), lambda l, k: (l, 2 * k + 3))
    )
    cross = send(
        three_b, pick(lambda l, k: (l + 1, 2 * k + 2), lambda l, k: (l - 1, 2 * k + 2))
    )
    mirror_odd = send(full, to_first(lambda l, k: (l ^ 1, 2 * k + 1)))
    mirror_even = send(three_a, to_first(lambda l, k: (l ^ 1, 2 * k)))
    beside = send(full, pick(lambda l, k: (l, 2 * k + 1), lambda l, k: (l, 2 * k + 2)))

    iso_msg, iso_three, left, left_three, local = pl.pallas_call(
        first_kernel,
        out_shape=(rows(4, SMALL), rows(3, SMALL), rows(4), rows(3), rows(6, 3 * SMALL)),
        in_specs=[hbm()] * 6,
        out_specs=(vmem(),) * 5,
        scratch_shapes=scratch(blocks),
        compiler_params=params(),
        name="first_bond",
    )(full, edge, cross, mirror_odd, mirror_even, beside)

    def worker(l, k, d, s):
        sector = 2 * k + l % 2 + s
        return (l - l % 2 + 2 * d + sector % 2, sector // 2 * 2 + sector % 2)

    local_r = send(local, to_second(lambda l, k: worker(l, k, 0, 0)))
    iso_1 = send(iso_msg, to_second(lambda l, k: worker(l, k, 0, -1)))
    iso_2 = send(iso_three, to_second(lambda l, k: worker(l, k, 0, -2)))
    left_1 = send(left, to_second(lambda l, k: worker(l, k, 1, 1)))
    left_2 = send(left_three, to_second(lambda l, k: worker(l, k, 1, 2)))
    if loops == 2:
        left_0 = local_r
    else:
        left_0 = send(left[: 3 * blocks], to_second(lambda l, k: worker(l, k, 1, 0)))

    mid, last, first, whole = pl.pallas_call(
        second_kernel,
        out_shape=(rows(2), rows(1), rows(1, SMALL), rows(4, SMALL)),
        in_specs=[hbm()] * 6,
        out_specs=(vmem(),) * 4,
        scratch_shapes=scratch(blocks)
        + [pltpu.VMEM((4 * blocks, blocks), BF16), pltpu.VMEM((4 * blocks, blocks), BF16)],
        compiler_params=params(),
        name="second_bond",
    )(local_r, iso_1, iso_2, left_0, left_1, left_2)

    def from_second(l, i, d, s):
        sector = i - s
        return (l - l % 2 - 2 * d + sector % 2, sector // 2 * 2 + 1 - sector % 2)

    def right_from(s, cores):
        return lambda l, i: from_second(l, i, 1, s) if l % 2 == 0 and i % 2 in cores else None

    first_r = send(first, right_from(0, (0, 1)))
    mid_r = send(mid, right_from(1, (0,) if loops == 2 else (0, 1)))
    last_r = send(last, right_from(2, (0, 1)))
    whole_r = send(whole, lambda l, i: from_second(l, i, 0, 0) if l % 2 else None)
    if loops == 2:
        mid_mine, level_far = mid, first_r
    else:
        mid_mine = mid_r
        level_far = send(
            iso_msg[4 * blocks :], lambda l, i: (l + 1, i) if l % 2 == 0 and i % 2 else None
        )
    sites, weights = pl.pallas_call(
        final_kernel,
        out_shape=(rows(4), jax.ShapeDtypeStruct((1, blocks), F32)),
        in_specs=[hbm()] * 7,
        out_specs=(vmem(),) * 2,
        scratch_shapes=[pltpu.VMEM((SMALL, blocks), BF16), pltpu.SemaphoreType.DMA((4,))],
        compiler_params=params(),
        name="assemble",
    )(first_r, mid_mine, mid_r, last_r, whole_r, iso_msg, level_far)
    return sites.reshape(1, 1, 4, blocks, blocks), weights[None]


def solution(mesh):
    return jax.shard_map(
        functools.partial(per_device, mesh.shape["loop"], mesh.shape["inner"]),
        mesh=mesh,
        in_specs=(
            P("loop", "inner", None, None, None),
            P("loop", "inner", None),
            P("loop", None, None),
            P("loop", "inner"),
        ),
        out_specs=(P("loop", "inner", None, None, None), P("loop", "inner", None)),
        check_vma=False,
    )
```

```python
import functools
import math

import jax
import jax.numpy as jnp
import numpy as np
from jax import lax
from jax.experimental import pallas as pl
from jax.experimental.pallas import tpu as pltpu
from jax.sharding import PartitionSpec as P

CHARGE = (0, 1, 1, 2)
AXES = ("loop", "inner")
BF16, F32 = jnp.bfloat16, jnp.float32
VMEM_BYTES = 64 << 20
HIGHEST = lax.Precision.HIGHEST


def gate_terms():
    table = {}
    for a in range(4):
        for b in range(4):
            table[a, b] = [
                (CHARGE[p] - CHARGE[a], p, q)
                for p in range(4)
                for q in range(4)
                if CHARGE[p] + CHARGE[q] == CHARGE[a] + CHARGE[b]
                and abs(CHARGE[p] - CHARGE[a]) <= 1
            ]
    return table


TERMS = gate_terms()
PIECES = {
    (0, 0): (0, 3, 4, 0),
    (0, 1): (4, 3, 4, 0),
    (0, 2): (5, 3, 4, 0),
    (0, 3): (9, 3, 4, 0),
    (-1, 1): (1, 0, 3, 0),
    (-1, 2): (2, 0, 3, 0),
    (-1, 3): (6, 0, 3, 0),
    (1, 0): (3, 7, 3, 1),
    (1, 1): (7, 7, 3, 1),
    (1, 2): (8, 7, 3, 1),
}


def theta_slots():
    slots, count = {}, 0
    for (distance, q), (_, _, rows, first) in PIECES.items():
        for p in range(rows):
            slots[distance, first + p, q] = count
            count += 1
    return slots, count


SLOTS, SLOT_COUNT = theta_slots()


def dot(a, b, dims, precision=None):
    return lax.dot_general(a, b, (dims, ((), ())), precision=precision, preferred_element_type=F32)


def split3(a):
    h = a.astype(BF16)
    r = a - h.astype(F32)
    m = r.astype(BF16)
    return h, m, (r - m.astype(F32)).astype(BF16)


def factor_rows(work, size, panel=32):
    tiles = panel // 8
    sub = lax.broadcasted_iota(jnp.int32, (8, 128), 0)
    for start in range(0, size, panel):
        low = start < size // 2
        chunks = [0, 1, 2] if low else [1, 2, 3]
        base = start % 128
        rows = [
            [work[start + 8 * t : start + 8 * t + 8, 128 * c : 128 * c + 128] for c in chunks]
            for t in range(tiles)
        ]

        def column(k):
            return {
                t: jnp.broadcast_to(rows[t][0][:, base + k : base + k + 1], (8, 128))
                for t in range(k // 8, tiles)
            }

        def at(col, k):
            return jnp.broadcast_to(col[k // 8][k % 8 : k % 8 + 1, :], (8, 128))

        pivots = [jnp.ones((8, 128), F32) for _ in range(tiles)]
        cols = {k: column(k) for k in range(8)}
        for g in range(tiles):
            if g + 1 < tiles:
                cols.update({k: column(k) for k in range(8 * g + 8, 8 * g + 16)})

            def below(col, j):
                return {
                    t: (jnp.where(sub > j % 8, v, 0.0) if t == j // 8 else v)
                    for t, v in col.items()
                    if t >= g
                }

            for j in range(8 * g, 8 * g + 8, 2):
                one, two = cols[j], cols[j + 1]
                a, b, c = at(one, j), at(one, j + 1), at(two, j + 1)
                det = a * c - b * b
                ra, rd = 1.0 / a, 1.0 / det
                first = {t: v * ra for t, v in below(one, j).items()}
                ratio = b * ra
                two = {t: two[t] - one[t] * ratio for t in one if t >= g}
                second = {t: v * (a * rd) for t, v in below(two, j + 1).items()}
                for k in cols:
                    if k > j + 1:
                        e1, e2 = at(one, k), at(two, k)
                        cols[k] = {
                            t: v - (first[t] * e1 + second[t] * e2) for t, v in cols[k].items()
                        }
                for i in range(len(chunks)):
                    r = j % 8
                    x0 = jnp.broadcast_to(rows[g][i][r : r + 1, :], (8, 128))
                    x1 = jnp.broadcast_to(rows[g][i][r + 1 : r + 2, :], (8, 128)) - ratio * x0
                    for t in range(g, tiles):
                        rows[t][i] = rows[t][i] - (first[t] * x0 + second[t] * x1)
                pivots[g] = jnp.where(
                    sub == j % 8, a, jnp.where(sub == j % 8 + 1, det * ra, pivots[g])
                )
        done = []
        for t in range(tiles):
            scale = lax.rsqrt(pivots[t])
            done.append([x * scale for x in rows[t]])
            for c, x in zip(chunks, done[t]):
                work[start + 8 * t : start + 8 * t + 8, 128 * c : 128 * c + 128] = x
        after = start + panel
        if after < size:
            h, m, l = split3(
                jnp.concatenate([jnp.concatenate(xs, axis=1) for xs in done], axis=0)
            )
            right = jnp.concatenate([h, m, h, l, h, m], axis=0)
            left = jnp.concatenate([h, h, m, h, l, m], axis=0)
            first = 128 * chunks[0]
            for lo, hi in ((after, after + panel), (after + panel, size)):
                if lo < hi:
                    update = dot(left[:, lo - first : hi - first], right, ((0,), (0,)))
                    for i, c in enumerate(chunks):
                        work[lo:hi, 128 * c : 128 * c + 128] -= update[:, 128 * i : 128 * i + 128]


SMALL = 32
W_ROW, K_ROW = 16, 19
LEVEL_ROW = 3


def put_split(ref, at, row):
    for n, part in enumerate(split3(row)):
        ref[at + n : at + n + 1, :] = part


def get_split(ref, at):
    h, m, l = (ref[at + n : at + n + 1, :].astype(F32) for n in range(3))
    return (h + m) + l


def prepare(block_ref, weight_ref, gate_ref, kept_ref, full, three_a, three_b, rows, small, sems):
    x = lax.axis_index("loop") % 2
    c = lax.axis_index("inner") % 2
    blocks = rows.shape[-1]
    load = pltpu.make_async_copy(block_ref, rows, sems.at[0])
    load.start()
    values = jnp.zeros((SMALL, blocks), F32)
    rowid = lax.broadcasted_iota(jnp.int32, (SMALL, blocks), 0)
    for n, part in enumerate(split3(weight_ref[...])):
        values = jnp.where(rowid == W_ROW + n, part.astype(F32), values)
    small[...] = jnp.where(rowid == K_ROW, kept_ref[...].astype(F32), values).astype(BF16)
    small[0:16, 0:16] = gate_ref[...].astype(BF16)
    load.wait()
    shift = pl.multiple_of(jnp.where(jnp.logical_and(x == 1, c == 1), blocks, 0), blocks)
    copies = []
    for n, (ref, at) in enumerate(((full, 0), (three_a, shift), (three_b, blocks))):
        size = ref.shape[0] - SMALL
        copies.append(
            pltpu.make_async_copy(rows.at[pl.ds(at, size)], ref.at[pl.ds(0, size)], sems.at[1 + n])
        )
        copies.append(
            pltpu.make_async_copy(small, ref.at[pl.ds(size, SMALL)], sems.at[4 + n])
        )
    for copy in copies:
        copy.start()
    for copy in copies:
        copy.wait()


def bond_body(
    a_ref, b_ref, below, here, above, kept, gate_rows, scaled, theta, matrix, proj, work, iso, left,
    gate_stage, gates, sem, right_ready, iso_ready
):
    blocks = b_ref.shape[-1]
    gate_stage[...] = gate_rows.astype(F32)
    copy = pltpu.make_async_copy(gate_stage, gates, sem)
    copy.start()
    for first, count, w in ((3, 4, here), (0, 3, below), (7, 3, above)):
        rows = slice(first * blocks, (first + count) * blocks)
        scaled[rows, :] = (a_ref[rows, :].astype(F32) * w).astype(BF16)
    basis = a_ref[3 * blocks : 7 * blocks, :].T
    right_ready()
    for (distance, q), (right, first_row, count, first) in PIECES.items():
        product = dot(
            scaled[first_row * blocks : (first_row + count) * blocks, :],
            b_ref[right * blocks : (right + 1) * blocks, :],
            ((1,), (0,)),
        )
        slot = SLOTS[distance, first, q]
        theta[slot * blocks : (slot + count) * blocks, :] = (
            product * (1.0 / math.sqrt(blocks))
        ).astype(BF16)
    copy.wait()

    def gate(a, b, p, q):
        return gates[4 * a + b, 4 * p + q]

    step = 16

    @pl.loop(0, blocks // step)
    def mix(chunk):
        at = pl.multiple_of(chunk * step, step)
        for half in range(blocks // 128):
            cut = slice(128 * half, 128 * half + 128)
            held = {}

            def term(distance, p, q):
                slot = SLOTS[distance, p, q]
                if slot not in held:
                    place = pl.ds(pl.multiple_of(slot * blocks + at, step), step)
                    held[slot] = theta[place, cut].astype(F32)
                return held[slot]

            for total in range(5):
                for a in range(4):
                    for b in range(4):
                        if CHARGE[a] + CHARGE[b] != total:
                            continue
                        value = None
                        for distance, p, q in TERMS[a, b]:
                            part = gate(a, b, p, q) * term(distance, p, q)
                            value = part if value is None else value + part
                        matrix[
                            pl.ds(pl.multiple_of(a * blocks + at, step), step),
                            b * blocks + 128 * half : b * blocks + 128 * half + 128,
                        ] = value.astype(BF16)
                held.clear()

    projected = dot(basis, matrix[...], ((1,), (0,)))
    slot_id = lax.broadcasted_iota(jnp.int32, projected.shape, 0).astype(F32)
    h, m, l = split3(jnp.where(slot_id < kept, projected, 0.0))
    for n, part in enumerate((h, m, l)):
        proj[n * blocks : (n + 1) * blocks, :] = part
    ri = lax.broadcasted_iota(jnp.int32, (blocks, blocks), 0)
    ci = lax.broadcasted_iota(jnp.int32, (blocks, blocks), 1)
    eye = jnp.where(ri == ci, 1.0, 0.0).astype(F32)
    outer = ((1,), (1,))
    mixed = dot(h, m, outer) + dot(h, l, outer)
    work[:, :blocks] = (dot(h, h, outer) + dot(m, m, outer)) + (mixed + mixed.T) + eye
    work[:, blocks:] = eye
    factor_rows(work, blocks)
    wh, wm, wl = split3(work[:, blocks:])
    h, m, l = (proj[n * blocks : (n + 1) * blocks, :] for n in range(3))
    inner = ((1,), (0,))
    ortho = (
        dot(jnp.concatenate([wh, wm, wl], axis=1), jnp.concatenate([h, h, h], axis=0), inner)
        + dot(jnp.concatenate([wh, wm], axis=1), jnp.concatenate([m, m], axis=0), inner)
        + dot(wh, l, inner)
    )
    ortho = (ortho * math.sqrt(4 * blocks)).astype(BF16)
    for p in range(4):
        iso[p * blocks : (p + 1) * blocks, :] = ortho[:, p * blocks : (p + 1) * blocks]
    iso_ready()
    carried = dot(matrix[...], ortho, outer) * (1.0 / math.sqrt(4 * blocks))
    level = jnp.sqrt(jnp.mean(carried * carried, axis=0, keepdims=True) + 1e-06)
    left[...] = (carried * (1.0 / level)).astype(BF16)
    return level


def first_kernel(
    own, edge, cross, mirror_odd, mirror_even, beside,
    iso_msg, iso_three, left_msg, left_three, local,
    a_ref, b_ref, small, scaled, theta, matrix, proj, work, gate_stage, gates, sems, sem,
    iso, left, pack,
):
    x = lax.axis_index("loop") % 2
    c = lax.axis_index("inner") % 2
    blocks = a_ref.shape[-1]
    plans = {
        0: [
            (a_ref, 0, edge, 0, 3), (a_ref, 3, own, 0, 4), (a_ref, 7, beside, 1, 3),
            (b_ref, 0, mirror_even, 0, 3), (b_ref, 3, mirror_odd, 0, 4), (b_ref, 7, cross, 0, 3),
        ],
        1: [
            (a_ref, 0, mirror_even, 0, 3), (a_ref, 3, mirror_odd, 0, 4), (a_ref, 7, cross, 0, 3),
            (b_ref, 0, own, 0, 3), (b_ref, 3, beside, 0, 4), (b_ref, 7, edge, 0, 3),
        ],
    }
    smalls = {
        0: [mirror_even, mirror_odd, edge, own, beside],
        1: [own, beside, mirror_even, mirror_odd, cross],
    }

    def move(source, at, target, to, rows, n):
        return pltpu.make_async_copy(
            source.at[pl.ds(at, rows)], target.at[pl.ds(to, rows)], sems.at[n]
        )

    @pl.when(x == c)
    def _():
        for role in (0, 1):

            @pl.when(x == role)
            def _(role=role):
                for n, (target, to, source, at, count) in enumerate(plans[role]):
                    move(source, at * blocks, target, to * blocks, count * blocks, n).start()
                for n, source in enumerate(smalls[role]):
                    move(source, source.shape[0] - SMALL, small, n * SMALL, SMALL, 6 + n).start()

        def arrived(chosen):
            for n, (target, to, _, _, count) in enumerate(plans[0]):
                if target is chosen:
                    move(own, 0, target, to * blocks, count * blocks, n).wait()

        copies = []

        def out(source, at, target, to, count, rest=0):
            rows = count * blocks + rest
            copies.append(move(source, at * blocks, target, to * blocks, rows, 11 + len(copies)))
            copies[-1].start()

        def iso_ready():
            out(iso, 0, iso_msg, 0, 4)
            out(iso, 1, iso_three, 0, 3)
            out(iso, 0, local, 0, 3)

        for n in range(5):
            move(own, 0, small, n * SMALL, SMALL, 6 + n).wait()
        out(small, 0, local, 6, 0, 2 * SMALL)
        below, here, above = (get_split(small, (2 + n) * SMALL + W_ROW) for n in range(3))
        kept = small[3 * SMALL + K_ROW : 3 * SMALL + K_ROW + 1, 0:1].astype(F32)
        arrived(a_ref)
        level = bond_body(
            a_ref, b_ref, below, here, above, kept, small[3 * SMALL : 3 * SMALL + 16, 0:128],
            scaled, theta, matrix, proj, work, iso, left, gate_stage, gates, sem,
            lambda: arrived(b_ref), iso_ready,
        )
        out(left, 0, left_msg, 0, 4)
        out(left, 1, left_three, 0, 3)
        out(left, 0, local, 3, 3)
        pack[...] = jnp.zeros((SMALL, blocks), BF16)
        put_split(pack, 0, get_split(small, W_ROW))
        put_split(pack, LEVEL_ROW, level)
        for ref in (iso_msg, iso_three, local):
            base = ref.shape[0] - SMALL
            copies.append(move(pack, 0, ref, base, SMALL, 11 + len(copies)))
            copies[-1].start()
        for copy in copies:
            copy.wait()


def as_column(row):
    return jnp.broadcast_to(row, (row.shape[1], row.shape[1])).T


def second_kernel(
    local, iso_1, iso_2, left_0, left_1, left_2,
    mid, last, first, whole,
    a_ref, b_ref, small, scaled, theta, matrix, proj, work, gate_stage, gates, sems, sem,
    iso, left,
):
    x = lax.axis_index("loop") % 2
    c = lax.axis_index("inner") % 2
    blocks = a_ref.shape[-1]
    moves = [
        (source, at * blocks, target, to * blocks, count * blocks)
        for source, at, target, to, count in (
            (iso_1, 0, a_ref, 0, 1), (iso_2, 0, a_ref, 1, 2), (local, 0, a_ref, 3, 1),
            (iso_1, 1, a_ref, 4, 2), (iso_2, 2, a_ref, 6, 1), (local, 1, a_ref, 7, 2),
            (iso_1, 3, a_ref, 9, 1), (left_0, left_0.shape[0] // blocks - 3, b_ref, 0, 3),
            (left_1, 0, b_ref, 3, 4), (left_2, 0, b_ref, 7, 3),
        )
    ]
    moves.append((local, 6 * blocks, small, 0, 3 * SMALL))
    for n, source in enumerate((iso_1, iso_2)):
        moves.append((source, source.shape[0] - SMALL, small, (3 + n) * SMALL, SMALL))

    @pl.when(x != c)
    def _():
        copies = [
            pltpu.make_async_copy(
                source.at[pl.ds(at, rows)], target.at[pl.ds(to, rows)], sems.at[n]
            )
            for n, (source, at, target, to, rows) in enumerate(moves)
        ]
        for copy in copies:
            copy.start()

        def arrived(right):
            for copy, (_, _, target, _, _) in zip(copies, moves):
                if (target is b_ref) == right:
                    copy.wait()

        arrived(False)
        below = get_split(small, 3 * SMALL)
        here, above = (get_split(small, n * SMALL + W_ROW) for n in range(2))
        kept = small[K_ROW : K_ROW + 1, 0:1].astype(F32)
        level = bond_body(
            a_ref, b_ref, below, here, above, kept, small[0:16, 0:128],
            scaled, theta, matrix, proj, work, iso, left, gate_stage, gates, sem,
            lambda: arrived(True), lambda: None,
        )
        scales = [as_column(get_split(small, n * SMALL + LEVEL_ROW)) for n in range(2, 5)]
        column = as_column(level)
        for p in range(4):
            rows = slice(p * blocks, (p + 1) * blocks)
            whole[rows, :] = (left[rows, :].astype(F32) * scales[CHARGE[p]]).astype(BF16)
        for ref, lo, hi in ((first, 0, 1), (mid, 1, 3), (last, 3, 4)):
            for p in range(lo, hi):
                value = iso[p * blocks : (p + 1) * blocks, :].astype(F32) * column
                ref[(p - lo) * blocks : (p - lo + 1) * blocks, :] = value.astype(BF16)
        for ref, value in ((first, get_split(small, 2 * SMALL + LEVEL_ROW)), (whole, level)):
            base = ref.shape[0] - SMALL
            ref[base : base + SMALL, :] = jnp.zeros((SMALL, blocks), BF16)
            put_split(ref, base + LEVEL_ROW, value)


def final_kernel(
    first, mid_mine, mid, last, whole, level_mine, level_far, out, weights, small, sems
):
    x = lax.axis_index("loop") % 2
    c = lax.axis_index("inner") % 2
    blocks = out.shape[-1]
    plans = {
        (0, 0): [(first, 0, 1), (mid, 1, 2), (last, 3, 1), (level_mine, 0, 0)],
        (0, 1): [(first, 0, 1), (mid_mine, 1, 2), (last, 3, 1), (level_far, 0, 0)],
        (1, 0): [(whole, 0, 4), (whole, 0, 0)],
        (1, 1): [(whole, 0, 4), (whole, 0, 0)],
    }
    for (role, core), plan in plans.items():

        @pl.when(jnp.logical_and(x == role, c == core))
        def _(plan=plan):
            copies = []
            for n, (source, to, count) in enumerate(plan):
                if count:
                    rows, goal = pl.ds(0, count * blocks), out.at[pl.ds(to * blocks, count * blocks)]
                else:
                    rows, goal = pl.ds(source.shape[0] - SMALL, SMALL), small
                copies.append(pltpu.make_async_copy(source.at[rows], goal, sems.at[n]))
            for copy in copies:
                copy.start()
            for copy in copies:
                copy.wait()

    weights[...] = get_split(small, LEVEL_ROW)


def scratch(blocks):
    return [
        pltpu.VMEM((10 * blocks, blocks), BF16),
        pltpu.VMEM((10 * blocks, blocks), BF16),
        pltpu.VMEM((5 * SMALL, blocks), BF16),
        pltpu.VMEM((10 * blocks, blocks), BF16),
        pltpu.VMEM((SLOT_COUNT * blocks, blocks), BF16),
        pltpu.VMEM((4 * blocks, 4 * blocks), BF16),
        pltpu.VMEM((3 * blocks, 4 * blocks), BF16),
        pltpu.VMEM((blocks, 2 * blocks), F32),
        pltpu.VMEM((16, 128), F32),
        pltpu.SMEM((16, 128), F32),
        pltpu.SemaphoreType.DMA((22,)),
        pltpu.SemaphoreType.DMA,
        pltpu.VMEM((4 * blocks, blocks), BF16),
        pltpu.VMEM((4 * blocks, blocks), BF16),
    ]


def vmem():
    return pl.BlockSpec(memory_space=pltpu.VMEM)


def hbm():
    return pl.BlockSpec(memory_space=pltpu.HBM)


def params():
    return pltpu.CompilerParams(vmem_limit_bytes=VMEM_BYTES)


def per_device(loops, inners, site_blocks, bond_weights, bond_gates, kept_slots):
    blocks = site_blocks.shape[-1]

    def rows(count, small=0):
        return jax.ShapeDtypeStruct((count * blocks + small, blocks), BF16)

    def send(value, where):
        route = []
        for l in range(loops):
            for i in range(inners):
                source = where(l, i)
                if source is not None:
                    sl, si = source
                    route.append(((sl % loops) * inners + si % inners, l * inners + i))
        return lax.ppermute(value, AXES, route)

    def to_first(where):
        return lambda l, i: where(l, i // 2) if i % 2 == l % 2 else None

    def to_second(where):
        return lambda l, i: where(l, i // 2) if i % 2 != l % 2 else None

    full, three_a, three_b = pl.pallas_call(
        prepare,
        out_shape=(rows(4, SMALL), rows(3, SMALL), rows(3, SMALL)),
        in_specs=[hbm()] + [vmem()] * 3,
        out_specs=(hbm(),) * 3,
        scratch_shapes=[
            pltpu.VMEM((4 * blocks, blocks), BF16),
            pltpu.VMEM((SMALL, blocks), BF16),
            pltpu.SemaphoreType.DMA((7,)),
        ],
        compiler_params=params(),
        name="prepare",
    )(site_blocks.reshape(4 * blocks, blocks), bond_weights[0], bond_gates[0], kept_slots)

    def pick(even, odd):
        return to_first(lambda l, k: (even if l % 2 == 0 else odd)(l, k))

    edge = send(
        three_a, pick(lambda l, k: (l, 2 * k - 1), lambda l, k: (l, 2 * k + 3))
    )
    cross = send(
        three_b, pick(lambda l, k: (l + 1, 2 * k + 2), lambda l, k: (l - 1, 2 * k + 2))
    )
    mirror_odd = send(full, to_first(lambda l, k: (l ^ 1, 2 * k + 1)))
    mirror_even = send(three_a, to_first(lambda l, k: (l ^ 1, 2 * k)))
    beside = send(full, pick(lambda l, k: (l, 2 * k + 1), lambda l, k: (l, 2 * k + 2)))

    iso_msg, iso_three, left_msg, left_three, local = pl.pallas_call(
        first_kernel,
        out_shape=(rows(4, SMALL), rows(3, SMALL), rows(4), rows(3), rows(6, 3 * SMALL)),
        in_specs=[hbm()] * 6,
        out_specs=(hbm(),) * 5,
        scratch_shapes=scratch(blocks) + [pltpu.VMEM((SMALL, blocks), BF16)],
        compiler_params=params(),
        name="first_bond",
    )(full, edge, cross, mirror_odd, mirror_even, beside)

    def worker(l, k, d, s):
        sector = 2 * k + l % 2 + s
        return (l - l % 2 + 2 * d + sector % 2, sector // 2 * 2 + sector % 2)

    local_r = send(local, to_second(lambda l, k: worker(l, k, 0, 0)))
    iso_1 = send(iso_msg, to_second(lambda l, k: worker(l, k, 0, -1)))
    iso_2 = send(iso_three, to_second(lambda l, k: worker(l, k, 0, -2)))
    left_1 = send(left_msg, to_second(lambda l, k: worker(l, k, 1, 1)))
    left_2 = send(left_three, to_second(lambda l, k: worker(l, k, 1, 2)))
    if loops == 2:
        left_0 = local_r
    else:
        left_0 = send(left_msg[: 3 * blocks], to_second(lambda l, k: worker(l, k, 1, 0)))

    mid, last, first, whole = pl.pallas_call(
        second_kernel,
        out_shape=(rows(2), rows(1), rows(1, SMALL), rows(4, SMALL)),
        in_specs=[hbm()] * 6,
        out_specs=(vmem(),) * 4,
        scratch_shapes=scratch(blocks),
        compiler_params=params(),
        name="second_bond",
    )(local_r, iso_1, iso_2, left_0, left_1, left_2)

    def from_second(l, i, d, s):
        sector = i - s
        return (l - l % 2 - 2 * d + sector % 2, sector // 2 * 2 + 1 - sector % 2)

    def right_from(s, cores):
        return lambda l, i: from_second(l, i, 1, s) if l % 2 == 0 and i % 2 in cores else None

    first_r = send(first, right_from(0, (0, 1)))
    mid_r = send(mid, right_from(1, (0,) if loops == 2 else (0, 1)))
    last_r = send(last, right_from(2, (0, 1)))
    whole_r = send(whole, lambda l, i: from_second(l, i, 0, 0) if l % 2 else None)
    if loops == 2:
        mid_mine, level_far = mid, first_r
    else:
        mid_mine = mid_r
        level_far = send(
            iso_msg[4 * blocks :], lambda l, i: (l + 1, i) if l % 2 == 0 and i % 2 else None
        )
    sites, weights = pl.pallas_call(
        final_kernel,
        out_shape=(rows(4), jax.ShapeDtypeStruct((1, blocks), F32)),
        in_specs=[hbm()] * 7,
        out_specs=(vmem(),) * 2,
        scratch_shapes=[pltpu.VMEM((SMALL, blocks), BF16), pltpu.SemaphoreType.DMA((4,))],
        compiler_params=params(),
        name="assemble",
    )(first_r, mid_mine, mid_r, last_r, whole_r, iso_msg, level_far)
    return sites.reshape(1, 1, 4, blocks, blocks), weights[None]


def solution(mesh):
    return jax.shard_map(
        functools.partial(per_device, mesh.shape["loop"], mesh.shape["inner"]),
        mesh=mesh,
        in_specs=(
            P("loop", "inner", None, None, None),
            P("loop", "inner", None),
            P("loop", None, None),
            P("loop", "inner"),
        ),
        out_specs=(P("loop", "inner", None, None, None), P("loop", "inner", None)),
        check_vma=False,
    )
```

```python
import functools
import math

import jax
import jax.numpy as jnp
import numpy as np
from jax import lax
from jax.experimental import pallas as pl
from jax.experimental.pallas import tpu as pltpu
from jax.sharding import PartitionSpec as P

CHARGE = (0, 1, 1, 2)
AXES = ("loop", "inner")
BF16, F32 = jnp.bfloat16, jnp.float32
VMEM_BYTES = 24 << 20
HIGHEST = lax.Precision.HIGHEST


def gate_terms():
    table = {}
    for a in range(4):
        for b in range(4):
            table[a, b] = [
                (CHARGE[p] - CHARGE[a], p, q)
                for p in range(4)
                for q in range(4)
                if CHARGE[p] + CHARGE[q] == CHARGE[a] + CHARGE[b]
                and abs(CHARGE[p] - CHARGE[a]) <= 1
            ]
    return table


TERMS = gate_terms()
PIECES = {
    (0, 0): (0, 3, 4, 0),
    (0, 1): (4, 3, 4, 0),
    (0, 2): (5, 3, 4, 0),
    (0, 3): (9, 3, 4, 0),
    (-1, 1): (1, 0, 3, 0),
    (-1, 2): (2, 0, 3, 0),
    (-1, 3): (6, 0, 3, 0),
    (1, 0): (3, 7, 3, 1),
    (1, 1): (7, 7, 3, 1),
    (1, 2): (8, 7, 3, 1),
}


def theta_slots():
    slots, count = {}, 0
    for (distance, q), (_, _, rows, first) in PIECES.items():
        for p in range(rows):
            slots[distance, first + p, q] = count
            count += 1
    return slots, count


SLOTS, SLOT_COUNT = theta_slots()


def dot(a, b, dims, precision=None):
    return lax.dot_general(a, b, (dims, ((), ())), precision=precision, preferred_element_type=F32)


def split3(a):
    h = a.astype(BF16)
    r = a - h.astype(F32)
    m = r.astype(BF16)
    return h, m, (r - m.astype(F32)).astype(BF16)


def factor_rows(work, size, panel=32):
    tiles = panel // 8
    sub = lax.broadcasted_iota(jnp.int32, (8, 128), 0)
    for start in range(0, size, panel):
        low = start < size // 2
        chunks = [0, 1, 2] if low else [1, 2, 3]
        base = start % 128
        rows = [
            [work[start + 8 * t : start + 8 * t + 8, 128 * c : 128 * c + 128] for c in chunks]
            for t in range(tiles)
        ]

        def column(k):
            return {
                t: jnp.broadcast_to(rows[t][0][:, base + k : base + k + 1], (8, 128))
                for t in range(k // 8, tiles)
            }

        def at(col, k):
            return jnp.broadcast_to(col[k // 8][k % 8 : k % 8 + 1, :], (8, 128))

        pivots = [jnp.ones((8, 128), F32) for _ in range(tiles)]
        cols = {k: column(k) for k in range(8)}
        for g in range(tiles):
            if g + 1 < tiles:
                cols.update({k: column(k) for k in range(8 * g + 8, 8 * g + 16)})

            def below(col, j):
                return {
                    t: (jnp.where(sub > j % 8, v, 0.0) if t == j // 8 else v)
                    for t, v in col.items()
                    if t >= g
                }

            for j in range(8 * g, 8 * g + 8, 2):
                one, two = cols[j], cols[j + 1]
                a, b, c = at(one, j), at(one, j + 1), at(two, j + 1)
                det = a * c - b * b
                ra, rd = 1.0 / a, 1.0 / det
                first = {t: v * ra for t, v in below(one, j).items()}
                ratio = b * ra
                two = {t: two[t] - one[t] * ratio for t in one if t >= g}
                second = {t: v * (a * rd) for t, v in below(two, j + 1).items()}
                for k in cols:
                    if k > j + 1:
                        e1, e2 = at(one, k), at(two, k)
                        cols[k] = {
                            t: v - (first[t] * e1 + second[t] * e2) for t, v in cols[k].items()
                        }
                for i in range(len(chunks)):
                    r = j % 8
                    x0 = jnp.broadcast_to(rows[g][i][r : r + 1, :], (8, 128))
                    x1 = jnp.broadcast_to(rows[g][i][r + 1 : r + 2, :], (8, 128)) - ratio * x0
                    for t in range(g, tiles):
                        rows[t][i] = rows[t][i] - (first[t] * x0 + second[t] * x1)
                pivots[g] = jnp.where(
                    sub == j % 8, a, jnp.where(sub == j % 8 + 1, det * ra, pivots[g])
                )
        done = []
        for t in range(tiles):
            scale = lax.rsqrt(pivots[t])
            done.append([x * scale for x in rows[t]])
            for c, x in zip(chunks, done[t]):
                work[start + 8 * t : start + 8 * t + 8, 128 * c : 128 * c + 128] = x
        after = start + panel
        if after < size:
            h, m, l = split3(
                jnp.concatenate([jnp.concatenate(xs, axis=1) for xs in done], axis=0)
            )
            right = jnp.concatenate([h, m, h, l, h, m], axis=0)
            left = jnp.concatenate([h, h, m, h, l, m], axis=0)
            first = 128 * chunks[0]
            for lo, hi in ((after, after + panel), (after + panel, size)):
                if lo < hi:
                    update = dot(left[:, lo - first : hi - first], right, ((0,), (0,)))
                    for i, c in enumerate(chunks):
                        work[lo:hi, 128 * c : 128 * c + 128] -= update[:, 128 * i : 128 * i + 128]


SMALL = 32
W_ROW, K_ROW = 16, 19
LEVEL_ROW = 3


def put_split(ref, at, row):
    for n, part in enumerate(split3(row)):
        ref[at + n : at + n + 1, :] = part


def get_split(ref, at):
    h, m, l = (ref[at + n : at + n + 1, :].astype(F32) for n in range(3))
    return (h + m) + l


def prepare(block_ref, weight_ref, gate_ref, kept_ref, full, head, tail, small, sems):
    blocks = block_ref.shape[-1]
    values = jnp.zeros((SMALL, blocks), F32)
    rowid = lax.broadcasted_iota(jnp.int32, (SMALL, blocks), 0)
    for n, part in enumerate(split3(weight_ref[...])):
        values = jnp.where(rowid == W_ROW + n, part.astype(F32), values)
    small[...] = jnp.where(rowid == K_ROW, kept_ref[...].astype(F32), values).astype(BF16)
    small[0:16, 0:16] = gate_ref[...].astype(BF16)
    copies = []
    for n, (ref, at) in enumerate(((full, 0), (tail, blocks), (head, 0))):
        size = ref.shape[0] - SMALL
        copies.append(
            pltpu.make_async_copy(
                block_ref.at[pl.ds(at, size)], ref.at[pl.ds(0, size)], sems.at[n]
            )
        )
        copies.append(
            pltpu.make_async_copy(small, ref.at[pl.ds(size, SMALL)], sems.at[3 + n])
        )
    for copy in copies:
        copy.start()
    for copy in copies:
        copy.wait()


def bond_body(
    a_ref, b_ref, below, here, above, kept, gate_rows, scaled, theta, matrix, proj, work, iso, left,
    gate_stage, gates, sem, right_ready, iso_ready
):
    blocks = b_ref.shape[-1]
    gate_stage[...] = gate_rows.astype(F32)
    copy = pltpu.make_async_copy(gate_stage, gates, sem)
    copy.start()
    for first, count, w in ((3, 4, here), (0, 3, below), (7, 3, above)):
        rows = slice(first * blocks, (first + count) * blocks)
        scaled[rows, :] = (a_ref[rows, :].astype(F32) * w).astype(BF16)
    basis = a_ref[3 * blocks : 7 * blocks, :].T
    right_ready()
    for (distance, q), (right, first_row, count, first) in PIECES.items():
        product = dot(
            scaled[first_row * blocks : (first_row + count) * blocks, :],
            b_ref[right * blocks : (right + 1) * blocks, :],
            ((1,), (0,)),
        )
        slot = SLOTS[distance, first, q]
        theta[slot * blocks : (slot + count) * blocks, :] = (
            product * (1.0 / math.sqrt(blocks))
        ).astype(BF16)
    copy.wait()

    def gate(a, b, p, q):
        return gates[4 * a + b, 4 * p + q]

    step = 16

    @pl.loop(0, blocks // step)
    def mix(chunk):
        at = pl.multiple_of(chunk * step, step)
        for half in range(blocks // 128):
            cut = slice(128 * half, 128 * half + 128)
            held = {}

            def term(distance, p, q):
                slot = SLOTS[distance, p, q]
                if slot not in held:
                    place = pl.ds(pl.multiple_of(slot * blocks + at, step), step)
                    held[slot] = theta[place, cut].astype(F32)
                return held[slot]

            for total in range(5):
                for a in range(4):
                    for b in range(4):
                        if CHARGE[a] + CHARGE[b] != total:
                            continue
                        value = None
                        for distance, p, q in TERMS[a, b]:
                            part = gate(a, b, p, q) * term(distance, p, q)
                            value = part if value is None else value + part
                        matrix[
                            pl.ds(pl.multiple_of(a * blocks + at, step), step),
                            b * blocks + 128 * half : b * blocks + 128 * half + 128,
                        ] = value.astype(BF16)
                held.clear()

    projected = dot(basis, matrix[...], ((1,), (0,)))
    slot_id = lax.broadcasted_iota(jnp.int32, projected.shape, 0).astype(F32)
    h, m, l = split3(jnp.where(slot_id < kept, projected, 0.0))
    for n, part in enumerate((h, m, l)):
        proj[n * blocks : (n + 1) * blocks, :] = part
    ri = lax.broadcasted_iota(jnp.int32, (blocks, blocks), 0)
    ci = lax.broadcasted_iota(jnp.int32, (blocks, blocks), 1)
    eye = jnp.where(ri == ci, 1.0, 0.0).astype(F32)
    outer = ((1,), (1,))
    mixed = dot(h, m, outer) + dot(h, l, outer)
    work[:, :blocks] = (dot(h, h, outer) + dot(m, m, outer)) + (mixed + mixed.T) + eye
    work[:, blocks:] = eye
    factor_rows(work, blocks)
    wh, wm, wl = split3(work[:, blocks:])
    h, m, l = (proj[n * blocks : (n + 1) * blocks, :] for n in range(3))
    inner = ((1,), (0,))
    ortho = (
        dot(jnp.concatenate([wh, wm, wl], axis=1), jnp.concatenate([h, h, h], axis=0), inner)
        + dot(jnp.concatenate([wh, wm], axis=1), jnp.concatenate([m, m], axis=0), inner)
        + dot(wh, l, inner)
    )
    ortho = (ortho * math.sqrt(4 * blocks)).astype(BF16)
    for p in range(4):
        iso[p * blocks : (p + 1) * blocks, :] = ortho[:, p * blocks : (p + 1) * blocks]
    iso_ready()
    carried = dot(matrix[...], ortho, outer) * (1.0 / math.sqrt(4 * blocks))
    level = jnp.sqrt(jnp.mean(carried * carried, axis=0, keepdims=True) + 1e-06)
    left[...] = (carried * (1.0 / level)).astype(BF16)
    return level


def first_kernel(
    own, here_full, next_full, next_tail, after_tail, here_head,
    iso_msg, iso_three, left_msg, left_three, local,
    a_ref, b_ref, small, scaled, theta, matrix, proj, work, gate_stage, gates, sems, sem,
    iso, left, pack,
):
    x = lax.axis_index("loop") % 2
    c = lax.axis_index("inner") % 2
    blocks = a_ref.shape[-1]
    plans = {
        0: [
            (a_ref, 0, own, 0, 3), (a_ref, 3, here_full, 0, 4), (a_ref, 7, next_tail, 0, 3),
            (b_ref, 0, here_head, 0, 3), (b_ref, 3, next_full, 0, 4), (b_ref, 7, after_tail, 0, 3),
        ],
        1: [
            (a_ref, 0, next_full, 0, 3), (a_ref, 3, here_full, 0, 4), (a_ref, 7, after_tail, 0, 3),
            (b_ref, 0, here_head, 0, 3), (b_ref, 3, own, 0, 4), (b_ref, 7, next_tail, 0, 3),
        ],
    }
    smalls = {
        0: [here_head, next_full, own, here_full, next_tail],
        1: [here_head, own, next_full, here_full, after_tail],
    }

    def move(source, at, target, to, rows, n):
        return pltpu.make_async_copy(
            source.at[pl.ds(at, rows)], target.at[pl.ds(to, rows)], sems.at[n]
        )

    @pl.when(x == c)
    def _():
        for role in (0, 1):

            @pl.when(x == role)
            def _(role=role):
                for n, (target, to, source, at, count) in enumerate(plans[role]):
                    move(source, at * blocks, target, to * blocks, count * blocks, n).start()
                for n, source in enumerate(smalls[role]):
                    move(source, source.shape[0] - SMALL, small, n * SMALL, SMALL, 6 + n).start()

        def arrived(chosen):
            for n, (target, to, _, _, count) in enumerate(plans[0]):
                if target is chosen:
                    move(own, 0, target, to * blocks, count * blocks, n).wait()

        copies = []

        def out(source, at, target, to, count, rest=0):
            rows = count * blocks + rest
            copies.append(move(source, at * blocks, target, to * blocks, rows, 11 + len(copies)))
            copies[-1].start()

        def iso_ready():
            out(iso, 0, iso_msg, 0, 4)
            out(iso, 1, iso_three, 0, 3)
            out(iso, 0, local, 0, 3)

        for n in range(5):
            move(own, 0, small, n * SMALL, SMALL, 6 + n).wait()
        out(small, 0, local, 6, 0, 2 * SMALL)
        below, here, above = (get_split(small, (2 + n) * SMALL + W_ROW) for n in range(3))
        kept = small[3 * SMALL + K_ROW : 3 * SMALL + K_ROW + 1, 0:1].astype(F32)
        arrived(a_ref)
        level = bond_body(
            a_ref, b_ref, below, here, above, kept, small[3 * SMALL : 3 * SMALL + 16, 0:128],
            scaled, theta, matrix, proj, work, iso, left, gate_stage, gates, sem,
            lambda: arrived(b_ref), iso_ready,
        )
        out(left, 0, left_msg, 0, 4)
        out(left, 1, left_three, 0, 3)
        out(left, 0, local, 3, 3)
        pack[...] = jnp.zeros((SMALL, blocks), BF16)
        put_split(pack, 0, get_split(small, W_ROW))
        put_split(pack, LEVEL_ROW, level)
        for ref in (iso_msg, iso_three, local):
            base = ref.shape[0] - SMALL
            copies.append(move(pack, 0, ref, base, SMALL, 11 + len(copies)))
            copies[-1].start()
        for copy in copies:
            copy.wait()


def as_column(row):
    return jnp.broadcast_to(row, (row.shape[1], row.shape[1])).T


def second_kernel(
    local, iso_1, iso_2, left_0, left_1, left_2,
    mid, last, first, whole,
    a_ref, b_ref, small, scaled, theta, matrix, proj, work, gate_stage, gates, sems, sem,
    iso, left,
):
    x = lax.axis_index("loop") % 2
    c = lax.axis_index("inner") % 2
    blocks = a_ref.shape[-1]
    moves = [
        (source, at * blocks, target, to * blocks, count * blocks)
        for source, at, target, to, count in (
            (iso_1, 0, a_ref, 0, 1), (iso_2, 0, a_ref, 1, 2), (local, 0, a_ref, 3, 1),
            (iso_1, 1, a_ref, 4, 2), (iso_2, 2, a_ref, 6, 1), (local, 1, a_ref, 7, 2),
            (iso_1, 3, a_ref, 9, 1), (left_0, left_0.shape[0] // blocks - 3, b_ref, 0, 3),
            (left_1, 0, b_ref, 3, 4), (left_2, 0, b_ref, 7, 3),
        )
    ]
    moves.append((local, 6 * blocks, small, 0, 3 * SMALL))
    for n, source in enumerate((iso_1, iso_2)):
        moves.append((source, source.shape[0] - SMALL, small, (3 + n) * SMALL, SMALL))

    @pl.when(x != c)
    def _():
        copies = [
            pltpu.make_async_copy(
                source.at[pl.ds(at, rows)], target.at[pl.ds(to, rows)], sems.at[n]
            )
            for n, (source, at, target, to, rows) in enumerate(moves)
        ]
        for copy in copies:
            copy.start()

        def arrived(right):
            for copy, (_, _, target, _, _) in zip(copies, moves):
                if (target is b_ref) == right:
                    copy.wait()

        arrived(False)
        below = get_split(small, 3 * SMALL)
        here, above = (get_split(small, n * SMALL + W_ROW) for n in range(2))
        kept = small[K_ROW : K_ROW + 1, 0:1].astype(F32)
        level = bond_body(
            a_ref, b_ref, below, here, above, kept, small[0:16, 0:128],
            scaled, theta, matrix, proj, work, iso, left, gate_stage, gates, sem,
            lambda: arrived(True), lambda: None,
        )
        scales = [as_column(get_split(small, n * SMALL + LEVEL_ROW)) for n in range(2, 5)]
        column = as_column(level)
        for p in range(4):
            rows = slice(p * blocks, (p + 1) * blocks)
            whole[rows, :] = (left[rows, :].astype(F32) * scales[CHARGE[p]]).astype(BF16)
        for ref, lo, hi in ((first, 0, 1), (mid, 1, 3), (last, 3, 4)):
            for p in range(lo, hi):
                value = iso[p * blocks : (p + 1) * blocks, :].astype(F32) * column
                ref[(p - lo) * blocks : (p - lo + 1) * blocks, :] = value.astype(BF16)
        for ref, value in ((first, get_split(small, 2 * SMALL + LEVEL_ROW)), (whole, level)):
            base = ref.shape[0] - SMALL
            ref[base : base + SMALL, :] = jnp.zeros((SMALL, blocks), BF16)
            put_split(ref, base + LEVEL_ROW, value)


def final_kernel(
    first_mine, first, mid, last, whole_mine, whole, level_mine, level_far, out, weights, small, sems
):
    x = lax.axis_index("loop") % 2
    c = lax.axis_index("inner") % 2
    blocks = out.shape[-1]
    plans = {
        (0, 0): [(first, 0, 1), (mid, 1, 2), (last, 3, 1), (level_far, 0, 0)],
        (0, 1): [(first_mine, 0, 1), (mid, 1, 2), (last, 3, 1), (level_mine, 0, 0)],
        (1, 0): [(whole_mine, 0, 4), (whole_mine, 0, 0)],
        (1, 1): [(whole, 0, 4), (whole, 0, 0)],
    }
    for (role, core), plan in plans.items():

        @pl.when(jnp.logical_and(x == role, c == core))
        def _(plan=plan):
            copies = []
            for n, (source, to, count) in enumerate(plan):
                if count:
                    rows, goal = pl.ds(0, count * blocks), out.at[pl.ds(to * blocks, count * blocks)]
                else:
                    rows, goal = pl.ds(source.shape[0] - SMALL, SMALL), small
                copies.append(pltpu.make_async_copy(source.at[rows], goal, sems.at[n]))
            for copy in copies:
                copy.start()
            for copy in copies:
                copy.wait()

    weights[...] = get_split(small, LEVEL_ROW)


def scratch(blocks):
    return [
        pltpu.VMEM((10 * blocks, blocks), BF16),
        pltpu.VMEM((10 * blocks, blocks), BF16),
        pltpu.VMEM((5 * SMALL, blocks), BF16),
        pltpu.VMEM((10 * blocks, blocks), BF16),
        pltpu.VMEM((SLOT_COUNT * blocks, blocks), BF16),
        pltpu.VMEM((4 * blocks, 4 * blocks), BF16),
        pltpu.VMEM((3 * blocks, 4 * blocks), BF16),
        pltpu.VMEM((blocks, 2 * blocks), F32),
        pltpu.VMEM((16, 128), F32),
        pltpu.SMEM((16, 128), F32),
        pltpu.SemaphoreType.DMA((22,)),
        pltpu.SemaphoreType.DMA,
        pltpu.VMEM((4 * blocks, blocks), BF16),
        pltpu.VMEM((4 * blocks, blocks), BF16),
    ]


def vmem():
    return pl.BlockSpec(memory_space=pltpu.VMEM)


def hbm():
    return pl.BlockSpec(memory_space=pl.ANY)


def params():
    return pltpu.CompilerParams(vmem_limit_bytes=VMEM_BYTES)


def per_device(loops, inners, site_blocks, bond_weights, bond_gates, kept_slots):
    blocks = site_blocks.shape[-1]

    def rows(count, small=0):
        return jax.ShapeDtypeStruct((count * blocks + small, blocks), BF16)

    def send(value, where):
        route = []
        for l in range(loops):
            for i in range(inners):
                source = where(l, i)
                if source is not None:
                    sl, si = source
                    route.append(((sl % loops) * inners + si % inners, l * inners + i))
        return lax.ppermute(value, AXES, route)

    def to_first(even, odd):
        return lambda l, i: (even, odd)[l % 2](l, i // 2) if i % 2 == l % 2 else None

    def to_second(where):
        return lambda l, i: where(l, i // 2) if i % 2 != l % 2 else None

    full, head, tail = pl.pallas_call(
        prepare,
        out_shape=(rows(4, SMALL), rows(3, SMALL), rows(3, SMALL)),
        in_specs=[vmem()] * 4,
        out_specs=(hbm(),) * 3,
        scratch_shapes=[pltpu.VMEM((SMALL, blocks), BF16), pltpu.SemaphoreType.DMA((6,))],
        compiler_params=params(),
        name="prepare",
    )(site_blocks.reshape(4 * blocks, blocks), bond_weights[0], bond_gates[0], kept_slots)

    next_full = send(
        full, to_first(lambda l, k: (l + 1, 2 * k + 2), lambda l, k: (l - 1, 2 * k - 1))
    )
    here_full = send(full, to_first(lambda l, k: (l, 2 * k + 1), lambda l, k: (l - 1, 2 * k)))
    next_tail = send(tail, to_first(lambda l, k: (l, 2 * k + 2), lambda l, k: (l, 2 * k + 2)))
    after_tail = send(
        tail, to_first(lambda l, k: (l + 1, 2 * k + 3), lambda l, k: (l - 1, 2 * k + 1))
    )
    here_head = send(head, to_first(lambda l, k: (l + 1, 2 * k + 1), lambda l, k: (l, 2 * k)))

    iso_msg, iso_three, left_msg, left_three, local = pl.pallas_call(
        first_kernel,
        out_shape=(rows(4, SMALL), rows(3, SMALL), rows(4), rows(3), rows(6, 3 * SMALL)),
        in_specs=[hbm()] * 6,
        out_specs=(hbm(),) * 5,
        scratch_shapes=scratch(blocks) + [pltpu.VMEM((SMALL, blocks), BF16)],
        compiler_params=params(),
        name="first_bond",
    )(full, here_full, next_full, next_tail, after_tail, here_head)

    def worker(l, k, d, s):
        sector = 2 * k + 1 - l % 2 + s
        site = 1 - sector % 2
        return (l - l % 2 + 2 * d + site, sector // 2 * 2 + site)

    local_r = send(local, to_second(lambda l, k: worker(l, k, 0, 0)))
    iso_1 = send(iso_msg, to_second(lambda l, k: worker(l, k, 0, -1)))
    iso_2 = send(iso_three, to_second(lambda l, k: worker(l, k, 0, -2)))
    left_1 = send(left_msg, to_second(lambda l, k: worker(l, k, 1, 1)))
    left_2 = send(left_three, to_second(lambda l, k: worker(l, k, 1, 2)))
    if loops == 2:
        left_0 = local_r
    else:
        left_0 = send(left_msg[: 3 * blocks], to_second(lambda l, k: worker(l, k, 1, 0)))

    mid, last, first, whole = pl.pallas_call(
        second_kernel,
        out_shape=(rows(2), rows(1), rows(1, SMALL), rows(4, SMALL)),
        in_specs=[hbm()] * 6,
        out_specs=(vmem(),) * 4,
        scratch_shapes=scratch(blocks),
        compiler_params=params(),
        name="second_bond",
    )(local_r, iso_1, iso_2, left_0, left_1, left_2)

    def from_second(l, i, d, s):
        sector = i - s
        site = 1 - sector % 2
        return (l - l % 2 - 2 * d + site, sector // 2 * 2 + 1 - site)

    def right_from(s, cores):
        return lambda l, i: from_second(l, i, 1, s) if l % 2 == 0 and i % 2 in cores else None

    first_r = send(first, right_from(0, (0,) if loops == 2 else (0, 1)))
    mid_r = send(mid, right_from(1, (0, 1)))
    last_r = send(last, right_from(2, (0, 1)))
    whole_r = send(whole, lambda l, i: from_second(l, i, 0, 0) if l % 2 and i % 2 else None)
    if loops == 2:
        first_mine, level_far = first, first_r
    else:
        first_mine = first_r
        level_far = send(
            iso_msg[4 * blocks :], lambda l, i: (l + 1, i + 1) if l % 2 == 0 and i % 2 == 0 else None
        )
    sites, weights = pl.pallas_call(
        final_kernel,
        out_shape=(rows(4), jax.ShapeDtypeStruct((1, blocks), F32)),
        in_specs=[hbm()] * 8,
        out_specs=(vmem(),) * 2,
        scratch_shapes=[pltpu.VMEM((SMALL, blocks), BF16), pltpu.SemaphoreType.DMA((4,))],
        compiler_params=params(),
        name="assemble",
    )(first_mine, first_r, mid_r, last_r, whole, whole_r, local_r, level_far)
    return sites.reshape(1, 1, 4, blocks, blocks), weights[None]


def solution(mesh):
    return jax.shard_map(
        functools.partial(per_device, mesh.shape["loop"], mesh.shape["inner"]),
        mesh=mesh,
        in_specs=(
            P("loop", "inner", None, None, None),
            P("loop", "inner", None),
            P("loop", None, None),
            P("loop", "inner"),
        ),
        out_specs=(P("loop", "inner", None, None, None), P("loop", "inner", None)),
        check_vma=False,
    )
```

```python
import functools
import math

import jax
import jax.numpy as jnp
import numpy as np
from jax import lax
from jax.experimental import pallas as pl
from jax.experimental.pallas import tpu as pltpu
from jax.sharding import PartitionSpec as P

CHARGE = (0, 1, 1, 2)
AXES = ("loop", "inner")
BF16, F32 = jnp.bfloat16, jnp.float32
VMEM_BYTES = 24 << 20
HIGHEST = lax.Precision.HIGHEST


def gate_terms():
    table = {}
    for a in range(4):
        for b in range(4):
            table[a, b] = [
                (CHARGE[p] - CHARGE[a], p, q)
                for p in range(4)
                for q in range(4)
                if CHARGE[p] + CHARGE[q] == CHARGE[a] + CHARGE[b]
                and abs(CHARGE[p] - CHARGE[a]) <= 1
            ]
    return table


TERMS = gate_terms()
PIECES = {
    (0, 0): (0, 3, 4, 0),
    (0, 1): (4, 3, 4, 0),
    (0, 2): (5, 3, 4, 0),
    (0, 3): (9, 3, 4, 0),
    (-1, 1): (1, 0, 3, 0),
    (-1, 2): (2, 0, 3, 0),
    (-1, 3): (6, 0, 3, 0),
    (1, 0): (3, 7, 3, 1),
    (1, 1): (7, 7, 3, 1),
    (1, 2): (8, 7, 3, 1),
}


def theta_slots():
    slots, count = {}, 0
    for (distance, q), (_, _, rows, first) in PIECES.items():
        for p in range(rows):
            slots[distance, first + p, q] = count
            count += 1
    return slots, count


SLOTS, SLOT_COUNT = theta_slots()


def dot(a, b, dims, precision=None):
    return lax.dot_general(a, b, (dims, ((), ())), precision=precision, preferred_element_type=F32)


def split3(a):
    h = a.astype(BF16)
    r = a - h.astype(F32)
    m = r.astype(BF16)
    return h, m, (r - m.astype(F32)).astype(BF16)


def factor_rows(work, size, panel=32):
    tiles = panel // 8
    sub = lax.broadcasted_iota(jnp.int32, (8, 128), 0)
    for start in range(0, size, panel):
        low = start < size // 2
        chunks = [0, 1, 2] if low else [1, 2, 3]
        base = start % 128
        rows = [
            [work[start + 8 * t : start + 8 * t + 8, 128 * c : 128 * c + 128] for c in chunks]
            for t in range(tiles)
        ]

        def column(k):
            return {
                t: jnp.broadcast_to(rows[t][0][:, base + k : base + k + 1], (8, 128))
                for t in range(k // 8, tiles)
            }

        def at(col, k):
            return jnp.broadcast_to(col[k // 8][k % 8 : k % 8 + 1, :], (8, 128))

        pivots = [jnp.ones((8, 128), F32) for _ in range(tiles)]
        cols = {k: column(k) for k in range(8)}
        for g in range(tiles):
            if g + 1 < tiles:
                cols.update({k: column(k) for k in range(8 * g + 8, 8 * g + 16)})

            def below(col, j):
                return {
                    t: (jnp.where(sub > j % 8, v, 0.0) if t == j // 8 else v)
                    for t, v in col.items()
                    if t >= g
                }

            for j in range(8 * g, 8 * g + 8, 2):
                one, two = cols[j], cols[j + 1]
                a, b, c = at(one, j), at(one, j + 1), at(two, j + 1)
                det = a * c - b * b
                ra, rd = 1.0 / a, 1.0 / det
                first = {t: v * ra for t, v in below(one, j).items()}
                ratio = b * ra
                two = {t: two[t] - one[t] * ratio for t in one if t >= g}
                second = {t: v * (a * rd) for t, v in below(two, j + 1).items()}
                for k in cols:
                    if k > j + 1:
                        e1, e2 = at(one, k), at(two, k)
                        cols[k] = {
                            t: v - (first[t] * e1 + second[t] * e2) for t, v in cols[k].items()
                        }
                for i in range(len(chunks)):
                    r = j % 8
                    x0 = jnp.broadcast_to(rows[g][i][r : r + 1, :], (8, 128))
                    x1 = jnp.broadcast_to(rows[g][i][r + 1 : r + 2, :], (8, 128)) - ratio * x0
                    for t in range(g, tiles):
                        rows[t][i] = rows[t][i] - (first[t] * x0 + second[t] * x1)
                pivots[g] = jnp.where(
                    sub == j % 8, a, jnp.where(sub == j % 8 + 1, det * ra, pivots[g])
                )
        done = []
        for t in range(tiles):
            scale = lax.rsqrt(pivots[t])
            done.append([x * scale for x in rows[t]])
            for c, x in zip(chunks, done[t]):
                work[start + 8 * t : start + 8 * t + 8, 128 * c : 128 * c + 128] = x
        after = start + panel
        if after < size:
            h, m, l = split3(
                jnp.concatenate([jnp.concatenate(xs, axis=1) for xs in done], axis=0)
            )
            right = jnp.concatenate([h, m, h, l, h, m], axis=0)
            left = jnp.concatenate([h, h, m, h, l, m], axis=0)
            first = 128 * chunks[0]
            for lo, hi in ((after, after + panel), (after + panel, size)):
                if lo < hi:
                    update = dot(left[:, lo - first : hi - first], right, ((0,), (0,)))
                    for i, c in enumerate(chunks):
                        work[lo:hi, 128 * c : 128 * c + 128] -= update[:, 128 * i : 128 * i + 128]


SMALL = 32
W_ROW, K_ROW = 16, 19
LEVEL_ROW = 3


def put_split(ref, at, row):
    for n, part in enumerate(split3(row)):
        ref[at + n : at + n + 1, :] = part


def get_split(ref, at):
    h, m, l = (ref[at + n : at + n + 1, :].astype(F32) for n in range(3))
    return (h + m) + l


def prepare(block_ref, weight_ref, gate_ref, kept_ref, full, head, tail, small, sems):
    blocks = block_ref.shape[-1]
    values = jnp.zeros((SMALL, blocks), F32)
    rowid = lax.broadcasted_iota(jnp.int32, (SMALL, blocks), 0)
    for n, part in enumerate(split3(weight_ref[...])):
        values = jnp.where(rowid == W_ROW + n, part.astype(F32), values)
    small[...] = jnp.where(rowid == K_ROW, kept_ref[...].astype(F32), values).astype(BF16)
    small[0:16, 0:16] = gate_ref[...].astype(BF16)
    copies = []
    for n, (ref, at) in enumerate(((full, 0), (tail, blocks), (head, 0))):
        size = ref.shape[0] - SMALL
        copies.append(
            pltpu.make_async_copy(
                block_ref.at[pl.ds(at, size)], ref.at[pl.ds(0, size)], sems.at[n]
            )
        )
        copies.append(
            pltpu.make_async_copy(small, ref.at[pl.ds(size, SMALL)], sems.at[3 + n])
        )
    for copy in copies:
        copy.start()
    for copy in copies:
        copy.wait()


def products(a_blocks, b_blocks, weights, scaled, theta):
    blocks = scaled.shape[-1]

    def block(place):
        ref, n = place
        return ref[n * blocks : (n + 1) * blocks, :]

    for n, place in enumerate(a_blocks):
        w = weights[0 if n < 3 else 1 if n < 7 else 2]
        scaled[n * blocks : (n + 1) * blocks, :] = (block(place).astype(F32) * w).astype(BF16)
    for (distance, q), (right, first_row, count, first) in PIECES.items():
        product = dot(
            scaled[first_row * blocks : (first_row + count) * blocks, :],
            block(b_blocks[right]),
            ((1,), (0,)),
        )
        slot = SLOTS[distance, first, q]
        theta[slot * blocks : (slot + count) * blocks, :] = (
            product * (1.0 / math.sqrt(blocks))
        ).astype(BF16)


def load_gates(gate_rows, gate_stage, gates, sem):
    gate_stage[...] = gate_rows.astype(F32)
    copy = pltpu.make_async_copy(gate_stage, gates, sem)
    copy.start()
    return copy


def bond_body(basis, kept, theta, matrix, proj, work, iso, left, gates, iso_ready):
    blocks = theta.shape[-1]

    def gate(a, b, p, q):
        return gates[4 * a + b, 4 * p + q]

    step = 16

    @pl.loop(0, blocks // step)
    def mix(chunk):
        at = pl.multiple_of(chunk * step, step)
        for half in range(blocks // 128):
            cut = slice(128 * half, 128 * half + 128)
            held = {}

            def term(distance, p, q):
                slot = SLOTS[distance, p, q]
                if slot not in held:
                    place = pl.ds(pl.multiple_of(slot * blocks + at, step), step)
                    held[slot] = theta[place, cut].astype(F32)
                return held[slot]

            for total in range(5):
                for a in range(4):
                    for b in range(4):
                        if CHARGE[a] + CHARGE[b] != total:
                            continue
                        value = None
                        for distance, p, q in TERMS[a, b]:
                            part = gate(a, b, p, q) * term(distance, p, q)
                            value = part if value is None else value + part
                        matrix[
                            pl.ds(pl.multiple_of(a * blocks + at, step), step),
                            b * blocks + 128 * half : b * blocks + 128 * half + 128,
                        ] = value.astype(BF16)
                held.clear()

    projected = dot(basis, matrix[...], ((1,), (0,)))
    slot_id = lax.broadcasted_iota(jnp.int32, projected.shape, 0).astype(F32)
    h, m, l = split3(jnp.where(slot_id < kept, projected, 0.0))
    for n, part in enumerate((h, m, l)):
        proj[n * blocks : (n + 1) * blocks, :] = part
    ri = lax.broadcasted_iota(jnp.int32, (blocks, blocks), 0)
    ci = lax.broadcasted_iota(jnp.int32, (blocks, blocks), 1)
    eye = jnp.where(ri == ci, 1.0, 0.0).astype(F32)
    outer = ((1,), (1,))
    mixed = dot(h, m, outer) + dot(h, l, outer)
    work[:, :blocks] = (dot(h, h, outer) + dot(m, m, outer)) + (mixed + mixed.T) + eye
    work[:, blocks:] = eye
    factor_rows(work, blocks)
    wh, wm, wl = split3(work[:, blocks:])
    h, m, l = (proj[n * blocks : (n + 1) * blocks, :] for n in range(3))
    inner = ((1,), (0,))
    ortho = (
        dot(jnp.concatenate([wh, wm, wl], axis=1), jnp.concatenate([h, h, h], axis=0), inner)
        + dot(jnp.concatenate([wh, wm], axis=1), jnp.concatenate([m, m], axis=0), inner)
        + dot(wh, l, inner)
    )
    ortho = (ortho * math.sqrt(4 * blocks)).astype(BF16)
    for p in range(4):
        iso[p * blocks : (p + 1) * blocks, :] = ortho[:, p * blocks : (p + 1) * blocks]
    iso_ready()
    carried = dot(matrix[...], ortho, outer) * (1.0 / math.sqrt(4 * blocks))
    level = jnp.sqrt(jnp.mean(carried * carried, axis=0, keepdims=True) + 1e-06)
    left[...] = (carried * (1.0 / level)).astype(BF16)
    return level


def first_kernel(
    own, here_full, next_full, here_head, after_tail, next_tail,
    iso, iso_three, left, left_three, local,
    scaled, theta, matrix, proj, work, gate_stage, gates, sems,
):
    x = lax.axis_index("loop") % 2
    c = lax.axis_index("inner") % 2
    blocks = scaled.shape[-1]

    def small(ref):
        return ref.shape[0] - SMALL

    def span(ref, count):
        return [(ref, n) for n in range(count)]

    @pl.when(x == c)
    def _():
        base = small(here_full)
        kept = here_full[base + K_ROW : base + K_ROW + 1, 0:1].astype(F32)
        gates_copy = load_gates(here_full[base : base + 16, 0:128], gate_stage, gates, sems.at[0])
        rest = 6 * blocks
        for role, (one, two, three, four) in enumerate(
            ((own, next_full, next_tail, after_tail), (next_full, own, after_tail, next_tail))
        ):

            @pl.when(x == role)
            def _(one=one, two=two, three=three, four=four):
                products(
                    span(one, 3) + span(here_full, 4) + span(three, 3),
                    span(here_head, 3) + span(two, 4) + span(four, 3),
                    [get_split(ref, small(ref) + W_ROW) for ref in (one, here_full, three)],
                    scaled,
                    theta,
                )
                for n, ref in enumerate((here_head, two)):
                    local[rest + n * SMALL : rest + (n + 1) * SMALL, :] = ref[small(ref) :, :]

        basis = here_full[0 : 4 * blocks, :].T
        gates_copy.wait()
        copies = []

        def out(source, at, target, to, count):
            copies.append(
                pltpu.make_async_copy(
                    source.at[pl.ds(at * blocks, count * blocks)],
                    target.at[pl.ds(to * blocks, count * blocks)],
                    sems.at[1 + len(copies)],
                )
            )
            copies[-1].start()

        def iso_ready():
            out(iso, 1, iso_three, 0, 3)
            out(iso, 0, local, 0, 3)

        level = bond_body(basis, kept, theta, matrix, proj, work, iso, left, gates, iso_ready)
        out(left, 1, left_three, 0, 3)
        out(left, 0, local, 3, 3)
        weights = get_split(local, rest + W_ROW)
        for ref in (iso, iso_three, local):
            ref[small(ref) :, :] = jnp.zeros((SMALL, blocks), BF16)
            put_split(ref, small(ref), weights)
            put_split(ref, small(ref) + LEVEL_ROW, level)
        for copy in copies:
            copy.wait()


def as_column(row):
    return jnp.broadcast_to(row, (row.shape[1], row.shape[1])).T


def second_kernel(
    local, iso_1, iso_2, left_0, left_1, left_2,
    mid, last, first, whole,
    scaled, theta, matrix, proj, work, gate_stage, gates, sems, iso, left,
):
    x = lax.axis_index("loop") % 2
    c = lax.axis_index("inner") % 2
    blocks = scaled.shape[-1]
    rest = 6 * blocks
    near = left_0.shape[0] // blocks - 3

    def small(ref):
        return ref.shape[0] - SMALL

    @pl.when(x != c)
    def _():
        kept = local[rest + K_ROW : rest + K_ROW + 1, 0:1].astype(F32)
        gates_copy = load_gates(local[rest : rest + 16, 0:128], gate_stage, gates, sems.at[0])
        here = [(local, 0), (iso_1, 1), (iso_1, 2), (iso_2, 2)]
        products(
            [(iso_1, 0), (iso_2, 0), (iso_2, 1)] + here + [(local, 1), (local, 2), (iso_1, 3)],
            [(left_0, near + n) for n in range(3)]
            + [(left_1, n) for n in range(4)]
            + [(left_2, n) for n in range(3)],
            [
                get_split(iso_1, small(iso_1)),
                get_split(local, rest + W_ROW),
                get_split(local, rest + SMALL + W_ROW),
            ],
            scaled,
            theta,
        )
        basis = jnp.concatenate(
            [ref[n * blocks : (n + 1) * blocks, :] for ref, n in here], axis=0
        ).T
        gates_copy.wait()
        level = bond_body(
            basis, kept, theta, matrix, proj, work, iso, left, gates, lambda: None
        )
        levels = [get_split(ref, small(ref) + LEVEL_ROW) for ref in (local, iso_1, iso_2)]
        column = as_column(level)
        for ref, lo, hi in ((last, 3, 4), (mid, 1, 3), (first, 0, 1)):
            for p in range(lo, hi):
                value = iso[p * blocks : (p + 1) * blocks, :].astype(F32) * column
                ref[(p - lo) * blocks : (p - lo + 1) * blocks, :] = value.astype(BF16)
        scales = [as_column(value) for value in levels]
        for p in range(4):
            rows = slice(p * blocks, (p + 1) * blocks)
            whole[rows, :] = (left[rows, :].astype(F32) * scales[CHARGE[p]]).astype(BF16)
        for ref, value in ((first, levels[0]), (whole, level)):
            ref[small(ref) :, :] = jnp.zeros((SMALL, blocks), BF16)
            put_split(ref, small(ref) + LEVEL_ROW, value)


def place(plan, out, sems):
    blocks = out.shape[-1]
    copies = []
    for n, (source, to, count) in enumerate(plan):
        copies.append(
            pltpu.make_async_copy(
                source.at[pl.ds(0, count * blocks)],
                out.at[pl.ds(to * blocks, count * blocks)],
                sems.at[n],
            )
        )
    for copy in copies:
        copy.start()
    return copies


def assemble(
    first_mine, first, mid, last, whole_mine, whole, level_mine, level_far, out, weights, sems
):
    x = lax.axis_index("loop") % 2
    c = lax.axis_index("inner") % 2
    even = [(mid, 1, 2), (last, 3, 1)]
    for role, core, plan, level in (
        (0, 0, [(first, 0, 1)] + even, level_far),
        (0, 1, [(first_mine, 0, 1)] + even, level_mine),
        (1, 0, [(whole_mine, 0, 4)], whole_mine),
        (1, 1, [(whole, 0, 4)], whole),
    ):

        @pl.when(jnp.logical_and(x == role, c == core))
        def _(plan=plan, level=level):
            copies = place(plan, out, sems)
            weights[...] = get_split(level, level.shape[0] - SMALL + LEVEL_ROW)
            for copy in copies:
                copy.wait()


def scratch(blocks):
    return [
        pltpu.VMEM((10 * blocks, blocks), BF16),
        pltpu.VMEM((SLOT_COUNT * blocks, blocks), BF16),
        pltpu.VMEM((4 * blocks, 4 * blocks), BF16),
        pltpu.VMEM((3 * blocks, 4 * blocks), BF16),
        pltpu.VMEM((blocks, 2 * blocks), F32),
        pltpu.VMEM((16, 128), F32),
        pltpu.SMEM((16, 128), F32),
        pltpu.SemaphoreType.DMA((5,)),
    ]


def vmem():
    return pl.BlockSpec(memory_space=pltpu.VMEM)


def hbm():
    return pl.BlockSpec(memory_space=pl.ANY)


def params():
    return pltpu.CompilerParams(vmem_limit_bytes=VMEM_BYTES)


def per_device(loops, inners, site_blocks, bond_weights, bond_gates, kept_slots):
    blocks = site_blocks.shape[-1]

    def rows(count, small=0):
        return jax.ShapeDtypeStruct((count * blocks + small, blocks), BF16)

    def send(value, where):
        route = []
        for l in range(loops):
            for i in range(inners):
                source = where(l, i)
                if source is not None:
                    sl, si = source
                    route.append(((sl % loops) * inners + si % inners, l * inners + i))
        return lax.ppermute(value, AXES, route)

    def to_first(even, odd):
        return lambda l, i: (even, odd)[l % 2](l, i // 2) if i % 2 == l % 2 else None

    def to_second(where):
        return lambda l, i: where(l, i // 2) if i % 2 != l % 2 else None

    full, head, tail = pl.pallas_call(
        prepare,
        out_shape=(rows(4, SMALL), rows(3, SMALL), rows(3, SMALL)),
        in_specs=[vmem()] * 4,
        out_specs=(hbm(),) * 3,
        scratch_shapes=[pltpu.VMEM((SMALL, blocks), BF16), pltpu.SemaphoreType.DMA((6,))],
        compiler_params=params(),
        name="prepare",
    )(site_blocks.reshape(4 * blocks, blocks), bond_weights[0], bond_gates[0], kept_slots)

    next_full = send(
        full, to_first(lambda l, k: (l + 1, 2 * k + 2), lambda l, k: (l - 1, 2 * k - 1))
    )
    here_full = send(full, to_first(lambda l, k: (l, 2 * k + 1), lambda l, k: (l - 1, 2 * k)))
    next_tail = send(tail, to_first(lambda l, k: (l, 2 * k + 2), lambda l, k: (l, 2 * k + 2)))
    after_tail = send(
        tail, to_first(lambda l, k: (l + 1, 2 * k + 3), lambda l, k: (l - 1, 2 * k + 1))
    )
    here_head = send(head, to_first(lambda l, k: (l + 1, 2 * k + 1), lambda l, k: (l, 2 * k)))

    iso_msg, iso_three, left_msg, left_three, local = pl.pallas_call(
        first_kernel,
        out_shape=(rows(4, SMALL), rows(3, SMALL), rows(4), rows(3), rows(6, 3 * SMALL)),
        in_specs=[vmem()] * 6,
        out_specs=(vmem(),) * 5,
        scratch_shapes=scratch(blocks),
        compiler_params=params(),
        name="first_bond",
    )(full, here_full, next_full, here_head, after_tail, next_tail)

    def worker(l, k, d, s):
        sector = 2 * k + 1 - l % 2 + s
        site = 1 - sector % 2
        return (l - l % 2 + 2 * d + site, sector // 2 * 2 + site)

    local_r = send(local, to_second(lambda l, k: worker(l, k, 0, 0)))
    iso_1 = send(iso_msg, to_second(lambda l, k: worker(l, k, 0, -1)))
    iso_2 = send(iso_three, to_second(lambda l, k: worker(l, k, 0, -2)))
    left_1 = send(left_msg, to_second(lambda l, k: worker(l, k, 1, 1)))
    left_2 = send(left_three, to_second(lambda l, k: worker(l, k, 1, 2)))
    if loops == 2:
        left_0 = local_r
    else:
        left_0 = send(left_msg[: 3 * blocks], to_second(lambda l, k: worker(l, k, 1, 0)))

    mid, last, first, whole = pl.pallas_call(
        second_kernel,
        out_shape=(rows(2), rows(1), rows(1, SMALL), rows(4, SMALL)),
        in_specs=[vmem()] * 6,
        out_specs=(vmem(),) * 4,
        scratch_shapes=scratch(blocks) + [pltpu.VMEM((4 * blocks, blocks), BF16)] * 2,
        compiler_params=params(),
        name="second_bond",
    )(local_r, iso_1, iso_2, left_0, left_1, left_2)

    def from_second(l, i, d, s):
        sector = i - s
        site = 1 - sector % 2
        return (l - l % 2 - 2 * d + site, sector // 2 * 2 + 1 - site)

    def right_from(s, cores):
        return lambda l, i: from_second(l, i, 1, s) if l % 2 == 0 and i % 2 in cores else None

    first_r = send(first, right_from(0, (0,) if loops == 2 else (0, 1)))
    mid_r = send(mid, right_from(1, (0, 1)))
    last_r = send(last, right_from(2, (0, 1)))
    whole_r = send(whole, lambda l, i: from_second(l, i, 0, 0) if l % 2 and i % 2 else None)
    if loops == 2:
        first_mine, level_far = first, first_r
    else:
        first_mine = first_r
        level_far = send(
            iso_msg[4 * blocks :], lambda l, i: (l + 1, i + 1) if l % 2 == 0 and i % 2 == 0 else None
        )
    sites, weights = pl.pallas_call(
        assemble,
        out_shape=(rows(4), jax.ShapeDtypeStruct((1, blocks), F32)),
        in_specs=[vmem()] * 8,
        out_specs=(hbm(), vmem()),
        scratch_shapes=[pltpu.SemaphoreType.DMA((3,))],
        compiler_params=params(),
        name="assemble",
    )(first_mine, first_r, mid_r, last_r, whole, whole_r, local_r, level_far)
    return sites.reshape(1, 1, 4, blocks, blocks), weights[None]


def solution(mesh):
    return jax.shard_map(
        functools.partial(per_device, mesh.shape["loop"], mesh.shape["inner"]),
        mesh=mesh,
        in_specs=(
            P("loop", "inner", None, None, None),
            P("loop", "inner", None),
            P("loop", None, None),
            P("loop", "inner"),
        ),
        out_specs=(P("loop", "inner", None, None, None), P("loop", "inner", None)),
        check_vma=False,
    )
```

```python
import functools
import math

import jax
import jax.numpy as jnp
import numpy as np
from jax import lax
from jax.experimental import pallas as pl
from jax.experimental.pallas import tpu as pltpu
from jax.sharding import PartitionSpec as P

CHARGE = (0, 1, 1, 2)
AXES = ("loop", "inner")
BF16, F32 = jnp.bfloat16, jnp.float32
VMEM_BYTES = 24 << 20
HIGHEST = lax.Precision.HIGHEST


def gate_terms():
    table = {}
    for a in range(4):
        for b in range(4):
            table[a, b] = [
                (CHARGE[p] - CHARGE[a], p, q)
                for p in range(4)
                for q in range(4)
                if CHARGE[p] + CHARGE[q] == CHARGE[a] + CHARGE[b]
                and abs(CHARGE[p] - CHARGE[a]) <= 1
            ]
    return table


TERMS = gate_terms()
PIECES = {
    (0, 0): (0, 3, 4, 0),
    (0, 1): (4, 3, 4, 0),
    (0, 2): (5, 3, 4, 0),
    (0, 3): (9, 3, 4, 0),
    (-1, 1): (1, 0, 3, 0),
    (-1, 2): (2, 0, 3, 0),
    (-1, 3): (6, 0, 3, 0),
    (1, 0): (3, 7, 3, 1),
    (1, 1): (7, 7, 3, 1),
    (1, 2): (8, 7, 3, 1),
}


def theta_slots():
    slots, count = {}, 0
    for (distance, q), (_, _, rows, first) in PIECES.items():
        for p in range(rows):
            slots[distance, first + p, q] = count
            count += 1
    return slots, count


SLOTS, SLOT_COUNT = theta_slots()


def dot(a, b, dims, precision=None):
    return lax.dot_general(a, b, (dims, ((), ())), precision=precision, preferred_element_type=F32)


def split3(a):
    h = a.astype(BF16)
    r = a - h.astype(F32)
    m = r.astype(BF16)
    return h, m, (r - m.astype(F32)).astype(BF16)


def factor_rows(work, size, panel=32):
    tiles = panel // 8
    sub = lax.broadcasted_iota(jnp.int32, (8, 128), 0)
    for start in range(0, size, panel):
        low = start < size // 2
        chunks = [0, 1, 2] if low else [1, 2, 3]
        base = start % 128
        rows = [
            [work[start + 8 * t : start + 8 * t + 8, 128 * c : 128 * c + 128] for c in chunks]
            for t in range(tiles)
        ]

        def column(k):
            return {
                t: jnp.broadcast_to(rows[t][0][:, base + k : base + k + 1], (8, 128))
                for t in range(k // 8, tiles)
            }

        def at(col, k):
            return jnp.broadcast_to(col[k // 8][k % 8 : k % 8 + 1, :], (8, 128))

        pivots = [jnp.ones((8, 128), F32) for _ in range(tiles)]
        cols = {k: column(k) for k in range(8)}
        for g in range(tiles):
            if g + 1 < tiles:
                cols.update({k: column(k) for k in range(8 * g + 8, 8 * g + 16)})

            def below(col, j):
                return {
                    t: (jnp.where(sub > j % 8, v, 0.0) if t == j // 8 else v)
                    for t, v in col.items()
                    if t >= g
                }

            for j in range(8 * g, 8 * g + 8, 2):
                one, two = cols[j], cols[j + 1]
                a, b, c = at(one, j), at(one, j + 1), at(two, j + 1)
                det = a * c - b * b
                ra, rd = 1.0 / a, 1.0 / det
                first = {t: v * ra for t, v in below(one, j).items()}
                ratio = b * ra
                two = {t: two[t] - one[t] * ratio for t in one if t >= g}
                second = {t: v * (a * rd) for t, v in below(two, j + 1).items()}
                for k in cols:
                    if k > j + 1:
                        e1, e2 = at(one, k), at(two, k)
                        cols[k] = {
                            t: v - (first[t] * e1 + second[t] * e2) for t, v in cols[k].items()
                        }
                for i in range(len(chunks)):
                    r = j % 8
                    x0 = jnp.broadcast_to(rows[g][i][r : r + 1, :], (8, 128))
                    x1 = jnp.broadcast_to(rows[g][i][r + 1 : r + 2, :], (8, 128)) - ratio * x0
                    for t in range(g, tiles):
                        rows[t][i] = rows[t][i] - (first[t] * x0 + second[t] * x1)
                pivots[g] = jnp.where(
                    sub == j % 8, a, jnp.where(sub == j % 8 + 1, det * ra, pivots[g])
                )
        done = []
        for t in range(tiles):
            scale = lax.rsqrt(pivots[t])
            done.append([x * scale for x in rows[t]])
            for c, x in zip(chunks, done[t]):
                work[start + 8 * t : start + 8 * t + 8, 128 * c : 128 * c + 128] = x
        after = start + panel
        if after < size:
            h, m, l = split3(
                jnp.concatenate([jnp.concatenate(xs, axis=1) for xs in done], axis=0)
            )
            right = jnp.concatenate([h, m, h, l, h, m], axis=0)
            left = jnp.concatenate([h, h, m, h, l, m], axis=0)
            first = 128 * chunks[0]
            for lo, hi in ((after, after + panel), (after + panel, size)):
                if lo < hi:
                    update = dot(left[:, lo - first : hi - first], right, ((0,), (0,)))
                    for i, c in enumerate(chunks):
                        work[lo:hi, 128 * c : 128 * c + 128] -= update[:, 128 * i : 128 * i + 128]


SMALL = 32
W_ROW, K_ROW = 16, 19
LEVEL_ROW = 3


def put_split(ref, at, row):
    for n, part in enumerate(split3(row)):
        ref[at + n : at + n + 1, :] = part


def get_split(ref, at):
    h, m, l = (ref[at + n : at + n + 1, :].astype(F32) for n in range(3))
    return (h + m) + l


def prepare(block_ref, weight_ref, gate_ref, kept_ref, full, head, tail, tail_too, small, sems):
    blocks = block_ref.shape[-1]
    values = jnp.zeros((SMALL, blocks), F32)
    rowid = lax.broadcasted_iota(jnp.int32, (SMALL, blocks), 0)
    for n, part in enumerate(split3(weight_ref[...])):
        values = jnp.where(rowid == W_ROW + n, part.astype(F32), values)
    small[...] = jnp.where(rowid == K_ROW, kept_ref[...].astype(F32), values).astype(BF16)
    small[0:16, 0:16] = gate_ref[...].astype(BF16)
    copies = []
    for n, (ref, at) in enumerate(((full, 0), (tail, blocks), (head, 0), (tail_too, blocks))):
        size = ref.shape[0] - SMALL
        copies.append(
            pltpu.make_async_copy(
                block_ref.at[pl.ds(at, size)], ref.at[pl.ds(0, size)], sems.at[n]
            )
        )
        copies.append(
            pltpu.make_async_copy(small, ref.at[pl.ds(size, SMALL)], sems.at[4 + n])
        )
    for copy in copies:
        copy.start()
    for copy in copies:
        copy.wait()


def products(a_blocks, b_blocks, weights, scaled, theta):
    blocks = scaled.shape[-1]

    def block(place):
        ref, n = place
        return ref[n * blocks : (n + 1) * blocks, :]

    for n, place in enumerate(a_blocks):
        w = weights[0 if n < 3 else 1 if n < 7 else 2]
        scaled[n * blocks : (n + 1) * blocks, :] = (block(place).astype(F32) * w).astype(BF16)
    for (distance, q), (right, first_row, count, first) in PIECES.items():
        product = dot(
            scaled[first_row * blocks : (first_row + count) * blocks, :],
            block(b_blocks[right]),
            ((1,), (0,)),
        )
        slot = SLOTS[distance, first, q]
        theta[slot * blocks : (slot + count) * blocks, :] = (
            product * (1.0 / math.sqrt(blocks))
        ).astype(BF16)


def load_gates(gate_rows, gate_stage, gates, sem):
    gate_stage[...] = gate_rows.astype(F32)
    copy = pltpu.make_async_copy(gate_stage, gates, sem)
    copy.start()
    return copy


def bond_body(basis, kept, theta, matrix, proj, work, iso, left, gates, iso_ready):
    blocks = theta.shape[-1]

    def gate(a, b, p, q):
        return gates[4 * a + b, 4 * p + q]

    step = 16

    @pl.loop(0, blocks // step)
    def mix(chunk):
        at = pl.multiple_of(chunk * step, step)
        for half in range(blocks // 128):
            cut = slice(128 * half, 128 * half + 128)
            held = {}

            def term(distance, p, q):
                slot = SLOTS[distance, p, q]
                if slot not in held:
                    place = pl.ds(pl.multiple_of(slot * blocks + at, step), step)
                    held[slot] = theta[place, cut].astype(F32)
                return held[slot]

            for total in range(5):
                for a in range(4):
                    for b in range(4):
                        if CHARGE[a] + CHARGE[b] != total:
                            continue
                        value = None
                        for distance, p, q in TERMS[a, b]:
                            part = gate(a, b, p, q) * term(distance, p, q)
                            value = part if value is None else value + part
                        matrix[
                            pl.ds(pl.multiple_of(a * blocks + at, step), step),
                            b * blocks + 128 * half : b * blocks + 128 * half + 128,
                        ] = value.astype(BF16)
                held.clear()

    projected = dot(basis, matrix[...], ((1,), (0,)))
    slot_id = lax.broadcasted_iota(jnp.int32, projected.shape, 0).astype(F32)
    h, m, l = split3(jnp.where(slot_id < kept, projected, 0.0))
    for n, part in enumerate((h, m, l)):
        proj[n * blocks : (n + 1) * blocks, :] = part
    ri = lax.broadcasted_iota(jnp.int32, (blocks, blocks), 0)
    ci = lax.broadcasted_iota(jnp.int32, (blocks, blocks), 1)
    eye = jnp.where(ri == ci, 1.0, 0.0).astype(F32)
    outer = ((1,), (1,))
    mixed = dot(h, m, outer) + dot(h, l, outer)
    work[:, :blocks] = (dot(h, h, outer) + dot(m, m, outer)) + (mixed + mixed.T) + eye
    work[:, blocks:] = eye
    factor_rows(work, blocks)
    wh, wm, wl = split3(work[:, blocks:])
    h, m, l = (proj[n * blocks : (n + 1) * blocks, :] for n in range(3))
    inner = ((1,), (0,))
    ortho = (
        dot(jnp.concatenate([wh, wm, wl], axis=1), jnp.concatenate([h, h, h], axis=0), inner)
        + dot(jnp.concatenate([wh, wm], axis=1), jnp.concatenate([m, m], axis=0), inner)
        + dot(wh, l, inner)
    )
    ortho = (ortho * math.sqrt(4 * blocks)).astype(BF16)
    for p in range(4):
        iso[p * blocks : (p + 1) * blocks, :] = ortho[:, p * blocks : (p + 1) * blocks]
    iso_ready()
    carried = dot(matrix[...], ortho, outer) * (1.0 / math.sqrt(4 * blocks))
    level = jnp.sqrt(jnp.mean(carried * carried, axis=0, keepdims=True) + 1e-06)
    left[...] = (carried * (1.0 / level)).astype(BF16)
    return level


def first_kernel(
    own, here_full, next_full, next_tail, after_tail, here_head,
    iso, iso_three, left, left_three, local,
    scaled, theta, matrix, proj, work, gate_stage, gates, sems,
):
    x = lax.axis_index("loop") % 2
    c = lax.axis_index("inner") % 2
    blocks = scaled.shape[-1]

    def small(ref):
        return ref.shape[0] - SMALL

    def span(ref, count):
        return [(ref, n) for n in range(count)]

    @pl.when(x == c)
    def _():
        base = small(here_full)
        kept = here_full[base + K_ROW : base + K_ROW + 1, 0:1].astype(F32)
        gates_copy = load_gates(here_full[base : base + 16, 0:128], gate_stage, gates, sems.at[0])
        rest = 6 * blocks
        for role, (one, two, three, four) in enumerate(
            ((own, next_full, next_tail, after_tail), (next_full, own, after_tail, next_tail))
        ):

            @pl.when(x == role)
            def _(one=one, two=two, three=three, four=four):
                products(
                    span(one, 3) + span(here_full, 4) + span(three, 3),
                    span(here_head, 3) + span(two, 4) + span(four, 3),
                    [get_split(ref, small(ref) + W_ROW) for ref in (one, here_full, three)],
                    scaled,
                    theta,
                )
                for n, ref in enumerate((here_head, two)):
                    local[rest + n * SMALL : rest + (n + 1) * SMALL, :] = ref[small(ref) :, :]

        basis = here_full[0 : 4 * blocks, :].T
        gates_copy.wait()
        copies = []

        def out(source, at, target, to, count):
            copies.append(
                pltpu.make_async_copy(
                    source.at[pl.ds(at * blocks, count * blocks)],
                    target.at[pl.ds(to * blocks, count * blocks)],
                    sems.at[1 + len(copies)],
                )
            )
            copies[-1].start()

        def iso_ready():
            out(iso, 1, iso_three, 0, 3)
            out(iso, 0, local, 0, 3)

        level = bond_body(basis, kept, theta, matrix, proj, work, iso, left, gates, iso_ready)
        out(left, 1, left_three, 0, 3)
        out(left, 0, local, 3, 3)
        weights = get_split(local, rest + W_ROW)
        for ref in (iso, iso_three, local):
            ref[small(ref) :, :] = jnp.zeros((SMALL, blocks), BF16)
            put_split(ref, small(ref), weights)
            put_split(ref, small(ref) + LEVEL_ROW, level)
        for copy in copies:
            copy.wait()


def as_column(row):
    return jnp.broadcast_to(row, (row.shape[1], row.shape[1])).T


def second_kernel(
    local, iso_1, iso_2, left_0, left_1, left_2,
    mid, last, first, whole,
    scaled, theta, matrix, proj, work, gate_stage, gates, sems, iso, left,
):
    x = lax.axis_index("loop") % 2
    c = lax.axis_index("inner") % 2
    blocks = scaled.shape[-1]
    rest = 6 * blocks
    near = left_0.shape[0] // blocks - 3

    def small(ref):
        return ref.shape[0] - SMALL

    @pl.when(x != c)
    def _():
        kept = local[rest + K_ROW : rest + K_ROW + 1, 0:1].astype(F32)
        gates_copy = load_gates(local[rest : rest + 16, 0:128], gate_stage, gates, sems.at[0])
        here = [(local, 0), (iso_1, 1), (iso_1, 2), (iso_2, 2)]
        products(
            [(iso_1, 0), (iso_2, 0), (iso_2, 1)] + here + [(local, 1), (local, 2), (iso_1, 3)],
            [(left_0, near + n) for n in range(3)]
            + [(left_1, n) for n in range(4)]
            + [(left_2, n) for n in range(3)],
            [
                get_split(iso_1, small(iso_1)),
                get_split(local, rest + W_ROW),
                get_split(local, rest + SMALL + W_ROW),
            ],
            scaled,
            theta,
        )
        basis = jnp.concatenate(
            [ref[n * blocks : (n + 1) * blocks, :] for ref, n in here], axis=0
        ).T
        gates_copy.wait()
        level = bond_body(
            basis, kept, theta, matrix, proj, work, iso, left, gates, lambda: None
        )
        levels = [get_split(ref, small(ref) + LEVEL_ROW) for ref in (local, iso_1, iso_2)]
        column = as_column(level)
        for ref, lo, hi in ((last, 3, 4), (mid, 1, 3), (first, 0, 1)):
            for p in range(lo, hi):
                value = iso[p * blocks : (p + 1) * blocks, :].astype(F32) * column
                ref[(p - lo) * blocks : (p - lo + 1) * blocks, :] = value.astype(BF16)
        scales = [as_column(value) for value in levels]
        for p in range(4):
            rows = slice(p * blocks, (p + 1) * blocks)
            whole[rows, :] = (left[rows, :].astype(F32) * scales[CHARGE[p]]).astype(BF16)
        for ref, value in ((first, levels[0]), (whole, level)):
            ref[small(ref) :, :] = jnp.zeros((SMALL, blocks), BF16)
            put_split(ref, small(ref) + LEVEL_ROW, value)


def place(plan, out, sems):
    blocks = out.shape[-1]
    copies = []
    for n, (source, to, count) in enumerate(plan):
        copies.append(
            pltpu.make_async_copy(
                source.at[pl.ds(0, count * blocks)],
                out.at[pl.ds(to * blocks, count * blocks)],
                sems.at[n],
            )
        )
    for copy in copies:
        copy.start()
    return copies


def assemble(
    first_mine, first, mid, last, whole_mine, whole, level_mine, level_far, out, weights, sems
):
    x = lax.axis_index("loop") % 2
    c = lax.axis_index("inner") % 2
    even = [(mid, 1, 2), (last, 3, 1)]
    for role, core, plan, level in (
        (0, 0, [(first, 0, 1)] + even, level_far),
        (0, 1, [(first_mine, 0, 1)] + even, level_mine),
        (1, 0, [(whole_mine, 0, 4)], whole_mine),
        (1, 1, [(whole, 0, 4)], whole),
    ):

        @pl.when(jnp.logical_and(x == role, c == core))
        def _(plan=plan, level=level):
            copies = place(plan, out, sems)
            weights[...] = get_split(level, level.shape[0] - SMALL + LEVEL_ROW)
            for copy in copies:
                copy.wait()


def scratch(blocks):
    return [
        pltpu.VMEM((10 * blocks, blocks), BF16),
        pltpu.VMEM((SLOT_COUNT * blocks, blocks), BF16),
        pltpu.VMEM((4 * blocks, 4 * blocks), BF16),
        pltpu.VMEM((3 * blocks, 4 * blocks), BF16),
        pltpu.VMEM((blocks, 2 * blocks), F32),
        pltpu.VMEM((16, 128), F32),
        pltpu.SMEM((16, 128), F32),
        pltpu.SemaphoreType.DMA((5,)),
    ]


def vmem():
    return pl.BlockSpec(memory_space=pltpu.VMEM)


def hbm():
    return pl.BlockSpec(memory_space=pl.ANY)


def params():
    return pltpu.CompilerParams(vmem_limit_bytes=VMEM_BYTES)


def per_device(loops, inners, site_blocks, bond_weights, bond_gates, kept_slots):
    blocks = site_blocks.shape[-1]

    def rows(count, small=0):
        return jax.ShapeDtypeStruct((count * blocks + small, blocks), BF16)

    def send(value, where):
        route = []
        for l in range(loops):
            for i in range(inners):
                source = where(l, i)
                if source is not None:
                    sl, si = source
                    route.append(((sl % loops) * inners + si % inners, l * inners + i))
        return lax.ppermute(value, AXES, route)

    def to_first(even, odd):
        return lambda l, i: (even, odd)[l % 2](l, i // 2) if i % 2 == l % 2 else None

    def to_second(where):
        return lambda l, i: where(l, i // 2) if i % 2 != l % 2 else None

    full, head, tail, tail_too = pl.pallas_call(
        prepare,
        out_shape=(rows(4, SMALL), rows(3, SMALL), rows(3, SMALL), rows(3, SMALL)),
        in_specs=[vmem()] * 4,
        out_specs=(hbm(),) * 4,
        scratch_shapes=[pltpu.VMEM((SMALL, blocks), BF16), pltpu.SemaphoreType.DMA((8,))],
        compiler_params=params(),
        name="prepare",
    )(site_blocks.reshape(4 * blocks, blocks), bond_weights[0], bond_gates[0], kept_slots)

    next_full = send(
        full, to_first(lambda l, k: (l + 1, 2 * k + 2), lambda l, k: (l - 1, 2 * k - 1))
    )
    here_full = send(full, to_first(lambda l, k: (l, 2 * k + 1), lambda l, k: (l - 1, 2 * k)))
    next_tail = send(tail, to_first(lambda l, k: (l, 2 * k + 2), lambda l, k: (l, 2 * k + 2)))
    after_tail = send(
        tail_too, to_first(lambda l, k: (l + 1, 2 * k + 3), lambda l, k: (l - 1, 2 * k + 1))
    )
    here_head = send(head, to_first(lambda l, k: (l + 1, 2 * k + 1), lambda l, k: (l, 2 * k)))

    iso_msg, iso_three, left_msg, left_three, local = pl.pallas_call(
        first_kernel,
        out_shape=(rows(4, SMALL), rows(3, SMALL), rows(4), rows(3), rows(6, 3 * SMALL)),
        in_specs=[vmem()] * 6,
        out_specs=(vmem(),) * 5,
        scratch_shapes=scratch(blocks),
        compiler_params=params(),
        name="first_bond",
    )(full, here_full, next_full, next_tail, after_tail, here_head)

    def worker(l, k, d, s):
        sector = 2 * k + 1 - l % 2 + s
        site = 1 - sector % 2
        return (l - l % 2 + 2 * d + site, sector // 2 * 2 + site)

    local_r = send(local, to_second(lambda l, k: worker(l, k, 0, 0)))
    iso_1 = send(iso_msg, to_second(lambda l, k: worker(l, k, 0, -1)))
    iso_2 = send(iso_three, to_second(lambda l, k: worker(l, k, 0, -2)))
    left_1 = send(left_msg, to_second(lambda l, k: worker(l, k, 1, 1)))
    left_2 = send(left_three, to_second(lambda l, k: worker(l, k, 1, 2)))
    if loops == 2:
        left_0 = local_r
    else:
        left_0 = send(left_msg[: 3 * blocks], to_second(lambda l, k: worker(l, k, 1, 0)))

    mid, last, first, whole = pl.pallas_call(
        second_kernel,
        out_shape=(rows(2), rows(1, SMALL + 16), rows(1, SMALL), rows(4, SMALL)),
        in_specs=[vmem()] * 6,
        out_specs=(vmem(),) * 4,
        scratch_shapes=scratch(blocks) + [pltpu.VMEM((4 * blocks, blocks), BF16)] * 2,
        compiler_params=params(),
        name="second_bond",
    )(local_r, iso_1, iso_2, left_0, left_1, left_2)

    def from_second(l, i, d, s):
        sector = i - s
        site = 1 - sector % 2
        return (l - l % 2 - 2 * d + site, sector // 2 * 2 + 1 - site)

    def right_from(s, cores):
        return lambda l, i: from_second(l, i, 1, s) if l % 2 == 0 and i % 2 in cores else None

    first_r = send(first, right_from(0, (0,) if loops == 2 else (0, 1)))
    mid_r = send(mid, right_from(1, (0, 1)))
    last_r = send(last, right_from(2, (0, 1)))
    whole_r = send(whole, lambda l, i: from_second(l, i, 0, 0) if l % 2 and i % 2 else None)
    if loops == 2:
        first_mine, level_far = first, first_r
    else:
        first_mine = first_r
        level_far = send(
            iso_msg[4 * blocks :], lambda l, i: (l + 1, i + 1) if l % 2 == 0 and i % 2 == 0 else None
        )
    sites, weights = pl.pallas_call(
        assemble,
        out_shape=(rows(4), jax.ShapeDtypeStruct((1, blocks), F32)),
        in_specs=[vmem()] * 8,
        out_specs=(hbm(), vmem()),
        scratch_shapes=[pltpu.SemaphoreType.DMA((3,))],
        compiler_params=params(),
        name="assemble",
    )(first_mine, first_r, mid_r, last_r, whole, whole_r, local_r, level_far)
    return sites.reshape(1, 1, 4, blocks, blocks), weights[None]


def solution(mesh):
    return jax.shard_map(
        functools.partial(per_device, mesh.shape["loop"], mesh.shape["inner"]),
        mesh=mesh,
        in_specs=(
            P("loop", "inner", None, None, None),
            P("loop", "inner", None),
            P("loop", None, None),
            P("loop", "inner"),
        ),
        out_specs=(P("loop", "inner", None, None, None), P("loop", "inner", None)),
        check_vma=False,
    )
```

```python
import functools
import math

import jax
import jax.numpy as jnp
import numpy as np
from jax import lax
from jax.experimental import pallas as pl
from jax.experimental.pallas import tpu as pltpu
from jax.sharding import PartitionSpec as P

CHARGE = (0, 1, 1, 2)
AXES = ("loop", "inner")
BF16, F32 = jnp.bfloat16, jnp.float32
VMEM_BYTES = 24 << 20
HIGHEST = lax.Precision.HIGHEST


def gate_terms():
    table = {}
    for a in range(4):
        for b in range(4):
            table[a, b] = [
                (CHARGE[p] - CHARGE[a], p, q)
                for p in range(4)
                for q in range(4)
                if CHARGE[p] + CHARGE[q] == CHARGE[a] + CHARGE[b]
                and abs(CHARGE[p] - CHARGE[a]) <= 1
            ]
    return table


TERMS = gate_terms()
PIECES = {
    (0, 0): (0, 3, 4, 0),
    (0, 1): (4, 3, 4, 0),
    (0, 2): (5, 3, 4, 0),
    (0, 3): (9, 3, 4, 0),
    (-1, 1): (1, 0, 3, 0),
    (-1, 2): (2, 0, 3, 0),
    (-1, 3): (6, 0, 3, 0),
    (1, 0): (3, 7, 3, 1),
    (1, 1): (7, 7, 3, 1),
    (1, 2): (8, 7, 3, 1),
}


def theta_slots():
    slots, count = {}, 0
    for (distance, q), (_, _, rows, first) in PIECES.items():
        for p in range(rows):
            slots[distance, first + p, q] = count
            count += 1
    return slots, count


SLOTS, SLOT_COUNT = theta_slots()


def dot(a, b, dims, precision=None):
    return lax.dot_general(a, b, (dims, ((), ())), precision=precision, preferred_element_type=F32)


def split3(a):
    h = a.astype(BF16)
    r = a - h.astype(F32)
    m = r.astype(BF16)
    return h, m, (r - m.astype(F32)).astype(BF16)


def factor_rows(work, size, panel=32):
    tiles = panel // 8
    sub = lax.broadcasted_iota(jnp.int32, (8, 128), 0)
    for start in range(0, size, panel):
        low = start < size // 2
        chunks = [0, 1, 2] if low else [1, 2, 3]
        base = start % 128
        rows = [
            [work[start + 8 * t : start + 8 * t + 8, 128 * c : 128 * c + 128] for c in chunks]
            for t in range(tiles)
        ]

        def column(k):
            return {
                t: jnp.broadcast_to(rows[t][0][:, base + k : base + k + 1], (8, 128))
                for t in range(k // 8, tiles)
            }

        def at(col, k):
            return jnp.broadcast_to(col[k // 8][k % 8 : k % 8 + 1, :], (8, 128))

        pivots = [jnp.ones((8, 128), F32) for _ in range(tiles)]
        cols = {k: column(k) for k in range(8)}
        for g in range(tiles):
            if g + 1 < tiles:
                cols.update({k: column(k) for k in range(8 * g + 8, 8 * g + 16)})

            def below(col, j):
                return {
                    t: (jnp.where(sub > j % 8, v, 0.0) if t == j // 8 else v)
                    for t, v in col.items()
                    if t >= g
                }

            for j in range(8 * g, 8 * g + 8, 2):
                one, two = cols[j], cols[j + 1]
                a, b, c = at(one, j), at(one, j + 1), at(two, j + 1)
                det = a * c - b * b
                ra, rd = 1.0 / a, 1.0 / det
                first = {t: v * ra for t, v in below(one, j).items()}
                ratio = b * ra
                two = {t: two[t] - one[t] * ratio for t in one if t >= g}
                second = {t: v * (a * rd) for t, v in below(two, j + 1).items()}
                for k in cols:
                    if k > j + 1:
                        e1, e2 = at(one, k), at(two, k)
                        cols[k] = {
                            t: v - (first[t] * e1 + second[t] * e2) for t, v in cols[k].items()
                        }
                for i in range(len(chunks)):
                    r = j % 8
                    x0 = jnp.broadcast_to(rows[g][i][r : r + 1, :], (8, 128))
                    x1 = jnp.broadcast_to(rows[g][i][r + 1 : r + 2, :], (8, 128)) - ratio * x0
                    for t in range(g, tiles):
                        rows[t][i] = rows[t][i] - (first[t] * x0 + second[t] * x1)
                pivots[g] = jnp.where(
                    sub == j % 8, a, jnp.where(sub == j % 8 + 1, det * ra, pivots[g])
                )
        done = []
        for t in range(tiles):
            scale = lax.rsqrt(pivots[t])
            done.append([x * scale for x in rows[t]])
            for c, x in zip(chunks, done[t]):
                work[start + 8 * t : start + 8 * t + 8, 128 * c : 128 * c + 128] = x
        after = start + panel
        if after < size:
            h, m, l = split3(
                jnp.concatenate([jnp.concatenate(xs, axis=1) for xs in done], axis=0)
            )
            right = jnp.concatenate([h, m, h, l, h, m], axis=0)
            left = jnp.concatenate([h, h, m, h, l, m], axis=0)
            first = 128 * chunks[0]
            for lo, hi in ((after, after + panel), (after + panel, size)):
                if lo < hi:
                    update = dot(left[:, lo - first : hi - first], right, ((0,), (0,)))
                    for i, c in enumerate(chunks):
                        work[lo:hi, 128 * c : 128 * c + 128] -= update[:, 128 * i : 128 * i + 128]


SMALL = 32
W_ROW, K_ROW = 16, 19
LEVEL_ROW = 3


def put_split(ref, at, row):
    for n, part in enumerate(split3(row)):
        ref[at + n : at + n + 1, :] = part


def get_split(ref, at):
    h, m, l = (ref[at + n : at + n + 1, :].astype(F32) for n in range(3))
    return (h + m) + l


def prepare(block_ref, weight_ref, gate_ref, kept_ref, full, head, tail, small, sems):
    blocks = block_ref.shape[-1]
    values = jnp.zeros((SMALL, blocks), F32)
    rowid = lax.broadcasted_iota(jnp.int32, (SMALL, blocks), 0)
    for n, part in enumerate(split3(weight_ref[...])):
        values = jnp.where(rowid == W_ROW + n, part.astype(F32), values)
    small[...] = jnp.where(rowid == K_ROW, kept_ref[...].astype(F32), values).astype(BF16)
    small[0:16, 0:16] = gate_ref[...].astype(BF16)
    copies = []
    for n, (ref, at) in enumerate(((full, 0), (tail, blocks), (head, 0))):
        size = ref.shape[0] - SMALL
        copies.append(
            pltpu.make_async_copy(
                block_ref.at[pl.ds(at, size)], ref.at[pl.ds(0, size)], sems.at[n]
            )
        )
        copies.append(
            pltpu.make_async_copy(small, ref.at[pl.ds(size, SMALL)], sems.at[3 + n])
        )
    for copy in copies:
        copy.start()
    for copy in copies:
        copy.wait()


def products(a_blocks, b_blocks, weights, scaled, theta):
    blocks = scaled.shape[-1]

    def block(place):
        ref, n = place
        return ref[n * blocks : (n + 1) * blocks, :]

    for n, place in enumerate(a_blocks):
        w = weights[0 if n < 3 else 1 if n < 7 else 2]
        scaled[n * blocks : (n + 1) * blocks, :] = (block(place).astype(F32) * w).astype(BF16)
    for (distance, q), (right, first_row, count, first) in PIECES.items():
        product = dot(
            scaled[first_row * blocks : (first_row + count) * blocks, :],
            block(b_blocks[right]),
            ((1,), (0,)),
        )
        slot = SLOTS[distance, first, q]
        theta[slot * blocks : (slot + count) * blocks, :] = (
            product * (1.0 / math.sqrt(blocks))
        ).astype(BF16)


def load_gates(gate_rows, gate_stage, gates, sem):
    gate_stage[...] = gate_rows.astype(F32)
    copy = pltpu.make_async_copy(gate_stage, gates, sem)
    copy.start()
    return copy


def bond_body(basis, kept, theta, matrix, proj, work, iso, left, gates, iso_ready):
    blocks = theta.shape[-1]

    def gate(a, b, p, q):
        return gates[4 * a + b, 4 * p + q]

    step = 16

    @pl.loop(0, blocks // step)
    def mix(chunk):
        at = pl.multiple_of(chunk * step, step)
        for half in range(blocks // 128):
            cut = slice(128 * half, 128 * half + 128)
            held = {}

            def term(distance, p, q):
                slot = SLOTS[distance, p, q]
                if slot not in held:
                    place = pl.ds(pl.multiple_of(slot * blocks + at, step), step)
                    held[slot] = theta[place, cut].astype(F32)
                return held[slot]

            for total in range(5):
                for a in range(4):
                    for b in range(4):
                        if CHARGE[a] + CHARGE[b] != total:
                            continue
                        value = None
                        for distance, p, q in TERMS[a, b]:
                            part = gate(a, b, p, q) * term(distance, p, q)
                            value = part if value is None else value + part
                        matrix[
                            pl.ds(pl.multiple_of(a * blocks + at, step), step),
                            b * blocks + 128 * half : b * blocks + 128 * half + 128,
                        ] = value.astype(BF16)
                held.clear()

    projected = dot(basis, matrix[...], ((1,), (0,)))
    slot_id = lax.broadcasted_iota(jnp.int32, projected.shape, 0).astype(F32)
    h, m, l = split3(jnp.where(slot_id < kept, projected, 0.0))
    for n, part in enumerate((h, m, l)):
        proj[n * blocks : (n + 1) * blocks, :] = part
    ri = lax.broadcasted_iota(jnp.int32, (blocks, blocks), 0)
    ci = lax.broadcasted_iota(jnp.int32, (blocks, blocks), 1)
    eye = jnp.where(ri == ci, 1.0, 0.0).astype(F32)
    outer = ((1,), (1,))
    mixed = dot(h, m, outer) + dot(h, l, outer)
    work[:, :blocks] = (dot(h, h, outer) + dot(m, m, outer)) + (mixed + mixed.T) + eye
    work[:, blocks:] = eye
    factor_rows(work, blocks)
    wh, wm, wl = split3(work[:, blocks:])
    h, m, l = (proj[n * blocks : (n + 1) * blocks, :] for n in range(3))
    inner = ((1,), (0,))
    ortho = (
        dot(jnp.concatenate([wh, wm, wl], axis=1), jnp.concatenate([h, h, h], axis=0), inner)
        + dot(jnp.concatenate([wh, wm], axis=1), jnp.concatenate([m, m], axis=0), inner)
        + dot(wh, l, inner)
    )
    ortho = (ortho * math.sqrt(4 * blocks)).astype(BF16)
    for p in range(4):
        iso[p * blocks : (p + 1) * blocks, :] = ortho[:, p * blocks : (p + 1) * blocks]
    iso_ready()
    flipped = ortho.T
    parts, total = [], 0.0
    for p in range(4):
        rows = matrix[p * blocks : (p + 1) * blocks, :]
        parts.append(dot(rows, flipped, inner) * (1.0 / math.sqrt(4 * blocks)))
        total = total + jnp.sum(parts[p] * parts[p], axis=0, keepdims=True)
    level = jnp.sqrt(total * (1.0 / (4 * blocks)) + 1e-06)
    scale = 1.0 / level
    for p in range(4):
        left[p * blocks : (p + 1) * blocks, :] = (parts[p] * scale).astype(BF16)
    return level


def first_kernel(
    own, here_full, next_full, here_head, after_tail, next_tail,
    iso, iso_three, left, left_three, local,
    scaled, theta, matrix, proj, work, gate_stage, gates, sems,
):
    x = lax.axis_index("loop") % 2
    c = lax.axis_index("inner") % 2
    blocks = scaled.shape[-1]

    def small(ref):
        return ref.shape[0] - SMALL

    def span(ref, count):
        return [(ref, n) for n in range(count)]

    @pl.when(x == c)
    def _():
        base = small(here_full)
        kept = here_full[base + K_ROW : base + K_ROW + 1, 0:1].astype(F32)
        gates_copy = load_gates(here_full[base : base + 16, 0:128], gate_stage, gates, sems.at[0])
        rest = 6 * blocks
        for role, (one, two, three, four) in enumerate(
            ((own, next_full, next_tail, after_tail), (next_full, own, after_tail, next_tail))
        ):

            @pl.when(x == role)
            def _(one=one, two=two, three=three, four=four):
                products(
                    span(one, 3) + span(here_full, 4) + span(three, 3),
                    span(here_head, 3) + span(two, 4) + span(four, 3),
                    [get_split(ref, small(ref) + W_ROW) for ref in (one, here_full, three)],
                    scaled,
                    theta,
                )
                for n, ref in enumerate((here_head, two)):
                    local[rest + n * SMALL : rest + (n + 1) * SMALL, :] = ref[small(ref) :, :]

        basis = here_full[0 : 4 * blocks, :].T
        gates_copy.wait()
        copies = []

        def out(source, at, target, to, count):
            copies.append(
                pltpu.make_async_copy(
                    source.at[pl.ds(at * blocks, count * blocks)],
                    target.at[pl.ds(to * blocks, count * blocks)],
                    sems.at[1 + len(copies)],
                )
            )
            copies[-1].start()

        def iso_ready():
            out(iso, 1, iso_three, 0, 3)
            out(iso, 0, local, 0, 3)

        level = bond_body(basis, kept, theta, matrix, proj, work, iso, left, gates, iso_ready)
        out(left, 1, left_three, 0, 3)
        out(left, 0, local, 3, 3)
        weights = get_split(local, rest + W_ROW)
        for ref in (iso, iso_three, local):
            ref[small(ref) :, :] = jnp.zeros((SMALL, blocks), BF16)
            put_split(ref, small(ref), weights)
            put_split(ref, small(ref) + LEVEL_ROW, level)
        for copy in copies:
            copy.wait()


def as_column(row):
    return jnp.broadcast_to(row, (row.shape[1], row.shape[1])).T


def second_kernel(
    local, iso_1, iso_2, left_0, left_1, left_2,
    mid, last, first, whole,
    scaled, theta, matrix, proj, work, gate_stage, gates, sems, iso, left,
):
    x = lax.axis_index("loop") % 2
    c = lax.axis_index("inner") % 2
    blocks = scaled.shape[-1]
    rest = 6 * blocks
    near = left_0.shape[0] // blocks - 3

    def small(ref):
        return ref.shape[0] - SMALL

    @pl.when(x != c)
    def _():
        kept = local[rest + K_ROW : rest + K_ROW + 1, 0:1].astype(F32)
        gates_copy = load_gates(local[rest : rest + 16, 0:128], gate_stage, gates, sems.at[0])
        here = [(local, 0), (iso_1, 1), (iso_1, 2), (iso_2, 2)]
        products(
            [(iso_1, 0), (iso_2, 0), (iso_2, 1)] + here + [(local, 1), (local, 2), (iso_1, 3)],
            [(left_0, near + n) for n in range(3)]
            + [(left_1, n) for n in range(4)]
            + [(left_2, n) for n in range(3)],
            [
                get_split(iso_1, small(iso_1)),
                get_split(local, rest + W_ROW),
                get_split(local, rest + SMALL + W_ROW),
            ],
            scaled,
            theta,
        )
        basis = jnp.concatenate(
            [ref[n * blocks : (n + 1) * blocks, :] for ref, n in here], axis=0
        ).T
        gates_copy.wait()
        level = bond_body(
            basis, kept, theta, matrix, proj, work, iso, left, gates, lambda: None
        )
        levels = [get_split(ref, small(ref) + LEVEL_ROW) for ref in (local, iso_1, iso_2)]
        column = as_column(level)
        for ref, lo, hi in ((last, 3, 4), (mid, 1, 3), (first, 0, 1)):
            for p in range(lo, hi):
                value = iso[p * blocks : (p + 1) * blocks, :].astype(F32) * column
                ref[(p - lo) * blocks : (p - lo + 1) * blocks, :] = value.astype(BF16)
        scales = [as_column(value) for value in levels]
        for p in range(4):
            rows = slice(p * blocks, (p + 1) * blocks)
            whole[rows, :] = (left[rows, :].astype(F32) * scales[CHARGE[p]]).astype(BF16)
        for ref, value in ((first, levels[0]), (whole, level)):
            ref[small(ref) :, :] = jnp.zeros((SMALL, blocks), BF16)
            put_split(ref, small(ref) + LEVEL_ROW, value)


def place(plan, out, sems):
    blocks = out.shape[-1]
    half = blocks // 2
    copies = []
    for source, to, count in plan:
        for n in range(2 * count):
            copies.append(
                pltpu.make_async_copy(
                    source.at[pl.ds(n * half, half)],
                    out.at[pl.ds(to * blocks + n * half, half)],
                    sems.at[len(copies)],
                )
            )
            copies[-1].start()
    return copies


def assemble(
    first_mine, first, mid, last, whole_mine, whole, level_mine, level_far, out, weights, sems
):
    x = lax.axis_index("loop") % 2
    c = lax.axis_index("inner") % 2
    even = [(mid, 1, 2), (last, 3, 1)]
    for role, core, plan, level in (
        (0, 0, [(first, 0, 1)] + even, level_far),
        (0, 1, [(first_mine, 0, 1)] + even, level_mine),
        (1, 0, [(whole_mine, 0, 4)], whole_mine),
        (1, 1, [(whole, 0, 4)], whole),
    ):

        @pl.when(jnp.logical_and(x == role, c == core))
        def _(plan=plan, level=level):
            copies = place(plan, out, sems)
            weights[...] = get_split(level, level.shape[0] - SMALL + LEVEL_ROW)
            for copy in copies:
                copy.wait()


def scratch(blocks):
    return [
        pltpu.VMEM((10 * blocks, blocks), BF16),
        pltpu.VMEM((SLOT_COUNT * blocks, blocks), BF16),
        pltpu.VMEM((4 * blocks, 4 * blocks), BF16),
        pltpu.VMEM((3 * blocks, 4 * blocks), BF16),
        pltpu.VMEM((blocks, 2 * blocks), F32),
        pltpu.VMEM((16, 128), F32),
        pltpu.SMEM((16, 128), F32),
        pltpu.SemaphoreType.DMA((5,)),
    ]


def vmem():
    return pl.BlockSpec(memory_space=pltpu.VMEM)


def hbm():
    return pl.BlockSpec(memory_space=pl.ANY)


def params():
    return pltpu.CompilerParams(vmem_limit_bytes=VMEM_BYTES)


def per_device(loops, inners, site_blocks, bond_weights, bond_gates, kept_slots):
    blocks = site_blocks.shape[-1]

    def rows(count, small=0):
        return jax.ShapeDtypeStruct((count * blocks + small, blocks), BF16)

    def send(value, where):
        route = []
        for l in range(loops):
            for i in range(inners):
                source = where(l, i)
                if source is not None:
                    sl, si = source
                    route.append(((sl % loops) * inners + si % inners, l * inners + i))
        return lax.ppermute(value, AXES, route)

    def to_first(even, odd):
        return lambda l, i: (even, odd)[l % 2](l, i // 2) if i % 2 == l % 2 else None

    def to_second(where):
        return lambda l, i: where(l, i // 2) if i % 2 != l % 2 else None

    full, head, tail = pl.pallas_call(
        prepare,
        out_shape=(rows(4, SMALL), rows(3, SMALL), rows(3, SMALL)),
        in_specs=[vmem()] * 4,
        out_specs=(hbm(),) * 3,
        scratch_shapes=[pltpu.VMEM((SMALL, blocks), BF16), pltpu.SemaphoreType.DMA((6,))],
        compiler_params=params(),
        name="prepare",
    )(site_blocks.reshape(4 * blocks, blocks), bond_weights[0], bond_gates[0], kept_slots)

    next_full = send(
        full, to_first(lambda l, k: (l + 1, 2 * k + 2), lambda l, k: (l - 1, 2 * k - 1))
    )
    here_full = send(full, to_first(lambda l, k: (l, 2 * k + 1), lambda l, k: (l - 1, 2 * k)))
    next_tail = send(tail, to_first(lambda l, k: (l, 2 * k + 2), lambda l, k: (l, 2 * k + 2)))
    after_tail = send(
        tail, to_first(lambda l, k: (l + 1, 2 * k + 3), lambda l, k: (l - 1, 2 * k + 1))
    )
    here_head = send(head, to_first(lambda l, k: (l + 1, 2 * k + 1), lambda l, k: (l, 2 * k)))

    iso_msg, iso_three, left_msg, left_three, local = pl.pallas_call(
        first_kernel,
        out_shape=(rows(4, SMALL), rows(3, SMALL), rows(4), rows(3), rows(6, 3 * SMALL)),
        in_specs=[vmem()] * 6,
        out_specs=(vmem(),) * 5,
        scratch_shapes=scratch(blocks),
        compiler_params=params(),
        name="first_bond",
    )(full, here_full, next_full, here_head, after_tail, next_tail)

    def worker(l, k, d, s):
        sector = 2 * k + 1 - l % 2 + s
        site = 1 - sector % 2
        return (l - l % 2 + 2 * d + site, sector // 2 * 2 + site)

    local_r = send(local, to_second(lambda l, k: worker(l, k, 0, 0)))
    iso_1 = send(iso_msg, to_second(lambda l, k: worker(l, k, 0, -1)))
    iso_2 = send(iso_three, to_second(lambda l, k: worker(l, k, 0, -2)))
    left_1 = send(left_msg, to_second(lambda l, k: worker(l, k, 1, 1)))
    left_2 = send(left_three, to_second(lambda l, k: worker(l, k, 1, 2)))
    if loops == 2:
        left_0 = local_r
    else:
        left_0 = send(left_msg[: 3 * blocks], to_second(lambda l, k: worker(l, k, 1, 0)))

    mid, last, first, whole = pl.pallas_call(
        second_kernel,
        out_shape=(rows(2), rows(1), rows(1, SMALL), rows(4, SMALL)),
        in_specs=[vmem()] * 6,
        out_specs=(vmem(),) * 4,
        scratch_shapes=scratch(blocks) + [pltpu.VMEM((4 * blocks, blocks), BF16)] * 2,
        compiler_params=params(),
        name="second_bond",
    )(local_r, iso_1, iso_2, left_0, left_1, left_2)

    def from_second(l, i, d, s):
        sector = i - s
        site = 1 - sector % 2
        return (l - l % 2 - 2 * d + site, sector // 2 * 2 + 1 - site)

    def right_from(s, cores):
        return lambda l, i: from_second(l, i, 1, s) if l % 2 == 0 and i % 2 in cores else None

    first_r = send(first, right_from(0, (0,) if loops == 2 else (0, 1)))
    mid_r = send(mid, right_from(1, (0, 1)))
    last_r = send(last, right_from(2, (0, 1)))
    whole_r = send(whole, lambda l, i: from_second(l, i, 0, 0) if l % 2 and i % 2 else None)
    if loops == 2:
        first_mine, level_far = first, first_r
    else:
        first_mine = first_r
        level_far = send(
            iso_msg[4 * blocks :], lambda l, i: (l + 1, i + 1) if l % 2 == 0 and i % 2 == 0 else None
        )
    sites, weights = pl.pallas_call(
        assemble,
        out_shape=(rows(4), jax.ShapeDtypeStruct((1, blocks), F32)),
        in_specs=[vmem()] * 8,
        out_specs=(hbm(), vmem()),
        scratch_shapes=[pltpu.SemaphoreType.DMA((8,))],
        compiler_params=params(),
        name="assemble",
    )(first_mine, first_r, mid_r, last_r, whole, whole_r, local_r, level_far)
    return sites.reshape(1, 1, 4, blocks, blocks), weights[None]


def solution(mesh):
    return jax.shard_map(
        functools.partial(per_device, mesh.shape["loop"], mesh.shape["inner"]),
        mesh=mesh,
        in_specs=(
            P("loop", "inner", None, None, None),
            P("loop", "inner", None),
            P("loop", None, None),
            P("loop", "inner"),
        ),
        out_specs=(P("loop", "inner", None, None, None), P("loop", "inner", None)),
        check_vma=False,
    )
```

```python
import functools
import math

import jax
import jax.numpy as jnp
import numpy as np
from jax import lax
from jax.experimental import pallas as pl
from jax.experimental.pallas import tpu as pltpu
from jax.sharding import PartitionSpec as P

CHARGE = (0, 1, 1, 2)
AXES = ("loop", "inner")
BF16, F32 = jnp.bfloat16, jnp.float32
VMEM_BYTES = 24 << 20
HIGHEST = lax.Precision.HIGHEST


def gate_terms():
    table = {}
    for a in range(4):
        for b in range(4):
            table[a, b] = [
                (CHARGE[p] - CHARGE[a], p, q)
                for p in range(4)
                for q in range(4)
                if CHARGE[p] + CHARGE[q] == CHARGE[a] + CHARGE[b]
                and abs(CHARGE[p] - CHARGE[a]) <= 1
            ]
    return table


TERMS = gate_terms()
PIECES = {
    (0, 0): (0, 3, 4, 0),
    (0, 1): (4, 3, 4, 0),
    (0, 2): (5, 3, 4, 0),
    (0, 3): (9, 3, 4, 0),
    (-1, 1): (1, 0, 3, 0),
    (-1, 2): (2, 0, 3, 0),
    (-1, 3): (6, 0, 3, 0),
    (1, 0): (3, 7, 3, 1),
    (1, 1): (7, 7, 3, 1),
    (1, 2): (8, 7, 3, 1),
}


def theta_slots():
    slots, count = {}, 0
    for (distance, q), (_, _, rows, first) in PIECES.items():
        for p in range(rows):
            slots[distance, first + p, q] = count
            count += 1
    return slots, count


SLOTS, SLOT_COUNT = theta_slots()


def dot(a, b, dims, precision=None):
    return lax.dot_general(a, b, (dims, ((), ())), precision=precision, preferred_element_type=F32)


def split3(a):
    h = a.astype(BF16)
    r = a - h.astype(F32)
    m = r.astype(BF16)
    return h, m, (r - m.astype(F32)).astype(BF16)


def factor_rows(work, size, panel=32):
    tiles = panel // 8
    sub = lax.broadcasted_iota(jnp.int32, (8, 128), 0)
    for start in range(0, size, panel):
        low = start < size // 2
        chunks = [0, 1, 2] if low else [1, 2, 3]
        base = start % 128
        rows = [
            [work[start + 8 * t : start + 8 * t + 8, 128 * c : 128 * c + 128] for c in chunks]
            for t in range(tiles)
        ]

        def column(k):
            return {
                t: jnp.broadcast_to(rows[t][0][:, base + k : base + k + 1], (8, 128))
                for t in range(k // 8, tiles)
            }

        def at(col, k):
            return jnp.broadcast_to(col[k // 8][k % 8 : k % 8 + 1, :], (8, 128))

        pivots = [jnp.ones((8, 128), F32) for _ in range(tiles)]
        cols = {k: column(k) for k in range(8)}
        for g in range(tiles):
            if g + 1 < tiles:
                cols.update({k: column(k) for k in range(8 * g + 8, 8 * g + 16)})

            def below(col, j):
                return {
                    t: (jnp.where(sub > j % 8, v, 0.0) if t == j // 8 else v)
                    for t, v in col.items()
                    if t >= g
                }

            for j in range(8 * g, 8 * g + 8, 2):
                one, two = cols[j], cols[j + 1]
                a, b, c = at(one, j), at(one, j + 1), at(two, j + 1)
                det = a * c - b * b
                ra, rd = 1.0 / a, 1.0 / det
                first = {t: v * ra for t, v in below(one, j).items()}
                ratio = b * ra
                two = {t: two[t] - one[t] * ratio for t in one if t >= g}
                second = {t: v * (a * rd) for t, v in below(two, j + 1).items()}
                for k in cols:
                    if k > j + 1:
                        e1, e2 = at(one, k), at(two, k)
                        cols[k] = {
                            t: v - (first[t] * e1 + second[t] * e2) for t, v in cols[k].items()
                        }
                for i in range(len(chunks)):
                    r = j % 8
                    x0 = jnp.broadcast_to(rows[g][i][r : r + 1, :], (8, 128))
                    x1 = jnp.broadcast_to(rows[g][i][r + 1 : r + 2, :], (8, 128)) - ratio * x0
                    for t in range(g, tiles):
                        rows[t][i] = rows[t][i] - (first[t] * x0 + second[t] * x1)
                pivots[g] = jnp.where(
                    sub == j % 8, a, jnp.where(sub == j % 8 + 1, det * ra, pivots[g])
                )
        done = []
        for t in range(tiles):
            scale = lax.rsqrt(pivots[t])
            done.append([x * scale for x in rows[t]])
            for c, x in zip(chunks, done[t]):
                work[start + 8 * t : start + 8 * t + 8, 128 * c : 128 * c + 128] = x
        after = start + panel
        if after < size:
            h, m, l = split3(
                jnp.concatenate([jnp.concatenate(xs, axis=1) for xs in done], axis=0)
            )
            right = jnp.concatenate([h, m, h, l, h, m], axis=0)
            left = jnp.concatenate([h, h, m, h, l, m], axis=0)
            first = 128 * chunks[0]
            for lo, hi in ((after, after + panel), (after + panel, size)):
                if lo < hi:
                    update = dot(left[:, lo - first : hi - first], right, ((0,), (0,)))
                    for i, c in enumerate(chunks):
                        work[lo:hi, 128 * c : 128 * c + 128] -= update[:, 128 * i : 128 * i + 128]


SMALL = 32
W_ROW, K_ROW = 16, 19
LEVEL_ROW = 3


def put_split(ref, at, row):
    for n, part in enumerate(split3(row)):
        ref[at + n : at + n + 1, :] = part


def get_split(ref, at):
    h, m, l = (ref[at + n : at + n + 1, :].astype(F32) for n in range(3))
    return (h + m) + l


def prepare(block_ref, weight_ref, gate_ref, kept_ref, full, head, tail, small, sems):
    blocks = block_ref.shape[-1]
    values = jnp.zeros((SMALL, blocks), F32)
    rowid = lax.broadcasted_iota(jnp.int32, (SMALL, blocks), 0)
    for n, part in enumerate(split3(weight_ref[...])):
        values = jnp.where(rowid == W_ROW + n, part.astype(F32), values)
    small[...] = jnp.where(rowid == K_ROW, kept_ref[...].astype(F32), values).astype(BF16)
    small[0:16, 0:16] = gate_ref[...].astype(BF16)
    copies = []
    for n, (ref, at) in enumerate(((full, 0), (tail, blocks), (head, 0))):
        size = ref.shape[0] - SMALL
        copies.append(
            pltpu.make_async_copy(
                block_ref.at[pl.ds(at, size)], ref.at[pl.ds(0, size)], sems.at[n]
            )
        )
        copies.append(
            pltpu.make_async_copy(small, ref.at[pl.ds(size, SMALL)], sems.at[3 + n])
        )
    for copy in copies:
        copy.start()
    for copy in copies:
        copy.wait()


def products(a_blocks, b_blocks, weights, scaled, theta, basis):
    blocks = scaled.shape[-1]

    def block(place):
        ref, n = place
        return ref[n * blocks : (n + 1) * blocks, :]

    for n, place in enumerate(a_blocks):
        w = weights[0 if n < 3 else 1 if n < 7 else 2]
        scaled[n * blocks : (n + 1) * blocks, :] = (block(place).astype(F32) * w).astype(BF16)
    for n in range(4):
        basis[:, n * blocks : (n + 1) * blocks] = block(a_blocks[3 + n]).T
    for (distance, q), (right, first_row, count, first) in PIECES.items():
        product = dot(
            scaled[first_row * blocks : (first_row + count) * blocks, :],
            block(b_blocks[right]),
            ((1,), (0,)),
        )
        slot = SLOTS[distance, first, q]
        theta[slot * blocks : (slot + count) * blocks, :] = (
            product * (1.0 / math.sqrt(blocks))
        ).astype(BF16)


def load_gates(gate_rows, gate_stage, gates, sem):
    gate_stage[...] = gate_rows.astype(F32)
    copy = pltpu.make_async_copy(gate_stage, gates, sem)
    copy.start()
    return copy


def bond_body(basis, kept, theta, matrix, proj, work, iso, left, gates, iso_ready):
    blocks = theta.shape[-1]

    def gate(a, b, p, q):
        return gates[4 * a + b, 4 * p + q]

    step = 16

    @pl.loop(0, blocks // step)
    def mix(chunk):
        at = pl.multiple_of(chunk * step, step)
        for half in range(blocks // 128):
            cut = slice(128 * half, 128 * half + 128)
            held = {}

            def term(distance, p, q):
                slot = SLOTS[distance, p, q]
                if slot not in held:
                    place = pl.ds(pl.multiple_of(slot * blocks + at, step), step)
                    held[slot] = theta[place, cut].astype(F32)
                return held[slot]

            for total in range(5):
                for a in range(4):
                    for b in range(4):
                        if CHARGE[a] + CHARGE[b] != total:
                            continue
                        value = None
                        for distance, p, q in TERMS[a, b]:
                            part = gate(a, b, p, q) * term(distance, p, q)
                            value = part if value is None else value + part
                        matrix[
                            pl.ds(pl.multiple_of(a * blocks + at, step), step),
                            b * blocks + 128 * half : b * blocks + 128 * half + 128,
                        ] = value.astype(BF16)
                held.clear()

    projected = dot(basis[...], matrix[...], ((1,), (0,)))
    slot_id = lax.broadcasted_iota(jnp.int32, projected.shape, 0).astype(F32)
    h, m, l = split3(jnp.where(slot_id < kept, projected, 0.0))
    for n, part in enumerate((h, m, l)):
        proj[n * blocks : (n + 1) * blocks, :] = part
    ri = lax.broadcasted_iota(jnp.int32, (blocks, blocks), 0)
    ci = lax.broadcasted_iota(jnp.int32, (blocks, blocks), 1)
    eye = jnp.where(ri == ci, 1.0, 0.0).astype(F32)
    outer = ((1,), (1,))
    mixed = dot(h, m, outer) + dot(h, l, outer)
    work[:, :blocks] = (dot(h, h, outer) + dot(m, m, outer)) + (mixed + mixed.T) + eye
    work[:, blocks:] = eye
    factor_rows(work, blocks)
    wh, wm, wl = split3(work[:, blocks:])
    h, m, l = (proj[n * blocks : (n + 1) * blocks, :] for n in range(3))
    inner = ((1,), (0,))
    ortho = (
        dot(jnp.concatenate([wh, wm, wl], axis=1), jnp.concatenate([h, h, h], axis=0), inner)
        + dot(jnp.concatenate([wh, wm], axis=1), jnp.concatenate([m, m], axis=0), inner)
        + dot(wh, l, inner)
    )
    ortho = (ortho * math.sqrt(4 * blocks)).astype(BF16)
    for p in range(4):
        iso[p * blocks : (p + 1) * blocks, :] = ortho[:, p * blocks : (p + 1) * blocks]
    iso_ready()
    flipped = ortho.T
    parts, total = [], 0.0
    for p in range(4):
        rows = matrix[p * blocks : (p + 1) * blocks, :]
        parts.append(dot(rows, flipped, inner) * (1.0 / math.sqrt(4 * blocks)))
        total = total + jnp.sum(parts[p] * parts[p], axis=0, keepdims=True)
    level = jnp.sqrt(total * (1.0 / (4 * blocks)) + 1e-06)
    scale = 1.0 / level
    for p in range(4):
        left[p * blocks : (p + 1) * blocks, :] = (parts[p] * scale).astype(BF16)
    return level


def first_kernel(
    own, here_full, next_full, here_head, after_tail, next_tail,
    iso, iso_three, left, left_three, local,
    scaled, theta, basis, matrix, proj, work, gate_stage, gates, sems,
):
    x = lax.axis_index("loop") % 2
    c = lax.axis_index("inner") % 2
    blocks = scaled.shape[-1]

    def small(ref):
        return ref.shape[0] - SMALL

    def span(ref, count):
        return [(ref, n) for n in range(count)]

    @pl.when(x == c)
    def _():
        base = small(here_full)
        kept = here_full[base + K_ROW : base + K_ROW + 1, 0:1].astype(F32)
        gates_copy = load_gates(here_full[base : base + 16, 0:128], gate_stage, gates, sems.at[0])
        rest = 6 * blocks
        for role, (one, two, three, four) in enumerate(
            ((own, next_full, next_tail, after_tail), (next_full, own, after_tail, next_tail))
        ):

            @pl.when(x == role)
            def _(one=one, two=two, three=three, four=four):
                products(
                    span(one, 3) + span(here_full, 4) + span(three, 3),
                    span(here_head, 3) + span(two, 4) + span(four, 3),
                    [get_split(ref, small(ref) + W_ROW) for ref in (one, here_full, three)],
                    scaled,
                    theta,
                    basis,
                )
                for n, ref in enumerate((here_head, two)):
                    local[rest + n * SMALL : rest + (n + 1) * SMALL, :] = ref[small(ref) :, :]

        gates_copy.wait()
        copies = []

        def out(source, at, target, to, count):
            copies.append(
                pltpu.make_async_copy(
                    source.at[pl.ds(at * blocks, count * blocks)],
                    target.at[pl.ds(to * blocks, count * blocks)],
                    sems.at[1 + len(copies)],
                )
            )
            copies[-1].start()

        def iso_ready():
            out(iso, 1, iso_three, 0, 3)
            out(iso, 0, local, 0, 3)

        level = bond_body(basis, kept, theta, matrix, proj, work, iso, left, gates, iso_ready)
        out(left, 1, left_three, 0, 3)
        out(left, 0, local, 3, 3)
        weights = get_split(local, rest + W_ROW)
        for ref in (iso, iso_three, local):
            ref[small(ref) :, :] = jnp.zeros((SMALL, blocks), BF16)
            put_split(ref, small(ref), weights)
            put_split(ref, small(ref) + LEVEL_ROW, level)
        for copy in copies:
            copy.wait()


def as_column(row):
    return jnp.broadcast_to(row, (128, row.shape[1])).T


def second_kernel(
    local, iso_1, iso_2, left_0, left_1, left_2,
    mid, last, first, whole,
    scaled, theta, basis, matrix, proj, work, gate_stage, gates, sems, iso, left, columns,
):
    x = lax.axis_index("loop") % 2
    c = lax.axis_index("inner") % 2
    blocks = scaled.shape[-1]
    rest = 6 * blocks
    near = left_0.shape[0] // blocks - 3

    def small(ref):
        return ref.shape[0] - SMALL

    @pl.when(x != c)
    def _():
        kept = local[rest + K_ROW : rest + K_ROW + 1, 0:1].astype(F32)
        gates_copy = load_gates(local[rest : rest + 16, 0:128], gate_stage, gates, sems.at[0])
        here = [(local, 0), (iso_1, 1), (iso_1, 2), (iso_2, 2)]
        products(
            [(iso_1, 0), (iso_2, 0), (iso_2, 1)] + here + [(local, 1), (local, 2), (iso_1, 3)],
            [(left_0, near + n) for n in range(3)]
            + [(left_1, n) for n in range(4)]
            + [(left_2, n) for n in range(3)],
            [
                get_split(iso_1, small(iso_1)),
                get_split(local, rest + W_ROW),
                get_split(local, rest + SMALL + W_ROW),
            ],
            scaled,
            theta,
            basis,
        )
        levels = [get_split(ref, small(ref) + LEVEL_ROW) for ref in (local, iso_1, iso_2)]
        for n, value in enumerate(levels):
            columns[n * blocks : (n + 1) * blocks, :] = as_column(value)
        gates_copy.wait()
        level = bond_body(
            basis, kept, theta, matrix, proj, work, iso, left, gates, lambda: None
        )
        column = jnp.concatenate([as_column(level)] * 2, axis=1)
        for ref, lo, hi in ((last, 3, 4), (mid, 1, 3), (first, 0, 1)):
            for p in range(lo, hi):
                value = iso[p * blocks : (p + 1) * blocks, :].astype(F32) * column
                ref[(p - lo) * blocks : (p - lo + 1) * blocks, :] = value.astype(BF16)
        scales = [
            jnp.concatenate([columns[n * blocks : (n + 1) * blocks, :]] * 2, axis=1)
            for n in range(3)
        ]
        for p in range(4):
            rows = slice(p * blocks, (p + 1) * blocks)
            whole[rows, :] = (left[rows, :].astype(F32) * scales[CHARGE[p]]).astype(BF16)
        for ref, value in ((first, levels[0]), (whole, level)):
            ref[small(ref) :, :] = jnp.zeros((SMALL, blocks), BF16)
            put_split(ref, small(ref) + LEVEL_ROW, value)


def place(plan, out, sems):
    blocks = out.shape[-1]
    half = blocks // 2
    copies = []
    for source, to, count in plan:
        for n in range(2 * count):
            copies.append(
                pltpu.make_async_copy(
                    source.at[pl.ds(n * half, half)],
                    out.at[pl.ds(to * blocks + n * half, half)],
                    sems.at[len(copies)],
                )
            )
            copies[-1].start()
    return copies


def assemble(
    first_mine, first, mid, last, whole_mine, whole, level_mine, level_far, out, weights, sems
):
    x = lax.axis_index("loop") % 2
    c = lax.axis_index("inner") % 2
    even = [(mid, 1, 2), (last, 3, 1)]
    for role, core, plan, level in (
        (0, 0, [(first, 0, 1)] + even, level_far),
        (0, 1, [(first_mine, 0, 1)] + even, level_mine),
        (1, 0, [(whole_mine, 0, 4)], whole_mine),
        (1, 1, [(whole, 0, 4)], whole),
    ):

        @pl.when(jnp.logical_and(x == role, c == core))
        def _(plan=plan, level=level):
            copies = place(plan, out, sems)
            weights[...] = get_split(level, level.shape[0] - SMALL + LEVEL_ROW)
            for copy in copies:
                copy.wait()


def scratch(blocks):
    return [
        pltpu.VMEM((10 * blocks, blocks), BF16),
        pltpu.VMEM((SLOT_COUNT * blocks, blocks), BF16),
        pltpu.VMEM((blocks, 4 * blocks), BF16),
        pltpu.VMEM((4 * blocks, 4 * blocks), BF16),
        pltpu.VMEM((3 * blocks, 4 * blocks), BF16),
        pltpu.VMEM((blocks, 2 * blocks), F32),
        pltpu.VMEM((16, 128), F32),
        pltpu.SMEM((16, 128), F32),
        pltpu.SemaphoreType.DMA((5,)),
    ]


def vmem():
    return pl.BlockSpec(memory_space=pltpu.VMEM)


def hbm():
    return pl.BlockSpec(memory_space=pl.ANY)


def params():
    return pltpu.CompilerParams(vmem_limit_bytes=VMEM_BYTES)


def per_device(loops, inners, site_blocks, bond_weights, bond_gates, kept_slots):
    blocks = site_blocks.shape[-1]

    def rows(count, small=0):
        return jax.ShapeDtypeStruct((count * blocks + small, blocks), BF16)

    def send(value, where):
        route = []
        for l in range(loops):
            for i in range(inners):
                source = where(l, i)
                if source is not None:
                    sl, si = source
                    route.append(((sl % loops) * inners + si % inners, l * inners + i))
        return lax.ppermute(value, AXES, route)

    def to_first(even, odd):
        return lambda l, i: (even, odd)[l % 2](l, i // 2) if i % 2 == l % 2 else None

    def to_second(where):
        return lambda l, i: where(l, i // 2) if i % 2 != l % 2 else None

    full, head, tail = pl.pallas_call(
        prepare,
        out_shape=(rows(4, SMALL), rows(3, SMALL), rows(3, SMALL)),
        in_specs=[vmem()] * 4,
        out_specs=(hbm(),) * 3,
        scratch_shapes=[pltpu.VMEM((SMALL, blocks), BF16), pltpu.SemaphoreType.DMA((6,))],
        compiler_params=params(),
        name="prepare",
    )(site_blocks.reshape(4 * blocks, blocks), bond_weights[0], bond_gates[0], kept_slots)

    next_full = send(
        full, to_first(lambda l, k: (l + 1, 2 * k + 2), lambda l, k: (l - 1, 2 * k - 1))
    )
    here_full = send(full, to_first(lambda l, k: (l, 2 * k + 1), lambda l, k: (l - 1, 2 * k)))
    next_tail = send(tail, to_first(lambda l, k: (l, 2 * k + 2), lambda l, k: (l, 2 * k + 2)))
    after_tail = send(
        tail, to_first(lambda l, k: (l + 1, 2 * k + 3), lambda l, k: (l - 1, 2 * k + 1))
    )
    here_head = send(head, to_first(lambda l, k: (l + 1, 2 * k + 1), lambda l, k: (l, 2 * k)))

    iso_msg, iso_three, left_msg, left_three, local = pl.pallas_call(
        first_kernel,
        out_shape=(rows(4, SMALL), rows(3, SMALL), rows(4), rows(3), rows(6, 3 * SMALL)),
        in_specs=[vmem()] * 6,
        out_specs=(vmem(),) * 5,
        scratch_shapes=scratch(blocks),
        compiler_params=params(),
        name="first_bond",
    )(full, here_full, next_full, here_head, after_tail, next_tail)

    def worker(l, k, d, s):
        sector = 2 * k + 1 - l % 2 + s
        site = 1 - sector % 2
        return (l - l % 2 + 2 * d + site, sector // 2 * 2 + site)

    local_r = send(local, to_second(lambda l, k: worker(l, k, 0, 0)))
    iso_1 = send(iso_msg, to_second(lambda l, k: worker(l, k, 0, -1)))
    iso_2 = send(iso_three, to_second(lambda l, k: worker(l, k, 0, -2)))
    left_1 = send(left_msg, to_second(lambda l, k: worker(l, k, 1, 1)))
    left_2 = send(left_three, to_second(lambda l, k: worker(l, k, 1, 2)))
    if loops == 2:
        left_0 = local_r
    else:
        left_0 = send(left_msg[: 3 * blocks], to_second(lambda l, k: worker(l, k, 1, 0)))

    mid, last, first, whole = pl.pallas_call(
        second_kernel,
        out_shape=(rows(2), rows(1), rows(1, SMALL), rows(4, SMALL)),
        in_specs=[vmem()] * 6,
        out_specs=(vmem(),) * 4,
        scratch_shapes=scratch(blocks)
        + [pltpu.VMEM((4 * blocks, blocks), BF16)] * 2
        + [pltpu.VMEM((3 * blocks, 128), F32)],
        compiler_params=params(),
        name="second_bond",
    )(local_r, iso_1, iso_2, left_0, left_1, left_2)

    def from_second(l, i, d, s):
        sector = i - s
        site = 1 - sector % 2
        return (l - l % 2 - 2 * d + site, sector // 2 * 2 + 1 - site)

    def right_from(s, cores):
        return lambda l, i: from_second(l, i, 1, s) if l % 2 == 0 and i % 2 in cores else None

    first_r = send(first, right_from(0, (0,) if loops == 2 else (0, 1)))
    mid_r = send(mid, right_from(1, (0, 1)))
    last_r = send(last, right_from(2, (0, 1)))
    whole_r = send(whole, lambda l, i: from_second(l, i, 0, 0) if l % 2 and i % 2 else None)
    if loops == 2:
        first_mine, level_far = first, first_r
    else:
        first_mine = first_r
        level_far = send(
            iso_msg[4 * blocks :], lambda l, i: (l + 1, i + 1) if l % 2 == 0 and i % 2 == 0 else None
        )
    sites, weights = pl.pallas_call(
        assemble,
        out_shape=(rows(4), jax.ShapeDtypeStruct((1, blocks), F32)),
        in_specs=[vmem()] * 8,
        out_specs=(hbm(), vmem()),
        scratch_shapes=[pltpu.SemaphoreType.DMA((8,))],
        compiler_params=params(),
        name="assemble",
    )(first_mine, first_r, mid_r, last_r, whole, whole_r, local_r, level_far)
    return sites.reshape(1, 1, 4, blocks, blocks), weights[None]


def solution(mesh):
    return jax.shard_map(
        functools.partial(per_device, mesh.shape["loop"], mesh.shape["inner"]),
        mesh=mesh,
        in_specs=(
            P("loop", "inner", None, None, None),
            P("loop", "inner", None),
            P("loop", None, None),
            P("loop", "inner"),
        ),
        out_specs=(P("loop", "inner", None, None, None), P("loop", "inner", None)),
        check_vma=False,
    )
```

```python
import functools
import math

import jax
import jax.numpy as jnp
import numpy as np
from jax import lax
from jax.experimental import pallas as pl
from jax.experimental.pallas import tpu as pltpu
from jax.sharding import PartitionSpec as P

CHARGE = (0, 1, 1, 2)
AXES = ("loop", "inner")
BF16, F32 = jnp.bfloat16, jnp.float32
VMEM_BYTES = 24 << 20
HIGHEST = lax.Precision.HIGHEST


def gate_terms():
    table = {}
    for a in range(4):
        for b in range(4):
            table[a, b] = [
                (CHARGE[p] - CHARGE[a], p, q)
                for p in range(4)
                for q in range(4)
                if CHARGE[p] + CHARGE[q] == CHARGE[a] + CHARGE[b]
                and abs(CHARGE[p] - CHARGE[a]) <= 1
            ]
    return table


TERMS = gate_terms()
PIECES = {
    (0, 0): (0, 3, 4, 0),
    (0, 1): (4, 3, 4, 0),
    (0, 2): (5, 3, 4, 0),
    (0, 3): (9, 3, 4, 0),
    (-1, 1): (1, 0, 3, 0),
    (-1, 2): (2, 0, 3, 0),
    (-1, 3): (6, 0, 3, 0),
    (1, 0): (3, 7, 3, 1),
    (1, 1): (7, 7, 3, 1),
    (1, 2): (8, 7, 3, 1),
}


def theta_slots():
    slots, count = {}, 0
    for (distance, q), (_, _, rows, first) in PIECES.items():
        for p in range(rows):
            slots[distance, first + p, q] = count
            count += 1
    return slots, count


SLOTS, SLOT_COUNT = theta_slots()


def dot(a, b, dims, precision=None):
    return lax.dot_general(a, b, (dims, ((), ())), precision=precision, preferred_element_type=F32)


def split3(a):
    h = a.astype(BF16)
    r = a - h.astype(F32)
    m = r.astype(BF16)
    return h, m, (r - m.astype(F32)).astype(BF16)


def factor_rows(work, size, panel=32):
    tiles = panel // 8
    sub = lax.broadcasted_iota(jnp.int32, (8, 128), 0)
    for start in range(0, size, panel):
        low = start < size // 2
        chunks = [0, 1, 2] if low else [1, 2, 3]
        base = start % 128
        rows = [
            [work[start + 8 * t : start + 8 * t + 8, 128 * c : 128 * c + 128] for c in chunks]
            for t in range(tiles)
        ]

        def column(k):
            return {
                t: jnp.broadcast_to(rows[t][0][:, base + k : base + k + 1], (8, 128))
                for t in range(k // 8, tiles)
            }

        def at(col, k):
            return jnp.broadcast_to(col[k // 8][k % 8 : k % 8 + 1, :], (8, 128))

        pivots = [jnp.ones((8, 128), F32) for _ in range(tiles)]
        cols = {k: column(k) for k in range(8)}
        for g in range(tiles):
            if g + 1 < tiles:
                cols.update({k: column(k) for k in range(8 * g + 8, 8 * g + 16)})

            def below(col, j):
                return {
                    t: (jnp.where(sub > j % 8, v, 0.0) if t == j // 8 else v)
                    for t, v in col.items()
                    if t >= g
                }

            for j in range(8 * g, 8 * g + 8, 2):
                one, two = cols[j], cols[j + 1]
                a, b, c = at(one, j), at(one, j + 1), at(two, j + 1)
                det = a * c - b * b
                ra, rd = 1.0 / a, 1.0 / det
                first = {t: v * ra for t, v in below(one, j).items()}
                ratio = b * ra
                two = {t: two[t] - one[t] * ratio for t in one if t >= g}
                second = {t: v * (a * rd) for t, v in below(two, j + 1).items()}
                for k in cols:
                    if k > j + 1:
                        e1, e2 = at(one, k), at(two, k)
                        cols[k] = {
                            t: v - (first[t] * e1 + second[t] * e2) for t, v in cols[k].items()
                        }
                for i in range(len(chunks)):
                    r = j % 8
                    x0 = jnp.broadcast_to(rows[g][i][r : r + 1, :], (8, 128))
                    x1 = jnp.broadcast_to(rows[g][i][r + 1 : r + 2, :], (8, 128)) - ratio * x0
                    for t in range(g, tiles):
                        rows[t][i] = rows[t][i] - (first[t] * x0 + second[t] * x1)
                pivots[g] = jnp.where(
                    sub == j % 8, a, jnp.where(sub == j % 8 + 1, det * ra, pivots[g])
                )
        done = []
        for t in range(tiles):
            scale = lax.rsqrt(pivots[t])
            done.append([x * scale for x in rows[t]])
            for c, x in zip(chunks, done[t]):
                work[start + 8 * t : start + 8 * t + 8, 128 * c : 128 * c + 128] = x
        after = start + panel
        if after < size:
            h, m, l = split3(
                jnp.concatenate([jnp.concatenate(xs, axis=1) for xs in done], axis=0)
            )
            right = jnp.concatenate([h, m, h, l, h, m], axis=0)
            left = jnp.concatenate([h, h, m, h, l, m], axis=0)
            first = 128 * chunks[0]
            for lo, hi in ((after, after + panel), (after + panel, size)):
                if lo < hi:
                    update = dot(left[:, lo - first : hi - first], right, ((0,), (0,)))
                    for i, c in enumerate(chunks):
                        work[lo:hi, 128 * c : 128 * c + 128] -= update[:, 128 * i : 128 * i + 128]


SMALL = 32
W_ROW, K_ROW = 16, 19
LEVEL_ROW = 3


def put_split(ref, at, row):
    for n, part in enumerate(split3(row)):
        ref[at + n : at + n + 1, :] = part


def get_split(ref, at):
    h, m, l = (ref[at + n : at + n + 1, :].astype(F32) for n in range(3))
    return (h + m) + l


def prepare(block_ref, weight_ref, gate_ref, kept_ref, full, head, tail, small, sems):
    blocks = block_ref.shape[-1]
    values = jnp.zeros((SMALL, blocks), F32)
    rowid = lax.broadcasted_iota(jnp.int32, (SMALL, blocks), 0)
    for n, part in enumerate(split3(weight_ref[...])):
        values = jnp.where(rowid == W_ROW + n, part.astype(F32), values)
    small[...] = jnp.where(rowid == K_ROW, kept_ref[...].astype(F32), values).astype(BF16)
    small[0:16, 0:16] = gate_ref[...].astype(BF16)
    copies = []
    for n, (ref, at) in enumerate(((full, 0), (tail, blocks), (head, 0))):
        size = ref.shape[0] - SMALL
        copies.append(
            pltpu.make_async_copy(
                block_ref.at[pl.ds(at, size)], ref.at[pl.ds(0, size)], sems.at[n]
            )
        )
        copies.append(
            pltpu.make_async_copy(small, ref.at[pl.ds(size, SMALL)], sems.at[3 + n])
        )
    for copy in copies:
        copy.start()
    for copy in copies:
        copy.wait()


def products(a_blocks, b_blocks, weights, scaled, theta, basis):
    blocks = scaled.shape[-1]

    def block(place):
        ref, n = place
        return ref[n * blocks : (n + 1) * blocks, :]

    for n, place in enumerate(a_blocks):
        w = weights[0 if n < 3 else 1 if n < 7 else 2]
        scaled[n * blocks : (n + 1) * blocks, :] = (block(place).astype(F32) * w).astype(BF16)
    for n in range(4):
        basis[:, n * blocks : (n + 1) * blocks] = block(a_blocks[3 + n]).T
    for (distance, q), (right, first_row, count, first) in PIECES.items():
        product = dot(
            scaled[first_row * blocks : (first_row + count) * blocks, :],
            block(b_blocks[right]),
            ((1,), (0,)),
        )
        slot = SLOTS[distance, first, q]
        theta[slot * blocks : (slot + count) * blocks, :] = (
            product * (1.0 / math.sqrt(blocks))
        ).astype(BF16)


def load_gates(gate_rows, gate_stage, gates, sem):
    gate_stage[...] = gate_rows.astype(F32)
    copy = pltpu.make_async_copy(gate_stage, gates, sem)
    copy.start()
    return copy


def bond_body(basis, kept, theta, matrix, proj, work, iso, left, gates, iso_ready):
    blocks = theta.shape[-1]

    def gate(a, b, p, q):
        return gates[4 * a + b, 4 * p + q]

    step = 16

    @pl.loop(0, blocks // step)
    def mix(chunk):
        at = pl.multiple_of(chunk * step, step)
        for half in range(blocks // 128):
            cut = slice(128 * half, 128 * half + 128)
            held = {}

            def term(distance, p, q):
                slot = SLOTS[distance, p, q]
                if slot not in held:
                    place = pl.ds(pl.multiple_of(slot * blocks + at, step), step)
                    held[slot] = theta[place, cut].astype(F32)
                return held[slot]

            for total in range(5):
                for a in range(4):
                    for b in range(4):
                        if CHARGE[a] + CHARGE[b] != total:
                            continue
                        value = None
                        for distance, p, q in TERMS[a, b]:
                            part = gate(a, b, p, q) * term(distance, p, q)
                            value = part if value is None else value + part
                        matrix[
                            pl.ds(pl.multiple_of(a * blocks + at, step), step),
                            b * blocks + 128 * half : b * blocks + 128 * half + 128,
                        ] = value.astype(BF16)
                held.clear()

    projected = dot(basis[...], matrix[...], ((1,), (0,)))
    slot_id = lax.broadcasted_iota(jnp.int32, projected.shape, 0).astype(F32)
    h, m, l = split3(jnp.where(slot_id < kept, projected, 0.0))
    for n, part in enumerate((h, m, l)):
        proj[n * blocks : (n + 1) * blocks, :] = part
    ri = lax.broadcasted_iota(jnp.int32, (blocks, blocks), 0)
    ci = lax.broadcasted_iota(jnp.int32, (blocks, blocks), 1)
    eye = jnp.where(ri == ci, 1.0, 0.0).astype(F32)
    outer = ((1,), (1,))
    mixed = dot(h, m, outer) + dot(h, l, outer)
    work[:, :blocks] = (dot(h, h, outer) + dot(m, m, outer)) + (mixed + mixed.T) + eye
    work[:, blocks:] = eye
    factor_rows(work, blocks)
    wh, wm, wl = split3(work[:, blocks:])
    h, m, l = (proj[n * blocks : (n + 1) * blocks, :] for n in range(3))
    inner = ((1,), (0,))
    ortho = (
        dot(jnp.concatenate([wh, wm, wl], axis=1), jnp.concatenate([h, h, h], axis=0), inner)
        + dot(jnp.concatenate([wh, wm], axis=1), jnp.concatenate([m, m], axis=0), inner)
        + dot(wh, l, inner)
    )
    ortho = (ortho * math.sqrt(4 * blocks)).astype(BF16)
    for p in range(4):
        iso[p * blocks : (p + 1) * blocks, :] = ortho[:, p * blocks : (p + 1) * blocks]
    iso_ready()
    flipped = ortho.T
    parts, total = [], 0.0
    for p in range(4):
        rows = matrix[p * blocks : (p + 1) * blocks, :]
        parts.append(dot(rows, flipped, inner) * (1.0 / math.sqrt(4 * blocks)))
        total = total + jnp.sum(parts[p] * parts[p], axis=0, keepdims=True)
    level = jnp.sqrt(total * (1.0 / (4 * blocks)) + 1e-06)
    scale = 1.0 / level
    for p in range(4):
        left[p * blocks : (p + 1) * blocks, :] = (parts[p] * scale).astype(BF16)
    return level


def first_kernel(
    own, here_full, next_full, here_head, after_tail, next_tail,
    iso, iso_three, left, left_three, local,
    scaled, theta, basis, matrix, proj, work, gate_stage, gates, sems,
):
    x = lax.axis_index("loop") % 2
    c = lax.axis_index("inner") % 2
    blocks = scaled.shape[-1]

    def small(ref):
        return ref.shape[0] - SMALL

    def span(ref, count):
        return [(ref, n) for n in range(count)]

    @pl.when(x == c)
    def _():
        base = small(here_full)
        kept = here_full[base + K_ROW : base + K_ROW + 1, 0:1].astype(F32)
        gates_copy = load_gates(here_full[base : base + 16, 0:128], gate_stage, gates, sems.at[0])
        rest = 6 * blocks
        for role, (one, two, three, four) in enumerate(
            ((own, next_full, next_tail, after_tail), (next_full, own, after_tail, next_tail))
        ):

            @pl.when(x == role)
            def _(one=one, two=two, three=three, four=four):
                products(
                    span(one, 3) + span(here_full, 4) + span(three, 3),
                    span(here_head, 3) + span(two, 4) + span(four, 3),
                    [get_split(ref, small(ref) + W_ROW) for ref in (one, here_full, three)],
                    scaled,
                    theta,
                    basis,
                )
                for n, ref in enumerate((here_head, two)):
                    local[rest + n * SMALL : rest + (n + 1) * SMALL, :] = ref[small(ref) :, :]

        gates_copy.wait()
        copies = []

        def out(source, at, target, to, count):
            copies.append(
                pltpu.make_async_copy(
                    source.at[pl.ds(at * blocks, count * blocks)],
                    target.at[pl.ds(to * blocks, count * blocks)],
                    sems.at[1 + len(copies)],
                )
            )
            copies[-1].start()

        def iso_ready():
            out(iso, 1, iso_three, 0, 3)
            out(iso, 0, local, 0, 3)

        level = bond_body(basis, kept, theta, matrix, proj, work, iso, left, gates, iso_ready)
        out(left, 1, left_three, 0, 3)
        out(left, 0, local, 3, 3)
        weights = get_split(local, rest + W_ROW)
        for ref in (iso, iso_three, local):
            ref[small(ref) :, :] = jnp.zeros((SMALL, blocks), BF16)
            put_split(ref, small(ref), weights)
            put_split(ref, small(ref) + LEVEL_ROW, level)
        for copy in copies:
            copy.wait()


def as_column(row):
    return jnp.broadcast_to(row, (128, row.shape[1])).T


def second_kernel(
    local, iso_1, iso_2, left_0, left_1, left_2,
    mid, last, three, whole,
    scaled, theta, basis, matrix, proj, work, gate_stage, gates, sems, iso, left, columns,
):
    x = lax.axis_index("loop") % 2
    c = lax.axis_index("inner") % 2
    blocks = scaled.shape[-1]
    rest = 6 * blocks
    near = left_0.shape[0] // blocks - 3

    def small(ref):
        return ref.shape[0] - SMALL

    @pl.when(x != c)
    def _():
        kept = local[rest + K_ROW : rest + K_ROW + 1, 0:1].astype(F32)
        gates_copy = load_gates(local[rest : rest + 16, 0:128], gate_stage, gates, sems.at[0])
        here = [(local, 0), (iso_1, 1), (iso_1, 2), (iso_2, 2)]
        products(
            [(iso_1, 0), (iso_2, 0), (iso_2, 1)] + here + [(local, 1), (local, 2), (iso_1, 3)],
            [(left_0, near + n) for n in range(3)]
            + [(left_1, n) for n in range(4)]
            + [(left_2, n) for n in range(3)],
            [
                get_split(iso_1, small(iso_1)),
                get_split(local, rest + W_ROW),
                get_split(local, rest + SMALL + W_ROW),
            ],
            scaled,
            theta,
            basis,
        )
        levels = [get_split(ref, small(ref) + LEVEL_ROW) for ref in (local, iso_1, iso_2)]
        for n, value in enumerate(levels):
            columns[n * blocks : (n + 1) * blocks, :] = as_column(value)
        gates_copy.wait()
        level = bond_body(
            basis, kept, theta, matrix, proj, work, iso, left, gates, lambda: None
        )
        column = jnp.concatenate([as_column(level)] * 2, axis=1)
        for p in range(4):
            value = iso[p * blocks : (p + 1) * blocks, :].astype(F32) * column
            value = value.astype(BF16)
            for ref, lo, hi in ((last, 3, 4), (mid, 1, 3), (three, 0, 3)):
                if lo <= p < hi:
                    ref[(p - lo) * blocks : (p - lo + 1) * blocks, :] = value
        scales = [
            jnp.concatenate([columns[n * blocks : (n + 1) * blocks, :]] * 2, axis=1)
            for n in range(3)
        ]
        for p in range(4):
            rows = slice(p * blocks, (p + 1) * blocks)
            whole[rows, :] = (left[rows, :].astype(F32) * scales[CHARGE[p]]).astype(BF16)
        for ref, value in ((three, levels[0]), (whole, level)):
            ref[small(ref) :, :] = jnp.zeros((SMALL, blocks), BF16)
            put_split(ref, small(ref) + LEVEL_ROW, value)


def place(plan, out, sems):
    blocks = out.shape[-1]
    half = blocks // 2
    copies = []
    for source, at, to, count in plan:
        for n in range(2 * count):
            copies.append(
                pltpu.make_async_copy(
                    source.at[pl.ds(at * blocks + n * half, half)],
                    out.at[pl.ds(to * blocks + n * half, half)],
                    sems.at[len(copies)],
                )
            )
            copies[-1].start()
    return copies


def assemble(
    three_mine, three, mid, handed, last, whole_mine, whole, level_mine, level_far, out, weights, sems
):
    x = lax.axis_index("loop") % 2
    c = lax.axis_index("inner") % 2
    for role, core, plan, level in (
        (0, 0, [(three, 0, 0, 1), (mid, 0, 1, 2), (last, 0, 3, 1)], level_far),
        (0, 1, [(three_mine, 0, 0, 1), (handed, 1, 1, 2), (last, 0, 3, 1)], level_mine),
        (1, 0, [(whole_mine, 0, 0, 4)], whole_mine),
        (1, 1, [(whole, 0, 0, 4)], whole),
    ):

        @pl.when(jnp.logical_and(x == role, c == core))
        def _(plan=plan, level=level):
            copies = place(plan, out, sems)
            weights[...] = get_split(level, level.shape[0] - SMALL + LEVEL_ROW)
            for copy in copies:
                copy.wait()


def scratch(blocks):
    return [
        pltpu.VMEM((10 * blocks, blocks), BF16),
        pltpu.VMEM((SLOT_COUNT * blocks, blocks), BF16),
        pltpu.VMEM((blocks, 4 * blocks), BF16),
        pltpu.VMEM((4 * blocks, 4 * blocks), BF16),
        pltpu.VMEM((3 * blocks, 4 * blocks), BF16),
        pltpu.VMEM((blocks, 2 * blocks), F32),
        pltpu.VMEM((16, 128), F32),
        pltpu.SMEM((16, 128), F32),
        pltpu.SemaphoreType.DMA((5,)),
    ]


def vmem():
    return pl.BlockSpec(memory_space=pltpu.VMEM)


def hbm():
    return pl.BlockSpec(memory_space=pl.ANY)


def params():
    return pltpu.CompilerParams(vmem_limit_bytes=VMEM_BYTES)


def per_device(loops, inners, site_blocks, bond_weights, bond_gates, kept_slots):
    blocks = site_blocks.shape[-1]

    def rows(count, small=0):
        return jax.ShapeDtypeStruct((count * blocks + small, blocks), BF16)

    def send(value, where):
        route = []
        for l in range(loops):
            for i in range(inners):
                source = where(l, i)
                if source is not None:
                    sl, si = source
                    route.append(((sl % loops) * inners + si % inners, l * inners + i))
        return lax.ppermute(value, AXES, route)

    def to_first(even, odd):
        return lambda l, i: (even, odd)[l % 2](l, i // 2) if i % 2 == l % 2 else None

    def to_second(where):
        return lambda l, i: where(l, i // 2) if i % 2 != l % 2 else None

    full, head, tail = pl.pallas_call(
        prepare,
        out_shape=(rows(4, SMALL), rows(3, SMALL), rows(3, SMALL)),
        in_specs=[vmem()] * 4,
        out_specs=(hbm(),) * 3,
        scratch_shapes=[pltpu.VMEM((SMALL, blocks), BF16), pltpu.SemaphoreType.DMA((6,))],
        compiler_params=params(),
        name="prepare",
    )(site_blocks.reshape(4 * blocks, blocks), bond_weights[0], bond_gates[0], kept_slots)

    next_full = send(
        full, to_first(lambda l, k: (l + 1, 2 * k + 2), lambda l, k: (l - 1, 2 * k - 1))
    )
    here_full = send(full, to_first(lambda l, k: (l, 2 * k + 1), lambda l, k: (l - 1, 2 * k)))
    next_tail = send(tail, to_first(lambda l, k: (l, 2 * k + 2), lambda l, k: (l, 2 * k + 2)))
    after_tail = send(
        tail, to_first(lambda l, k: (l + 1, 2 * k + 3), lambda l, k: (l - 1, 2 * k + 1))
    )
    here_head = send(head, to_first(lambda l, k: (l + 1, 2 * k + 1), lambda l, k: (l, 2 * k)))

    iso_msg, iso_three, left_msg, left_three, local = pl.pallas_call(
        first_kernel,
        out_shape=(rows(4, SMALL), rows(3, SMALL), rows(4), rows(3), rows(6, 3 * SMALL)),
        in_specs=[vmem()] * 6,
        out_specs=(vmem(),) * 5,
        scratch_shapes=scratch(blocks),
        compiler_params=params(),
        name="first_bond",
    )(full, here_full, next_full, here_head, after_tail, next_tail)

    def worker(l, k, d, s):
        sector = 2 * k + 1 - l % 2 + s
        site = 1 - sector % 2
        return (l - l % 2 + 2 * d + site, sector // 2 * 2 + site)

    local_r = send(local, to_second(lambda l, k: worker(l, k, 0, 0)))
    iso_1 = send(iso_msg, to_second(lambda l, k: worker(l, k, 0, -1)))
    iso_2 = send(iso_three, to_second(lambda l, k: worker(l, k, 0, -2)))
    left_1 = send(left_msg, to_second(lambda l, k: worker(l, k, 1, 1)))
    left_2 = send(left_three, to_second(lambda l, k: worker(l, k, 1, 2)))
    if loops == 2:
        left_0 = local_r
    else:
        left_0 = send(left_msg[: 3 * blocks], to_second(lambda l, k: worker(l, k, 1, 0)))

    mid, last, three, whole = pl.pallas_call(
        second_kernel,
        out_shape=(rows(2), rows(1), rows(3, SMALL), rows(4, SMALL)),
        in_specs=[vmem()] * 6,
        out_specs=(vmem(),) * 4,
        scratch_shapes=scratch(blocks)
        + [pltpu.VMEM((4 * blocks, blocks), BF16)] * 2
        + [pltpu.VMEM((3 * blocks, 128), F32)],
        compiler_params=params(),
        name="second_bond",
    )(local_r, iso_1, iso_2, left_0, left_1, left_2)

    def from_second(l, i, d, s):
        sector = i - s
        site = 1 - sector % 2
        return (l - l % 2 - 2 * d + site, sector // 2 * 2 + 1 - site)

    def right_from(s, cores):
        return lambda l, i: from_second(l, i, 1, s) if l % 2 == 0 and i % 2 in cores else None

    three_r = send(three, right_from(0, (0,)))
    mid_r = send(mid, right_from(1, (0,)))
    last_r = send(last, right_from(2, (0, 1)))
    whole_r = send(whole, lambda l, i: from_second(l, i, 0, 0) if l % 2 and i % 2 else None)
    handed = send(three_r, lambda l, i: (l, i - 1) if l % 2 == 0 and i % 2 else None)
    if loops == 2:
        three_mine, level_far = three, three_r
    else:
        three_mine = send(three, right_from(0, (1,)))
        level_far = send(
            iso_msg[4 * blocks :], lambda l, i: (l + 1, i + 1) if l % 2 == 0 and i % 2 == 0 else None
        )
    sites, weights = pl.pallas_call(
        assemble,
        out_shape=(rows(4), jax.ShapeDtypeStruct((1, blocks), F32)),
        in_specs=[vmem()] * 9,
        out_specs=(hbm(), vmem()),
        scratch_shapes=[pltpu.SemaphoreType.DMA((8,))],
        compiler_params=params(),
        name="assemble",
    )(three_mine, three_r, mid_r, handed, last_r, whole, whole_r, local_r, level_far)
    return sites.reshape(1, 1, 4, blocks, blocks), weights[None]


def solution(mesh):
    return jax.shard_map(
        functools.partial(per_device, mesh.shape["loop"], mesh.shape["inner"]),
        mesh=mesh,
        in_specs=(
            P("loop", "inner", None, None, None),
            P("loop", "inner", None),
            P("loop", None, None),
            P("loop", "inner"),
        ),
        out_specs=(P("loop", "inner", None, None, None), P("loop", "inner", None)),
        check_vma=False,
    )
```

```python
import functools
import math

import jax
import jax.numpy as jnp
import numpy as np
from jax import lax
from jax.experimental import pallas as pl
from jax.experimental.pallas import tpu as pltpu
from jax.sharding import PartitionSpec as P

CHARGE = (0, 1, 1, 2)
AXES = ("loop", "inner")
BF16, F32 = jnp.bfloat16, jnp.float32
VMEM_BYTES = 24 << 20
HIGHEST = lax.Precision.HIGHEST


def gate_terms():
    table = {}
    for a in range(4):
        for b in range(4):
            table[a, b] = [
                (CHARGE[p] - CHARGE[a], p, q)
                for p in range(4)
                for q in range(4)
                if CHARGE[p] + CHARGE[q] == CHARGE[a] + CHARGE[b]
                and abs(CHARGE[p] - CHARGE[a]) <= 1
            ]
    return table


TERMS = gate_terms()
PIECES = {
    (0, 0): (0, 3, 4, 0),
    (0, 1): (4, 3, 4, 0),
    (0, 2): (5, 3, 4, 0),
    (0, 3): (9, 3, 4, 0),
    (-1, 1): (1, 0, 3, 0),
    (-1, 2): (2, 0, 3, 0),
    (-1, 3): (6, 0, 3, 0),
    (1, 0): (3, 7, 3, 1),
    (1, 1): (7, 7, 3, 1),
    (1, 2): (8, 7, 3, 1),
}


def theta_slots():
    slots, count = {}, 0
    for (distance, q), (_, _, rows, first) in PIECES.items():
        for p in range(rows):
            slots[distance, first + p, q] = count
            count += 1
    return slots, count


SLOTS, SLOT_COUNT = theta_slots()


def dot(a, b, dims, precision=None):
    return lax.dot_general(a, b, (dims, ((), ())), precision=precision, preferred_element_type=F32)


def split3(a):
    h = a.astype(BF16)
    r = a - h.astype(F32)
    m = r.astype(BF16)
    return h, m, (r - m.astype(F32)).astype(BF16)


def factor_rows(work, size, panel=32):
    tiles = panel // 8
    sub = lax.broadcasted_iota(jnp.int32, (8, 128), 0)
    for start in range(0, size, panel):
        low = start < size // 2
        chunks = [0, 1, 2] if low else [1, 2, 3]
        base = start % 128
        rows = [
            [work[start + 8 * t : start + 8 * t + 8, 128 * c : 128 * c + 128] for c in chunks]
            for t in range(tiles)
        ]

        def column(k):
            return {
                t: jnp.broadcast_to(rows[t][0][:, base + k : base + k + 1], (8, 128))
                for t in range(k // 8, tiles)
            }

        def at(col, k):
            return jnp.broadcast_to(col[k // 8][k % 8 : k % 8 + 1, :], (8, 128))

        pivots = [jnp.ones((8, 128), F32) for _ in range(tiles)]
        cols = {k: column(k) for k in range(8)}
        for g in range(tiles):
            if g + 1 < tiles:
                cols.update({k: column(k) for k in range(8 * g + 8, 8 * g + 16)})

            def below(col, j):
                return {
                    t: (jnp.where(sub > j % 8, v, 0.0) if t == j // 8 else v)
                    for t, v in col.items()
                    if t >= g
                }

            for j in range(8 * g, 8 * g + 8, 2):
                one, two = cols[j], cols[j + 1]
                a, b, c = at(one, j), at(one, j + 1), at(two, j + 1)
                det = a * c - b * b
                ra, rd = 1.0 / a, 1.0 / det
                first = {t: v * ra for t, v in below(one, j).items()}
                ratio = b * ra
                two = {t: two[t] - one[t] * ratio for t in one if t >= g}
                second = {t: v * (a * rd) for t, v in below(two, j + 1).items()}
                for k in cols:
                    if k > j + 1:
                        e1, e2 = at(one, k), at(two, k)
                        cols[k] = {
                            t: v - (first[t] * e1 + second[t] * e2) for t, v in cols[k].items()
                        }
                for i in range(len(chunks)):
                    r = j % 8
                    x0 = jnp.broadcast_to(rows[g][i][r : r + 1, :], (8, 128))
                    x1 = jnp.broadcast_to(rows[g][i][r + 1 : r + 2, :], (8, 128)) - ratio * x0
                    for t in range(g, tiles):
                        rows[t][i] = rows[t][i] - (first[t] * x0 + second[t] * x1)
                pivots[g] = jnp.where(
                    sub == j % 8, a, jnp.where(sub == j % 8 + 1, det * ra, pivots[g])
                )
        done = []
        for t in range(tiles):
            scale = lax.rsqrt(pivots[t])
            done.append([x * scale for x in rows[t]])
            for c, x in zip(chunks, done[t]):
                work[start + 8 * t : start + 8 * t + 8, 128 * c : 128 * c + 128] = x
        after = start + panel
        if after < size:
            h, m, l = split3(
                jnp.concatenate([jnp.concatenate(xs, axis=1) for xs in done], axis=0)
            )
            right = jnp.concatenate([h, m, h, l, h, m], axis=0)
            left = jnp.concatenate([h, h, m, h, l, m], axis=0)
            first = 128 * chunks[0]
            for lo, hi in ((after, after + panel), (after + panel, size)):
                if lo < hi:
                    update = dot(left[:, lo - first : hi - first], right, ((0,), (0,)))
                    for i, c in enumerate(chunks):
                        work[lo:hi, 128 * c : 128 * c + 128] -= update[:, 128 * i : 128 * i + 128]


SMALL = 32
W_ROW, K_ROW = 16, 19
LEVEL_ROW = 3


def put_split(ref, at, row):
    for n, part in enumerate(split3(row)):
        ref[at + n : at + n + 1, :] = part


def get_split(ref, at):
    h, m, l = (ref[at + n : at + n + 1, :].astype(F32) for n in range(3))
    return (h + m) + l


def prepare(block_ref, weight_ref, gate_ref, kept_ref, full, head, tail, small, sems):
    blocks = block_ref.shape[-1]
    values = jnp.zeros((SMALL, blocks), F32)
    rowid = lax.broadcasted_iota(jnp.int32, (SMALL, blocks), 0)
    for n, part in enumerate(split3(weight_ref[...])):
        values = jnp.where(rowid == W_ROW + n, part.astype(F32), values)
    small[...] = jnp.where(rowid == K_ROW, kept_ref[...].astype(F32), values).astype(BF16)
    small[0:16, 0:16] = gate_ref[...].astype(BF16)
    copies = []
    for n, (ref, at) in enumerate(((full, 0), (tail, blocks), (head, 0))):
        size = ref.shape[0] - SMALL
        copies.append(
            pltpu.make_async_copy(
                block_ref.at[pl.ds(at, size)], ref.at[pl.ds(0, size)], sems.at[n]
            )
        )
        copies.append(
            pltpu.make_async_copy(small, ref.at[pl.ds(size, SMALL)], sems.at[3 + n])
        )
    for copy in copies:
        copy.start()
    for copy in copies:
        copy.wait()


def products(a_blocks, b_blocks, weights, scaled, theta, basis):
    blocks = scaled.shape[-1]

    def block(place):
        ref, n = place
        return ref[n * blocks : (n + 1) * blocks, :]

    for n, place in enumerate(a_blocks):
        w = weights[0 if n < 3 else 1 if n < 7 else 2]
        scaled[n * blocks : (n + 1) * blocks, :] = (block(place).astype(F32) * w).astype(BF16)
    for n in range(4):
        basis[:, n * blocks : (n + 1) * blocks] = block(a_blocks[3 + n]).T
    for (distance, q), (right, first_row, count, first) in PIECES.items():
        product = dot(
            scaled[first_row * blocks : (first_row + count) * blocks, :],
            block(b_blocks[right]),
            ((1,), (0,)),
        )
        slot = SLOTS[distance, first, q]
        theta[slot * blocks : (slot + count) * blocks, :] = (
            product * (1.0 / math.sqrt(blocks))
        ).astype(BF16)


def load_gates(gate_rows, gate_stage, gates, sem):
    gate_stage[...] = gate_rows.astype(F32)
    copy = pltpu.make_async_copy(gate_stage, gates, sem)
    copy.start()
    return copy


def bond_body(basis, kept, theta, matrix, proj, work, iso, put_left, gates, iso_ready):
    blocks = theta.shape[-1]

    def gate(a, b, p, q):
        return gates[4 * a + b, 4 * p + q]

    step = 16

    @pl.loop(0, blocks // step)
    def mix(chunk):
        at = pl.multiple_of(chunk * step, step)
        for half in range(blocks // 128):
            cut = slice(128 * half, 128 * half + 128)
            held = {}

            def term(distance, p, q):
                slot = SLOTS[distance, p, q]
                if slot not in held:
                    place = pl.ds(pl.multiple_of(slot * blocks + at, step), step)
                    held[slot] = theta[place, cut].astype(F32)
                return held[slot]

            for total in range(5):
                for a in range(4):
                    for b in range(4):
                        if CHARGE[a] + CHARGE[b] != total:
                            continue
                        value = None
                        for distance, p, q in TERMS[a, b]:
                            part = gate(a, b, p, q) * term(distance, p, q)
                            value = part if value is None else value + part
                        matrix[
                            pl.ds(pl.multiple_of(a * blocks + at, step), step),
                            b * blocks + 128 * half : b * blocks + 128 * half + 128,
                        ] = value.astype(BF16)
                held.clear()

    projected = dot(basis[...], matrix[...], ((1,), (0,)))
    slot_id = lax.broadcasted_iota(jnp.int32, projected.shape, 0).astype(F32)
    h, m, l = split3(jnp.where(slot_id < kept, projected, 0.0))
    for n, part in enumerate((h, m, l)):
        proj[n * blocks : (n + 1) * blocks, :] = part
    ri = lax.broadcasted_iota(jnp.int32, (blocks, blocks), 0)
    ci = lax.broadcasted_iota(jnp.int32, (blocks, blocks), 1)
    eye = jnp.where(ri == ci, 1.0, 0.0).astype(F32)
    outer = ((1,), (1,))
    mixed = dot(h, m, outer) + dot(h, l, outer)
    work[:, :blocks] = (dot(h, h, outer) + dot(m, m, outer)) + (mixed + mixed.T) + eye
    work[:, blocks:] = eye
    factor_rows(work, blocks)
    wh, wm, wl = split3(work[:, blocks:])
    h, m, l = (proj[n * blocks : (n + 1) * blocks, :] for n in range(3))
    inner = ((1,), (0,))
    ortho = (
        dot(jnp.concatenate([wh, wm, wl], axis=1), jnp.concatenate([h, h, h], axis=0), inner)
        + dot(jnp.concatenate([wh, wm], axis=1), jnp.concatenate([m, m], axis=0), inner)
        + dot(wh, l, inner)
    )
    ortho = (ortho * math.sqrt(4 * blocks)).astype(BF16)
    for p in range(4):
        iso[p * blocks : (p + 1) * blocks, :] = ortho[:, p * blocks : (p + 1) * blocks]
    iso_ready()
    flipped = ortho.T
    parts, total = [], 0.0
    for p in range(4):
        rows = matrix[p * blocks : (p + 1) * blocks, :]
        parts.append(dot(rows, flipped, inner) * (1.0 / math.sqrt(4 * blocks)))
        total = total + jnp.sum(parts[p] * parts[p], axis=0, keepdims=True)
    level = jnp.sqrt(total * (1.0 / (4 * blocks)) + 1e-06)
    scale = 1.0 / level
    for p in range(4):
        put_left(p, (parts[p] * scale).astype(BF16))
    return level


def first_kernel(
    own, here_full, next_full, here_head, after_tail, next_tail,
    iso, iso_three, left, left_three, local,
    scaled, theta, basis, matrix, proj, work, gate_stage, gates, sems,
):
    x = lax.axis_index("loop") % 2
    c = lax.axis_index("inner") % 2
    blocks = scaled.shape[-1]

    def small(ref):
        return ref.shape[0] - SMALL

    def span(ref, count):
        return [(ref, n) for n in range(count)]

    @pl.when(x == c)
    def _():
        base = small(here_full)
        kept = here_full[base + K_ROW : base + K_ROW + 1, 0:1].astype(F32)
        gates_copy = load_gates(here_full[base : base + 16, 0:128], gate_stage, gates, sems.at[0])
        rest = 6 * blocks
        for role, (one, two, three, four) in enumerate(
            ((own, next_full, next_tail, after_tail), (next_full, own, after_tail, next_tail))
        ):

            @pl.when(x == role)
            def _(one=one, two=two, three=three, four=four):
                products(
                    span(one, 3) + span(here_full, 4) + span(three, 3),
                    span(here_head, 3) + span(two, 4) + span(four, 3),
                    [get_split(ref, small(ref) + W_ROW) for ref in (one, here_full, three)],
                    scaled,
                    theta,
                    basis,
                )
                for n, ref in enumerate((here_head, two)):
                    local[rest + n * SMALL : rest + (n + 1) * SMALL, :] = ref[small(ref) :, :]

        gates_copy.wait()
        copies = []

        def out(source, at, target, to, count):
            copies.append(
                pltpu.make_async_copy(
                    source.at[pl.ds(at * blocks, count * blocks)],
                    target.at[pl.ds(to * blocks, count * blocks)],
                    sems.at[1 + len(copies)],
                )
            )
            copies[-1].start()

        def iso_ready():
            out(iso, 1, iso_three, 0, 3)
            out(iso, 0, local, 0, 3)

        def put_left(p, value):
            for ref, at in ((left, p), (left_three, p - 1), (local, p + 3 if p < 3 else -1)):
                if at >= 0:
                    ref[at * blocks : (at + 1) * blocks, :] = value

        level = bond_body(basis, kept, theta, matrix, proj, work, iso, put_left, gates, iso_ready)
        weights = get_split(local, rest + W_ROW)
        for ref in (iso, iso_three, local):
            ref[small(ref) :, :] = jnp.zeros((SMALL, blocks), BF16)
            put_split(ref, small(ref), weights)
            put_split(ref, small(ref) + LEVEL_ROW, level)
        for copy in copies:
            copy.wait()


def as_column(row):
    return jnp.broadcast_to(row, (128, row.shape[1])).T


def second_kernel(
    local, iso_1, iso_2, left_0, left_1, left_2,
    mid, last, first, whole,
    scaled, theta, basis, matrix, proj, work, gate_stage, gates, sems, iso, left, columns,
):
    x = lax.axis_index("loop") % 2
    c = lax.axis_index("inner") % 2
    blocks = scaled.shape[-1]
    rest = 6 * blocks
    near = left_0.shape[0] // blocks - 3

    def small(ref):
        return ref.shape[0] - SMALL

    @pl.when(x != c)
    def _():
        kept = local[rest + K_ROW : rest + K_ROW + 1, 0:1].astype(F32)
        gates_copy = load_gates(local[rest : rest + 16, 0:128], gate_stage, gates, sems.at[0])
        here = [(local, 0), (iso_1, 1), (iso_1, 2), (iso_2, 2)]
        products(
            [(iso_1, 0), (iso_2, 0), (iso_2, 1)] + here + [(local, 1), (local, 2), (iso_1, 3)],
            [(left_0, near + n) for n in range(3)]
            + [(left_1, n) for n in range(4)]
            + [(left_2, n) for n in range(3)],
            [
                get_split(iso_1, small(iso_1)),
                get_split(local, rest + W_ROW),
                get_split(local, rest + SMALL + W_ROW),
            ],
            scaled,
            theta,
            basis,
        )
        levels = [get_split(ref, small(ref) + LEVEL_ROW) for ref in (local, iso_1, iso_2)]
        for n, value in enumerate(levels):
            columns[n * blocks : (n + 1) * blocks, :] = as_column(value)
        gates_copy.wait()
        def put_left(p, value):
            left[p * blocks : (p + 1) * blocks, :] = value

        level = bond_body(
            basis, kept, theta, matrix, proj, work, iso, put_left, gates, lambda: None
        )
        column = jnp.concatenate([as_column(level)] * 2, axis=1)
        for ref, lo, hi in ((last, 3, 4), (mid, 1, 3), (first, 0, 1)):
            for p in range(lo, hi):
                value = iso[p * blocks : (p + 1) * blocks, :].astype(F32) * column
                ref[(p - lo) * blocks : (p - lo + 1) * blocks, :] = value.astype(BF16)
        scales = [
            jnp.concatenate([columns[n * blocks : (n + 1) * blocks, :]] * 2, axis=1)
            for n in range(3)
        ]
        for p in range(4):
            rows = slice(p * blocks, (p + 1) * blocks)
            whole[rows, :] = (left[rows, :].astype(F32) * scales[CHARGE[p]]).astype(BF16)
        for ref, value in ((first, levels[0]), (whole, level)):
            ref[small(ref) :, :] = jnp.zeros((SMALL, blocks), BF16)
            put_split(ref, small(ref) + LEVEL_ROW, value)


def place(plan, out, sems):
    blocks = out.shape[-1]
    half = blocks // 2
    copies = []
    for source, to, count in plan:
        for n in range(2 * count):
            copies.append(
                pltpu.make_async_copy(
                    source.at[pl.ds(n * half, half)],
                    out.at[pl.ds(to * blocks + n * half, half)],
                    sems.at[len(copies)],
                )
            )
            copies[-1].start()
    return copies


def assemble(
    first_mine, first, mid, last, whole_mine, whole, level_mine, level_far, out, weights, sems
):
    x = lax.axis_index("loop") % 2
    c = lax.axis_index("inner") % 2
    even = [(mid, 1, 2), (last, 3, 1)]
    for role, core, plan, level in (
        (0, 0, [(first, 0, 1)] + even, level_far),
        (0, 1, [(first_mine, 0, 1)] + even, level_mine),
        (1, 0, [(whole_mine, 0, 4)], whole_mine),
        (1, 1, [(whole, 0, 4)], whole),
    ):

        @pl.when(jnp.logical_and(x == role, c == core))
        def _(plan=plan, level=level):
            copies = place(plan, out, sems)
            weights[...] = get_split(level, level.shape[0] - SMALL + LEVEL_ROW)
            for copy in copies:
                copy.wait()


def scratch(blocks):
    return [
        pltpu.VMEM((10 * blocks, blocks), BF16),
        pltpu.VMEM((SLOT_COUNT * blocks, blocks), BF16),
        pltpu.VMEM((blocks, 4 * blocks), BF16),
        pltpu.VMEM((4 * blocks, 4 * blocks), BF16),
        pltpu.VMEM((3 * blocks, 4 * blocks), BF16),
        pltpu.VMEM((blocks, 2 * blocks), F32),
        pltpu.VMEM((16, 128), F32),
        pltpu.SMEM((16, 128), F32),
        pltpu.SemaphoreType.DMA((5,)),
    ]


def vmem():
    return pl.BlockSpec(memory_space=pltpu.VMEM)


def hbm():
    return pl.BlockSpec(memory_space=pl.ANY)


def params():
    return pltpu.CompilerParams(vmem_limit_bytes=VMEM_BYTES)


def per_device(loops, inners, site_blocks, bond_weights, bond_gates, kept_slots):
    blocks = site_blocks.shape[-1]

    def rows(count, small=0):
        return jax.ShapeDtypeStruct((count * blocks + small, blocks), BF16)

    def send(value, where):
        route = []
        for l in range(loops):
            for i in range(inners):
                source = where(l, i)
                if source is not None:
                    sl, si = source
                    route.append(((sl % loops) * inners + si % inners, l * inners + i))
        return lax.ppermute(value, AXES, route)

    def to_first(even, odd):
        return lambda l, i: (even, odd)[l % 2](l, i // 2) if i % 2 == l % 2 else None

    def to_second(where):
        return lambda l, i: where(l, i // 2) if i % 2 != l % 2 else None

    full, head, tail = pl.pallas_call(
        prepare,
        out_shape=(rows(4, SMALL), rows(3, SMALL), rows(3, SMALL)),
        in_specs=[vmem()] * 4,
        out_specs=(hbm(),) * 3,
        scratch_shapes=[pltpu.VMEM((SMALL, blocks), BF16), pltpu.SemaphoreType.DMA((6,))],
        compiler_params=params(),
        name="prepare",
    )(site_blocks.reshape(4 * blocks, blocks), bond_weights[0], bond_gates[0], kept_slots)

    next_full = send(
        full, to_first(lambda l, k: (l + 1, 2 * k + 2), lambda l, k: (l - 1, 2 * k - 1))
    )
    here_full = send(full, to_first(lambda l, k: (l, 2 * k + 1), lambda l, k: (l - 1, 2 * k)))
    next_tail = send(tail, to_first(lambda l, k: (l, 2 * k + 2), lambda l, k: (l, 2 * k + 2)))
    after_tail = send(
        tail, to_first(lambda l, k: (l + 1, 2 * k + 3), lambda l, k: (l - 1, 2 * k + 1))
    )
    here_head = send(head, to_first(lambda l, k: (l + 1, 2 * k + 1), lambda l, k: (l, 2 * k)))

    iso_msg, iso_three, left_msg, left_three, local = pl.pallas_call(
        first_kernel,
        out_shape=(rows(4, SMALL), rows(3, SMALL), rows(4), rows(3), rows(6, 3 * SMALL)),
        in_specs=[vmem()] * 6,
        out_specs=(vmem(),) * 5,
        scratch_shapes=scratch(blocks),
        compiler_params=params(),
        name="first_bond",
    )(full, here_full, next_full, here_head, after_tail, next_tail)

    def worker(l, k, d, s):
        sector = 2 * k + 1 - l % 2 + s
        site = 1 - sector % 2
        return (l - l % 2 + 2 * d + site, sector // 2 * 2 + site)

    local_r = send(local, to_second(lambda l, k: worker(l, k, 0, 0)))
    iso_1 = send(iso_msg, to_second(lambda l, k: worker(l, k, 0, -1)))
    iso_2 = send(iso_three, to_second(lambda l, k: worker(l, k, 0, -2)))
    left_1 = send(left_msg, to_second(lambda l, k: worker(l, k, 1, 1)))
    left_2 = send(left_three, to_second(lambda l, k: worker(l, k, 1, 2)))
    if loops == 2:
        left_0 = local_r
    else:
        left_0 = send(left_msg[: 3 * blocks], to_second(lambda l, k: worker(l, k, 1, 0)))

    mid, last, first, whole = pl.pallas_call(
        second_kernel,
        out_shape=(rows(2), rows(1), rows(1, SMALL), rows(4, SMALL)),
        in_specs=[vmem()] * 6,
        out_specs=(vmem(),) * 4,
        scratch_shapes=scratch(blocks)
        + [pltpu.VMEM((4 * blocks, blocks), BF16)] * 2
        + [pltpu.VMEM((3 * blocks, 128), F32)],
        compiler_params=params(),
        name="second_bond",
    )(local_r, iso_1, iso_2, left_0, left_1, left_2)

    def from_second(l, i, d, s):
        sector = i - s
        site = 1 - sector % 2
        return (l - l % 2 - 2 * d + site, sector // 2 * 2 + 1 - site)

    def right_from(s, cores):
        return lambda l, i: from_second(l, i, 1, s) if l % 2 == 0 and i % 2 in cores else None

    first_r = send(first, right_from(0, (0,) if loops == 2 else (0, 1)))
    mid_r = send(mid, right_from(1, (0, 1)))
    last_r = send(last, right_from(2, (0, 1)))
    whole_r = send(whole, lambda l, i: from_second(l, i, 0, 0) if l % 2 and i % 2 else None)
    if loops == 2:
        first_mine, level_far = first, first_r
    else:
        first_mine = first_r
        level_far = send(
            iso_msg[4 * blocks :], lambda l, i: (l + 1, i + 1) if l % 2 == 0 and i % 2 == 0 else None
        )
    sites, weights = pl.pallas_call(
        assemble,
        out_shape=(rows(4), jax.ShapeDtypeStruct((1, blocks), F32)),
        in_specs=[vmem()] * 8,
        out_specs=(hbm(), vmem()),
        scratch_shapes=[pltpu.SemaphoreType.DMA((8,))],
        compiler_params=params(),
        name="assemble",
    )(first_mine, first_r, mid_r, last_r, whole, whole_r, local_r, level_far)
    return sites.reshape(1, 1, 4, blocks, blocks), weights[None]


def solution(mesh):
    return jax.shard_map(
        functools.partial(per_device, mesh.shape["loop"], mesh.shape["inner"]),
        mesh=mesh,
        in_specs=(
            P("loop", "inner", None, None, None),
            P("loop", "inner", None),
            P("loop", None, None),
            P("loop", "inner"),
        ),
        out_specs=(P("loop", "inner", None, None, None), P("loop", "inner", None)),
        check_vma=False,
    )
```

```python
import functools
import math

import jax
import jax.numpy as jnp
import numpy as np
from jax import lax
from jax.experimental import pallas as pl
from jax.experimental.pallas import tpu as pltpu
from jax.sharding import PartitionSpec as P

CHARGE = (0, 1, 1, 2)
AXES = ("loop", "inner")
BF16, F32 = jnp.bfloat16, jnp.float32
VMEM_BYTES = 24 << 20
HIGHEST = lax.Precision.HIGHEST


def gate_terms():
    table = {}
    for a in range(4):
        for b in range(4):
            table[a, b] = [
                (CHARGE[p] - CHARGE[a], p, q)
                for p in range(4)
                for q in range(4)
                if CHARGE[p] + CHARGE[q] == CHARGE[a] + CHARGE[b]
                and abs(CHARGE[p] - CHARGE[a]) <= 1
            ]
    return table


TERMS = gate_terms()
PIECES = {
    (0, 0): (0, 3, 4, 0),
    (0, 1): (4, 3, 4, 0),
    (0, 2): (5, 3, 4, 0),
    (0, 3): (9, 3, 4, 0),
    (-1, 1): (1, 0, 3, 0),
    (-1, 2): (2, 0, 3, 0),
    (-1, 3): (6, 0, 3, 0),
    (1, 0): (3, 7, 3, 1),
    (1, 1): (7, 7, 3, 1),
    (1, 2): (8, 7, 3, 1),
}


def theta_slots():
    slots, count = {}, 0
    for (distance, q), (_, _, rows, first) in PIECES.items():
        for p in range(rows):
            slots[distance, first + p, q] = count
            count += 1
    return slots, count


SLOTS, SLOT_COUNT = theta_slots()


def dot(a, b, dims, precision=None):
    return lax.dot_general(a, b, (dims, ((), ())), precision=precision, preferred_element_type=F32)


def split3(a):
    h = a.astype(BF16)
    r = a - h.astype(F32)
    m = r.astype(BF16)
    return h, m, (r - m.astype(F32)).astype(BF16)


def factor_rows(work, size, panel=32):
    tiles = panel // 8
    sub = lax.broadcasted_iota(jnp.int32, (8, 128), 0)
    for start in range(0, size, panel):
        low = start < size // 2
        chunks = [0, 1, 2] if low else [1, 2, 3]
        base = start % 128
        rows = [
            [work[start + 8 * t : start + 8 * t + 8, 128 * c : 128 * c + 128] for c in chunks]
            for t in range(tiles)
        ]

        def column(k):
            return {
                t: jnp.broadcast_to(rows[t][0][:, base + k : base + k + 1], (8, 128))
                for t in range(k // 8, tiles)
            }

        def at(col, k):
            return jnp.broadcast_to(col[k // 8][k % 8 : k % 8 + 1, :], (8, 128))

        pivots = [jnp.ones((8, 128), F32) for _ in range(tiles)]
        cols = {k: column(k) for k in range(8)}
        for g in range(tiles):
            if g + 1 < tiles:
                cols.update({k: column(k) for k in range(8 * g + 8, 8 * g + 16)})

            def below(col, j):
                return {
                    t: (jnp.where(sub > j % 8, v, 0.0) if t == j // 8 else v)
                    for t, v in col.items()
                    if t >= g
                }

            for j in range(8 * g, 8 * g + 8, 2):
                one, two = cols[j], cols[j + 1]
                a, b, c = at(one, j), at(one, j + 1), at(two, j + 1)
                det = a * c - b * b
                ra, rd = 1.0 / a, 1.0 / det
                first = {t: v * ra for t, v in below(one, j).items()}
                ratio = b * ra
                two = {t: two[t] - one[t] * ratio for t in one if t >= g}
                second = {t: v * (a * rd) for t, v in below(two, j + 1).items()}
                for k in cols:
                    if k > j + 1:
                        e1, e2 = at(one, k), at(two, k)
                        cols[k] = {
                            t: v - (first[t] * e1 + second[t] * e2) for t, v in cols[k].items()
                        }
                for i in range(len(chunks)):
                    r = j % 8
                    x0 = jnp.broadcast_to(rows[g][i][r : r + 1, :], (8, 128))
                    x1 = jnp.broadcast_to(rows[g][i][r + 1 : r + 2, :], (8, 128)) - ratio * x0
                    for t in range(g, tiles):
                        rows[t][i] = rows[t][i] - (first[t] * x0 + second[t] * x1)
                pivots[g] = jnp.where(
                    sub == j % 8, a, jnp.where(sub == j % 8 + 1, det * ra, pivots[g])
                )
        done = []
        for t in range(tiles):
            scale = lax.rsqrt(pivots[t])
            done.append([x * scale for x in rows[t]])
            for c, x in zip(chunks, done[t]):
                work[start + 8 * t : start + 8 * t + 8, 128 * c : 128 * c + 128] = x
        after = start + panel
        if after < size:
            h, m, l = split3(
                jnp.concatenate([jnp.concatenate(xs, axis=1) for xs in done], axis=0)
            )
            right = jnp.concatenate([h, m, h, l, h, m], axis=0)
            left = jnp.concatenate([h, h, m, h, l, m], axis=0)
            first = 128 * chunks[0]
            for lo, hi in ((after, after + panel), (after + panel, size)):
                if lo < hi:
                    update = dot(left[:, lo - first : hi - first], right, ((0,), (0,)))
                    for i, c in enumerate(chunks):
                        work[lo:hi, 128 * c : 128 * c + 128] -= update[:, 128 * i : 128 * i + 128]


SMALL = 32
W_ROW, K_ROW = 16, 19
LEVEL_ROW = 3


def put_split(ref, at, row):
    for n, part in enumerate(split3(row)):
        ref[at + n : at + n + 1, :] = part


def get_split(ref, at):
    h, m, l = (ref[at + n : at + n + 1, :].astype(F32) for n in range(3))
    return (h + m) + l


def prepare(block_ref, weight_ref, gate_ref, kept_ref, full, head, tail, small, sems):
    blocks = block_ref.shape[-1]
    values = jnp.zeros((SMALL, blocks), F32)
    rowid = lax.broadcasted_iota(jnp.int32, (SMALL, blocks), 0)
    for n, part in enumerate(split3(weight_ref[...])):
        values = jnp.where(rowid == W_ROW + n, part.astype(F32), values)
    small[...] = jnp.where(rowid == K_ROW, kept_ref[...].astype(F32), values).astype(BF16)
    small[0:16, 0:16] = gate_ref[...].astype(BF16)
    copies = []
    for n, (ref, at) in enumerate(((full, 0), (tail, blocks), (head, 0))):
        size = ref.shape[0] - SMALL
        copies.append(
            pltpu.make_async_copy(
                block_ref.at[pl.ds(at, size)], ref.at[pl.ds(0, size)], sems.at[n]
            )
        )
        copies.append(
            pltpu.make_async_copy(small, ref.at[pl.ds(size, SMALL)], sems.at[3 + n])
        )
    for copy in copies:
        copy.start()
    for copy in copies:
        copy.wait()


def exact_root(blocks):
    return math.log2(blocks) % 2 == 0


def products(a_blocks, b_blocks, weights, scaled, theta, basis):
    blocks = scaled.shape[-1]

    def block(place):
        ref, n = place
        return ref[n * blocks : (n + 1) * blocks, :]

    for n, place in enumerate(a_blocks):
        w = weights[0 if n < 3 else 1 if n < 7 else 2]
        scaled[n * blocks : (n + 1) * blocks, :] = (block(place).astype(F32) * w).astype(BF16)
    for n in range(4):
        basis[:, n * blocks : (n + 1) * blocks] = block(a_blocks[3 + n]).T
    for (distance, q), (right, first_row, count, first) in PIECES.items():
        product = dot(
            scaled[first_row * blocks : (first_row + count) * blocks, :],
            block(b_blocks[right]),
            ((1,), (0,)),
        )
        slot = SLOTS[distance, first, q]
        if not exact_root(blocks):
            product = product * (1.0 / math.sqrt(blocks))
        theta[slot * blocks : (slot + count) * blocks, :] = product.astype(BF16)


def load_gates(gate_rows, blocks, gate_stage, gates, sem):
    factor = 1.0 / math.sqrt(blocks) if exact_root(blocks) else 1.0
    gate_stage[...] = gate_rows.astype(F32) * factor
    copy = pltpu.make_async_copy(gate_stage, gates, sem)
    copy.start()
    return copy


def bond_body(basis, kept, theta, matrix, proj, work, iso, put_left, gates, iso_ready):
    blocks = theta.shape[-1]

    def gate(a, b, p, q):
        return gates[4 * a + b, 4 * p + q]

    step = 16

    @pl.loop(0, blocks // step)
    def mix(chunk):
        at = pl.multiple_of(chunk * step, step)
        for half in range(blocks // 128):
            cut = slice(128 * half, 128 * half + 128)
            held = {}

            def term(distance, p, q):
                slot = SLOTS[distance, p, q]
                if slot not in held:
                    place = pl.ds(pl.multiple_of(slot * blocks + at, step), step)
                    held[slot] = theta[place, cut].astype(F32)
                return held[slot]

            for total in range(5):
                for a in range(4):
                    for b in range(4):
                        if CHARGE[a] + CHARGE[b] != total:
                            continue
                        value = None
                        for distance, p, q in TERMS[a, b]:
                            part = gate(a, b, p, q) * term(distance, p, q)
                            value = part if value is None else value + part
                        matrix[
                            pl.ds(pl.multiple_of(a * blocks + at, step), step),
                            b * blocks + 128 * half : b * blocks + 128 * half + 128,
                        ] = value.astype(BF16)
                held.clear()

    projected = dot(basis[...], matrix[...], ((1,), (0,)))
    slot_id = lax.broadcasted_iota(jnp.int32, projected.shape, 0).astype(F32)
    h, m, l = split3(jnp.where(slot_id < kept, projected, 0.0))
    for n, part in enumerate((h, m, l)):
        proj[n * blocks : (n + 1) * blocks, :] = part
    ri = lax.broadcasted_iota(jnp.int32, (blocks, blocks), 0)
    ci = lax.broadcasted_iota(jnp.int32, (blocks, blocks), 1)
    eye = jnp.where(ri == ci, 1.0, 0.0).astype(F32)
    outer = ((1,), (1,))
    mixed = dot(h, m, outer) + dot(h, l, outer)
    work[:, :blocks] = (dot(h, h, outer) + dot(m, m, outer)) + (mixed + mixed.T) + eye
    work[:, blocks:] = eye
    factor_rows(work, blocks)
    root = math.sqrt(4 * blocks)
    wh, wm, wl = split3(work[:, blocks:] * (root if exact_root(blocks) else 1.0))
    h, m, l = (proj[n * blocks : (n + 1) * blocks, :] for n in range(3))
    inner = ((1,), (0,))
    ortho = (
        dot(jnp.concatenate([wh, wm, wl], axis=1), jnp.concatenate([h, h, h], axis=0), inner)
        + dot(jnp.concatenate([wh, wm], axis=1), jnp.concatenate([m, m], axis=0), inner)
        + dot(wh, l, inner)
    )
    ortho = (ortho * (1.0 if exact_root(blocks) else root)).astype(BF16)
    for p in range(4):
        iso[p * blocks : (p + 1) * blocks, :] = ortho[:, p * blocks : (p + 1) * blocks]
    iso_ready()
    flipped = ortho.T
    parts, total = [], 0.0
    for p in range(4):
        rows = matrix[p * blocks : (p + 1) * blocks, :]
        parts.append(dot(rows, flipped, inner) * (1.0 / math.sqrt(4 * blocks)))
        total = total + jnp.sum(parts[p] * parts[p], axis=0, keepdims=True)
    level = jnp.sqrt(total * (1.0 / (4 * blocks)) + 1e-06)
    scale = 1.0 / level
    for p in range(4):
        put_left(p, (parts[p] * scale).astype(BF16))
    return level


def first_kernel(
    own, here_full, next_full, here_head, after_tail, next_tail,
    iso, iso_three, left, left_three, local,
    scaled, theta, basis, matrix, proj, work, gate_stage, gates, sems,
):
    x = lax.axis_index("loop") % 2
    c = lax.axis_index("inner") % 2
    blocks = scaled.shape[-1]

    def small(ref):
        return ref.shape[0] - SMALL

    def span(ref, count):
        return [(ref, n) for n in range(count)]

    @pl.when(x == c)
    def _():
        base = small(here_full)
        kept = here_full[base + K_ROW : base + K_ROW + 1, 0:1].astype(F32)
        gates_copy = load_gates(here_full[base : base + 16, 0:128], blocks, gate_stage, gates, sems.at[0])
        rest = 6 * blocks
        for role, (one, two, three, four) in enumerate(
            ((own, next_full, next_tail, after_tail), (next_full, own, after_tail, next_tail))
        ):

            @pl.when(x == role)
            def _(one=one, two=two, three=three, four=four):
                products(
                    span(one, 3) + span(here_full, 4) + span(three, 3),
                    span(here_head, 3) + span(two, 4) + span(four, 3),
                    [get_split(ref, small(ref) + W_ROW) for ref in (one, here_full, three)],
                    scaled,
                    theta,
                    basis,
                )
                for n, ref in enumerate((here_head, two)):
                    local[rest + n * SMALL : rest + (n + 1) * SMALL, :] = ref[small(ref) :, :]

        gates_copy.wait()
        copies = []

        def out(source, at, target, to, count):
            copies.append(
                pltpu.make_async_copy(
                    source.at[pl.ds(at * blocks, count * blocks)],
                    target.at[pl.ds(to * blocks, count * blocks)],
                    sems.at[1 + len(copies)],
                )
            )
            copies[-1].start()

        def iso_ready():
            out(iso, 1, iso_three, 0, 3)
            out(iso, 0, local, 0, 3)

        def put_left(p, value):
            for ref, at in ((left, p), (left_three, p - 1), (local, p + 3 if p < 3 else -1)):
                if at >= 0:
                    ref[at * blocks : (at + 1) * blocks, :] = value

        level = bond_body(basis, kept, theta, matrix, proj, work, iso, put_left, gates, iso_ready)
        weights = get_split(local, rest + W_ROW)
        for ref in (iso, iso_three, local):
            ref[small(ref) :, :] = jnp.zeros((SMALL, blocks), BF16)
            put_split(ref, small(ref), weights)
            put_split(ref, small(ref) + LEVEL_ROW, level)
        for copy in copies:
            copy.wait()


def as_column(row):
    return jnp.broadcast_to(row, (128, row.shape[1])).T


def second_kernel(
    local, iso_1, iso_2, left_0, left_1, left_2,
    mid, last, first, whole,
    scaled, theta, basis, matrix, proj, work, gate_stage, gates, sems, iso, left, columns,
):
    x = lax.axis_index("loop") % 2
    c = lax.axis_index("inner") % 2
    blocks = scaled.shape[-1]
    rest = 6 * blocks
    near = left_0.shape[0] // blocks - 3

    def small(ref):
        return ref.shape[0] - SMALL

    @pl.when(x != c)
    def _():
        kept = local[rest + K_ROW : rest + K_ROW + 1, 0:1].astype(F32)
        gates_copy = load_gates(local[rest : rest + 16, 0:128], blocks, gate_stage, gates, sems.at[0])
        here = [(local, 0), (iso_1, 1), (iso_1, 2), (iso_2, 2)]
        products(
            [(iso_1, 0), (iso_2, 0), (iso_2, 1)] + here + [(local, 1), (local, 2), (iso_1, 3)],
            [(left_0, near + n) for n in range(3)]
            + [(left_1, n) for n in range(4)]
            + [(left_2, n) for n in range(3)],
            [
                get_split(iso_1, small(iso_1)),
                get_split(local, rest + W_ROW),
                get_split(local, rest + SMALL + W_ROW),
            ],
            scaled,
            theta,
            basis,
        )
        levels = [get_split(ref, small(ref) + LEVEL_ROW) for ref in (local, iso_1, iso_2)]
        for n, value in enumerate(levels):
            columns[n * blocks : (n + 1) * blocks, :] = as_column(value)
        gates_copy.wait()
        def put_left(p, value):
            left[p * blocks : (p + 1) * blocks, :] = value

        level = bond_body(
            basis, kept, theta, matrix, proj, work, iso, put_left, gates, lambda: None
        )
        column = jnp.concatenate([as_column(level)] * 2, axis=1)
        for ref, lo, hi in ((last, 3, 4), (mid, 1, 3), (first, 0, 1)):
            for p in range(lo, hi):
                value = iso[p * blocks : (p + 1) * blocks, :].astype(F32) * column
                ref[(p - lo) * blocks : (p - lo + 1) * blocks, :] = value.astype(BF16)
        scales = [
            jnp.concatenate([columns[n * blocks : (n + 1) * blocks, :]] * 2, axis=1)
            for n in range(3)
        ]
        for p in range(4):
            rows = slice(p * blocks, (p + 1) * blocks)
            whole[rows, :] = (left[rows, :].astype(F32) * scales[CHARGE[p]]).astype(BF16)
        for ref, value in ((first, levels[0]), (whole, level)):
            ref[small(ref) :, :] = jnp.zeros((SMALL, blocks), BF16)
            put_split(ref, small(ref) + LEVEL_ROW, value)


def place(plan, out, sems):
    blocks = out.shape[-1]
    half = blocks // 2
    copies = []
    for source, to, count in plan:
        for n in range(2 * count):
            copies.append(
                pltpu.make_async_copy(
                    source.at[pl.ds(n * half, half)],
                    out.at[pl.ds(to * blocks + n * half, half)],
                    sems.at[len(copies)],
                )
            )
            copies[-1].start()
    return copies


def assemble(
    first_mine, first, mid, last, whole_mine, whole, level_mine, level_far, out, weights, sems
):
    x = lax.axis_index("loop") % 2
    c = lax.axis_index("inner") % 2
    even = [(mid, 1, 2), (last, 3, 1)]
    for role, core, plan, level in (
        (0, 0, [(first, 0, 1)] + even, level_far),
        (0, 1, [(first_mine, 0, 1)] + even, level_mine),
        (1, 0, [(whole_mine, 0, 4)], whole_mine),
        (1, 1, [(whole, 0, 4)], whole),
    ):

        @pl.when(jnp.logical_and(x == role, c == core))
        def _(plan=plan, level=level):
            copies = place(plan, out, sems)
            weights[...] = get_split(level, level.shape[0] - SMALL + LEVEL_ROW)
            for copy in copies:
                copy.wait()


def scratch(blocks):
    return [
        pltpu.VMEM((10 * blocks, blocks), BF16),
        pltpu.VMEM((SLOT_COUNT * blocks, blocks), BF16),
        pltpu.VMEM((blocks, 4 * blocks), BF16),
        pltpu.VMEM((4 * blocks, 4 * blocks), BF16),
        pltpu.VMEM((3 * blocks, 4 * blocks), BF16),
        pltpu.VMEM((blocks, 2 * blocks), F32),
        pltpu.VMEM((16, 128), F32),
        pltpu.SMEM((16, 128), F32),
        pltpu.SemaphoreType.DMA((5,)),
    ]


def vmem():
    return pl.BlockSpec(memory_space=pltpu.VMEM)


def hbm():
    return pl.BlockSpec(memory_space=pl.ANY)


def params():
    return pltpu.CompilerParams(vmem_limit_bytes=VMEM_BYTES)


def per_device(loops, inners, site_blocks, bond_weights, bond_gates, kept_slots):
    blocks = site_blocks.shape[-1]

    def rows(count, small=0):
        return jax.ShapeDtypeStruct((count * blocks + small, blocks), BF16)

    def send(value, where):
        route = []
        for l in range(loops):
            for i in range(inners):
                source = where(l, i)
                if source is not None:
                    sl, si = source
                    route.append(((sl % loops) * inners + si % inners, l * inners + i))
        return lax.ppermute(value, AXES, route)

    def to_first(even, odd):
        return lambda l, i: (even, odd)[l % 2](l, i // 2) if i % 2 == l % 2 else None

    def to_second(where):
        return lambda l, i: where(l, i // 2) if i % 2 != l % 2 else None

    full, head, tail = pl.pallas_call(
        prepare,
        out_shape=(rows(4, SMALL), rows(3, SMALL), rows(3, SMALL)),
        in_specs=[vmem()] * 4,
        out_specs=(hbm(),) * 3,
        scratch_shapes=[pltpu.VMEM((SMALL, blocks), BF16), pltpu.SemaphoreType.DMA((6,))],
        compiler_params=params(),
        name="prepare",
    )(site_blocks.reshape(4 * blocks, blocks), bond_weights[0], bond_gates[0], kept_slots)

    next_full = send(
        full, to_first(lambda l, k: (l + 1, 2 * k + 2), lambda l, k: (l - 1, 2 * k - 1))
    )
    here_full = send(full, to_first(lambda l, k: (l, 2 * k + 1), lambda l, k: (l - 1, 2 * k)))
    next_tail = send(tail, to_first(lambda l, k: (l, 2 * k + 2), lambda l, k: (l, 2 * k + 2)))
    after_tail = send(
        tail, to_first(lambda l, k: (l + 1, 2 * k + 3), lambda l, k: (l - 1, 2 * k + 1))
    )
    here_head = send(head, to_first(lambda l, k: (l + 1, 2 * k + 1), lambda l, k: (l, 2 * k)))

    iso_msg, iso_three, left_msg, left_three, local = pl.pallas_call(
        first_kernel,
        out_shape=(rows(4, SMALL), rows(3, SMALL), rows(4), rows(3), rows(6, 3 * SMALL)),
        in_specs=[vmem()] * 6,
        out_specs=(vmem(),) * 5,
        scratch_shapes=scratch(blocks),
        compiler_params=params(),
        name="first_bond",
    )(full, here_full, next_full, here_head, after_tail, next_tail)

    def worker(l, k, d, s):
        sector = 2 * k + 1 - l % 2 + s
        site = 1 - sector % 2
        return (l - l % 2 + 2 * d + site, sector // 2 * 2 + site)

    local_r = send(local, to_second(lambda l, k: worker(l, k, 0, 0)))
    iso_1 = send(iso_msg, to_second(lambda l, k: worker(l, k, 0, -1)))
    iso_2 = send(iso_three, to_second(lambda l, k: worker(l, k, 0, -2)))
    left_1 = send(left_msg, to_second(lambda l, k: worker(l, k, 1, 1)))
    left_2 = send(left_three, to_second(lambda l, k: worker(l, k, 1, 2)))
    if loops == 2:
        left_0 = local_r
    else:
        left_0 = send(left_msg[: 3 * blocks], to_second(lambda l, k: worker(l, k, 1, 0)))

    mid, last, first, whole = pl.pallas_call(
        second_kernel,
        out_shape=(rows(2), rows(1), rows(1, SMALL), rows(4, SMALL)),
        in_specs=[vmem()] * 6,
        out_specs=(vmem(),) * 4,
        scratch_shapes=scratch(blocks)
        + [pltpu.VMEM((4 * blocks, blocks), BF16)] * 2
        + [pltpu.VMEM((3 * blocks, 128), F32)],
        compiler_params=params(),
        name="second_bond",
    )(local_r, iso_1, iso_2, left_0, left_1, left_2)

    def from_second(l, i, d, s):
        sector = i - s
        site = 1 - sector % 2
        return (l - l % 2 - 2 * d + site, sector // 2 * 2 + 1 - site)

    def right_from(s, cores):
        return lambda l, i: from_second(l, i, 1, s) if l % 2 == 0 and i % 2 in cores else None

    first_r = send(first, right_from(0, (0,) if loops == 2 else (0, 1)))
    mid_r = send(mid, right_from(1, (0, 1)))
    last_r = send(last, right_from(2, (0, 1)))
    whole_r = send(whole, lambda l, i: from_second(l, i, 0, 0) if l % 2 and i % 2 else None)
    if loops == 2:
        first_mine, level_far = first, first_r
    else:
        first_mine = first_r
        level_far = send(
            iso_msg[4 * blocks :], lambda l, i: (l + 1, i + 1) if l % 2 == 0 and i % 2 == 0 else None
        )
    sites, weights = pl.pallas_call(
        assemble,
        out_shape=(rows(4), jax.ShapeDtypeStruct((1, blocks), F32)),
        in_specs=[vmem()] * 8,
        out_specs=(hbm(), vmem()),
        scratch_shapes=[pltpu.SemaphoreType.DMA((8,))],
        compiler_params=params(),
        name="assemble",
    )(first_mine, first_r, mid_r, last_r, whole, whole_r, local_r, level_far)
    return sites.reshape(1, 1, 4, blocks, blocks), weights[None]


def solution(mesh):
    return jax.shard_map(
        functools.partial(per_device, mesh.shape["loop"], mesh.shape["inner"]),
        mesh=mesh,
        in_specs=(
            P("loop", "inner", None, None, None),
            P("loop", "inner", None),
            P("loop", None, None),
            P("loop", "inner"),
        ),
        out_specs=(P("loop", "inner", None, None, None), P("loop", "inner", None)),
        check_vma=False,
    )
```
